256 devices in a mesh: row: 16 (over z, y_hi), col: 16 (over y_lo, x, core).
Axes of the slice: x: 4, y: 4 (y_hi: 2, y_lo: 2; y = y_hi * 2 + y_lo), z: 8, core: 2. Of those that a mesh axis runs over, the one named last changes fastest.
Arguments:
- object_field: float32 [2, 8192, 8192], P(None, 'row', 'col'), may hold values from -6 to 6
- probe: float32 [2, 256, 256], replicated, may hold values from -5 to 5
- positions: int32 [512, 2], P(('row', 'col')), may hold values from 0 to 8191, as said below
- amplitudes: float32 [512, 256, 256], P(('row', 'col')), may hold values from 0 to 3
- counts: int32 [256], P(('row', 'col')), may hold values from 1 to 2, as said below
Outputs:
- object_grad: float32 [2, 8192, 8192], P(None, 'row', 'col')
- probe_grad: float32 [2, 256, 256], replicated
The draws below stay inside these ranges and needn't reach their ends.
Inputs may be any that keep to these rules, and one draw needn't show every extreme that they name: Every slot's window starts inside the tile of the device that holds the slot: positions of slot s lie in tile s div 2, numbered row by row over 16 x 16 tiles. `counts`: some tile has exactly 2 live slots.
All inputs are finite; a program needn't handle non-finite values.
Results may differ from the reference program's by a relative error of at most 0.0003.
Values sent between devices are 32-bit elements; how exact they have to be, the bound alone decides.
No kernel may reach another device: no remote copies, remote signals or barrier semaphores. Data moves between devices by JAX's collectives and lax.ppermute only.
A program may use at most 64 MiB of HBM per device.

```python
import jax
import jax.numpy as jnp
from jax import lax

WIN = 256
TS = 512
CAP = 2
TILES_Y = 16
TILES_X = 16
NY = 8192
NX = 8192
SLOTS = 512


def draw_positions(key, part):
    slot_index = jnp.arange(CAP * TILES_Y * TILES_X, dtype=jnp.int32)
    tile_index = slot_index // CAP
    key_list = jax.random.split(key, 2)
    offset_row = jax.random.randint(key_list[0], slot_index.shape, 0, TS, dtype=jnp.int32)
    offset_col = jax.random.randint(key_list[1], slot_index.shape, 0, TS, dtype=jnp.int32)
    corner_row = tile_index // TILES_X * TS + offset_row
    corner_col = tile_index % TILES_X * TS + offset_col
    return jnp.stack([corner_row, corner_col], axis=1).astype(jnp.int32)


def draw_counts(key, part):
    key_list = jax.random.split(key, 4)
    tile_index = jnp.arange(TILES_Y * TILES_X, dtype=jnp.int32)
    tile_row = tile_index // TILES_X
    tile_col = tile_index % TILES_X
    band_rows = max(1, TILES_Y // 2)
    band_cols = TILES_X // 2
    first_row = jax.random.randint(key_list[0], (), 0, TILES_Y - band_rows + 1, dtype=jnp.int32)
    first_col = jax.random.randint(key_list[1], (), 0, TILES_X - band_cols + 1, dtype=jnp.int32)
    hot_region = (tile_row >= first_row) & (tile_row < first_row + band_rows) & (tile_col >= first_col) & (tile_col < first_col + band_cols)
    cold_count = jax.random.randint(key_list[2], tile_index.shape, 1, max(2, CAP // 4 + 1), dtype=jnp.int32)
    hot_count = jax.random.randint(key_list[3], tile_index.shape, CAP // 2 + 1, CAP + 1, dtype=jnp.int32)
    drawn_count = jnp.where(hot_region, hot_count, cold_count)
    peak_tile = (tile_row == first_row) & (tile_col == first_col)
    return jnp.where(peak_tile, CAP, drawn_count).astype(jnp.int32)


def block_levels(own_key, extent, shards, smallest, top_value):
    loudness = 1.0
    for position, blocks in shards:
        heights = jax.random.uniform(jax.random.fold_in(jax.random.fold_in(own_key, 6), position), (blocks,), jnp.float32, smallest / len(shards), top_value / len(shards))
        loudness = loudness * jnp.repeat(jnp.exp(heights), extent[position] // blocks).reshape((-1,) + (1,) * (len(extent) - 1 - position))
    return loudness


def gaussian(key, shape, scale, most, cuts=(), kind=jnp.bfloat16):
    result = jax.random.normal(key, shape, jnp.float32) * scale
    if len(cuts) > 0:
        result = block_levels(key, shape, cuts, -0.22, 0.18) * result
    return jnp.clip(result, min=-most, max=most).astype(kind)


def setup_inputs(seed: int = 0) -> dict:
    arg_keys = jax.random.split(jax.random.key(seed), 6)
    return {
        "object_field": gaussian(arg_keys[0], (2, NY, NX), 1.0, 6.0, ((1, 16), (2, 16)), jnp.float32),
        "probe": gaussian(arg_keys[1], (2, WIN, WIN), 0.7, 5.0, (), jnp.float32),
        "positions": draw_positions(jax.random.fold_in(arg_keys[5], 71), 0),
        "amplitudes": jnp.clip(3.0 * jax.random.uniform(arg_keys[3], (SLOTS, WIN, WIN), jnp.float32) ** block_levels(arg_keys[3], (SLOTS, WIN, WIN), ((0, 256),), -0.2, 0.2), 0.0, 3.0),
        "counts": draw_counts(jax.random.fold_in(arg_keys[5], 71), 0),
    }


def reference(object_field, probe, positions, amplitudes, counts):
    complex_object = object_field[0] + 1j * object_field[1]
    complex_probe = probe[0] + 1j * probe[1]
    padded = jnp.pad(complex_object, ((0, WIN), (0, WIN)))
    slot_index = jnp.arange(positions.shape[0], dtype=jnp.int32)
    live_mask = (slot_index % CAP < counts[slot_index // CAP]).astype(object_field.dtype)

    def accumulate(state_pair, scan_item):
        grad_object, grad_probe = state_pair
        corner, measured, live_one = scan_item
        start_row = corner[0].astype(jnp.int32)
        start_col = corner[1].astype(jnp.int32)
        patch_field = lax.dynamic_slice(padded, (start_row, start_col), (WIN, WIN))
        far_field = jnp.fft.fft2(complex_probe * patch_field, norm='ortho')
        magnitude = jnp.sqrt(far_field.real ** 2 + far_field.imag ** 2 + 1.0)
        back_field = jnp.fft.ifft2((1.0 - measured / magnitude) * far_field, norm='ortho') * live_one
        current = lax.dynamic_slice(grad_object, (start_row, start_col), (WIN, WIN))
        grad_object = lax.dynamic_update_slice(grad_object, current + jnp.conj(complex_probe) * back_field, (start_row, start_col))
        return ((grad_object, grad_probe + jnp.conj(patch_field) * back_field), None)
    initial = (jnp.zeros_like(padded), jnp.zeros_like(complex_probe))
    (grad_object, grad_probe), ignored = lax.scan(accumulate, initial, (positions, amplitudes, live_mask))
    grad_object = grad_object[:NY, :NX]
    return (jnp.stack([grad_object.real, grad_object.imag]), jnp.stack([grad_probe.real, grad_probe.imag]))
```

```python
import functools
import math

import jax
import jax.numpy as jnp
import ml_dtypes
import numpy as np
from jax import lax
from jax.experimental import pallas as pl
from jax.experimental.pallas import tpu as pltpu
from jax.sharding import PartitionSpec as P

AXES = ("row", "col")
ANY = pl.BlockSpec(memory_space=pl.ANY)
SMEM = pl.BlockSpec(memory_space=pltpu.SMEM)
VMEM = pl.BlockSpec(memory_space=pltpu.VMEM)
MIB = 1024 * 1024
SIZES = {"x": 4, "y": 4, "z": 8, "core": 2}


def shifted(block, axis, distance):
    devices = range(lax.axis_size(axis))
    route = [(i - distance, i) for i in devices if i - distance in devices]
    return lax.ppermute(block, axis, route)


def dft_tables(window):
    index = np.arange(window)
    phases = (np.outer(index, index) % window) * (2.0 * math.pi / window)
    re, im = np.cos(phases) / math.sqrt(window), -np.sin(phases) / math.sqrt(window)
    table = np.block([[re, im], [-im, re]])
    high = table.astype(ml_dtypes.bfloat16)
    low = (table - high.astype(np.float64)).astype(ml_dtypes.bfloat16)
    return high, low, high.T.copy(), low.T.copy()


def probe_kernel(window, tile, pos_ref, probe_ref, out_ref):
    for slot in range(out_ref.shape[0]):
        row = lax.rem(lax.rem(pos_ref[slot, 0], tile), window)
        col = lax.rem(lax.rem(pos_ref[slot, 1], tile), window)
        for plane in range(2):
            turned = pltpu.roll(probe_ref[plane], row, 0)
            out_ref[slot, plane] = pltpu.roll(turned, col, 1)


def turned_probe(positions, probe, tile):
    slots, window = positions.shape[0], probe.shape[1]
    return pl.pallas_call(
        functools.partial(probe_kernel, window, tile),
        out_shape=jax.ShapeDtypeStruct((slots, 2, window, window), jnp.float32),
        in_specs=[SMEM, VMEM],
        out_specs=VMEM,
        cost_estimate=pl.CostEstimate(flops=4000000, bytes_accessed=2 * MIB, transcendentals=0),
        name="turned_probe",
    )(positions, probe)


def split(value):
    high = value.astype(jnp.bfloat16)
    return high, (value - high.astype(jnp.float32)).astype(jnp.bfloat16)


def dot(first, second):
    return jnp.dot(first, second, preferred_element_type=jnp.float32)


def dot_right(value, high_ref, low_ref):
    high, low = split(value)
    return dot(high, high_ref[...]) + (dot(low, high_ref[...]) + dot(high, low_ref[...]))


def dot_left(high_ref, low_ref, value):
    high, low = split(value)
    return dot(high_ref[...], high) + (dot(high_ref[...], low) + dot(low_ref[...], high))


def slots_kernel(
    window, tile,
    counts_ref, pos_ref, object_hbm, right_hbm, below0_hbm, below1_hbm, corner_hbm,
    turned_hbm, amp_hbm, high_hbm, low_hbm, thigh_hbm, tlow_hbm,
    tile_out, right_out, below0_out, below1_out, corner_out, probe_out,
    ext, grad, turned, amp, high, low, thigh, tlow, patch, probe_grad, sems,
):
    w, t = window, tile
    e = t + w
    moves = [
        (object_hbm, ext.at[:, 0:t, 0:t]),
        (right_hbm, ext.at[:, 0:t, t:e]),
        (below0_hbm, ext.at[:, t:e, 0:w]),
        (below1_hbm, ext.at[:, t:e, w:t]),
        (corner_hbm, ext.at[:, t:e, t:e]),
        (turned_hbm, turned),
        (amp_hbm, amp),
        (high_hbm, high),
        (low_hbm, low),
        (thigh_hbm, thigh),
        (tlow_hbm, tlow),
    ]
    copies = [pltpu.make_async_copy(a, b, sems.at[i]) for i, (a, b) in enumerate(moves)]
    for copy in copies:
        copy.start()
    grad[...] = jnp.zeros_like(grad)
    probe_grad[...] = jnp.zeros_like(probe_grad)
    for copy in copies:
        copy.wait()
    rows = lax.broadcasted_iota(jnp.int32, (w, w), 0)
    cols = lax.broadcasted_iota(jnp.int32, (w, w), 1)

    def one_slot(slot, carry):
        top = lax.rem(pos_ref[slot, 0], t)
        left = lax.rem(pos_ref[slot, 1], t)
        row_turn, col_turn = lax.rem(top, w), lax.rem(left, w)
        row_at = pl.multiple_of((top // w) * w, w)
        col_at = pl.multiple_of((left // w) * w, w)
        in_low = rows < row_turn
        in_right = cols < col_turn
        blocks = [
            (pl.ds(row_at, w), pl.ds(col_at, w), ~in_low & ~in_right),
            (pl.ds(row_at, w), pl.ds(col_at + w, w), ~in_low & in_right),
            (pl.ds(row_at + w, w), pl.ds(col_at, w), in_low & ~in_right),
            (pl.ds(row_at + w, w), pl.ds(col_at + w, w), in_low & in_right),
        ]
        for plane in range(2):
            upper = jnp.where(
                in_right, ext[plane, blocks[1][0], blocks[1][1]], ext[plane, blocks[0][0], blocks[0][1]]
            )
            lower = jnp.where(
                in_right, ext[plane, blocks[3][0], blocks[3][1]], ext[plane, blocks[2][0], blocks[2][1]]
            )
            patch[plane] = jnp.where(in_low, lower, upper)
        probe_re, probe_im = turned[slot, 0], turned[slot, 1]
        wave = jnp.concatenate(
            [probe_re * patch[0] - probe_im * patch[1], probe_re * patch[1] + probe_im * patch[0]], axis=1
        )
        half = dot_right(wave, high, low)
        half = jnp.concatenate([half[:, :w], half[:, w:]], axis=0)
        far = dot_left(thigh, tlow, half)
        far_re, far_im = far[:w], far[w:]
        factor = 1.0 - amp[slot] / jnp.sqrt(far_re * far_re + far_im * far_im + 1.0)
        wave = jnp.concatenate([factor * far_re, factor * far_im], axis=1)
        half = dot_right(wave, thigh, tlow)
        half = jnp.concatenate([half[:, :w], half[:, w:]], axis=0)
        back = dot_left(high, low, half)
        back_re, back_im = back[:w], back[w:]
        terms = (
            turned[slot, 0] * back_re + turned[slot, 1] * back_im,
            turned[slot, 0] * back_im - turned[slot, 1] * back_re,
        )
        for at_rows, at_cols, mask in blocks:
            for plane in range(2):
                grad[plane, at_rows, at_cols] += jnp.where(mask, terms[plane], 0.0)
        terms = (patch[0] * back_re + patch[1] * back_im, patch[0] * back_im - patch[1] * back_re)
        for plane in range(2):
            term = pltpu.roll(terms[plane], lax.rem(w - row_turn, w), 0)
            probe_grad[plane] += pltpu.roll(term, lax.rem(w - col_turn, w), 1)
        return carry

    lax.fori_loop(0, counts_ref[0], one_slot, 0)
    moves = [
        (probe_grad, probe_out),
        (grad.at[:, t:e, t:e], corner_out),
        (grad.at[:, t:e, w:t], below1_out),
        (grad.at[:, t:e, 0:w], below0_out),
        (grad.at[:, 0:t, t:e], right_out),
        (grad.at[:, 0:t, 0:t], tile_out),
    ]
    copies = [pltpu.make_async_copy(a, b, sems.at[i]) for i, (a, b) in enumerate(moves)]
    for copy in copies:
        copy.start()
    for copy in copies:
        copy.wait()


def slot_terms(counts, positions, object_field, right, below0, below1, corner, turned, amplitudes):
    w, t = below0.shape[1], object_field.shape[1]
    slots = positions.shape[0]
    tables = [jnp.asarray(table) for table in dft_tables(w)]
    f32 = functools.partial(jax.ShapeDtypeStruct, dtype=jnp.float32)
    block = f32((2, w, w))
    return pl.pallas_call(
        functools.partial(slots_kernel, w, t),
        out_shape=[f32((2, t, t)), f32((2, t, w)), block, block, block, block],
        in_specs=[SMEM, SMEM] + [ANY] * 11,
        out_specs=[ANY] * 6,
        scratch_shapes=[
            pltpu.VMEM((2, t + w, t + w), jnp.float32),
            pltpu.VMEM((2, t + w, t + w), jnp.float32),
            pltpu.VMEM((slots, 2, w, w), jnp.float32),
            pltpu.VMEM((slots, w, w), jnp.float32),
            pltpu.VMEM((2 * w, 2 * w), jnp.bfloat16),
            pltpu.VMEM((2 * w, 2 * w), jnp.bfloat16),
            pltpu.VMEM((2 * w, 2 * w), jnp.bfloat16),
            pltpu.VMEM((2 * w, 2 * w), jnp.bfloat16),
            pltpu.VMEM((2, w, w), jnp.float32),
            pltpu.VMEM((2, w, w), jnp.float32),
            pltpu.SemaphoreType.DMA((11,)),
        ],
        compiler_params=pltpu.CompilerParams(vmem_limit_bytes=32 * MIB),
        cost_estimate=pl.CostEstimate(flops=3 * 10**9, bytes_accessed=14 * MIB, transcendentals=0),
        name="slot_terms",
    )(counts, positions, object_field, right, below0, below1, corner, turned, amplitudes, *tables)


def combine_kernel(half, tile_ref, left_ref, above0_ref, above1_ref, out_ref):
    w = left_ref.shape[2]
    first, second = tile_ref[:, :, :w] + left_ref[...], tile_ref[:, :, w:]

    @pl.when(pl.program_id(0) < half)
    def _():
        out_ref[:, :, :w] = first + above0_ref[...]
        out_ref[:, :, w:] = second + above1_ref[...]

    @pl.when(pl.program_id(0) >= half)
    def _():
        out_ref[:, :, :w] = first
        out_ref[:, :, w:] = second


def combined(tile_grad, from_left, above0, above1):
    t, w = tile_grad.shape[1], from_left.shape[2]
    step = w // 2
    half = w // step
    above = pl.BlockSpec((2, step, w), lambda i: (0, jnp.minimum(i, half - 1), 0))
    return pl.pallas_call(
        functools.partial(combine_kernel, half),
        out_shape=jax.ShapeDtypeStruct(tile_grad.shape, jnp.float32),
        grid=(t // step,),
        in_specs=[
            pl.BlockSpec((2, step, t), lambda i: (0, i, 0)),
            pl.BlockSpec((2, step, w), lambda i: (0, i, 0)),
            above,
            above,
        ],
        out_specs=pl.BlockSpec((2, step, t), lambda i: (0, i, 0)),
        cost_estimate=pl.CostEstimate(flops=10**6, bytes_accessed=6 * MIB, transcendentals=0),
        name="combined",
    )(tile_grad, from_left, above0, above1)


def place(x, y, z, core):
    return (z % 8 * 2 + y % 4 // 2) * 16 + y % 2 * 8 + x % 4 * 2 + core % 2


def moved(value, **distance):
    route = []
    for x in range(4):
        for y in range(4):
            for z in range(8):
                for core in range(2):
                    target = place(
                        x + distance.get("x", 0), y + distance.get("y", 0),
                        z + distance.get("z", 0), core + distance.get("core", 0),
                    )
                    route.append((place(x, y, z, core), target))
    return lax.ppermute(value, AXES, route)


def scattered(value, axis, index):
    size = SIZES[axis]
    rows = value.shape[0] // size
    chunk = lambda i: lax.dynamic_slice(value, (i % size * rows, 0), (rows, value.shape[1]))
    parts = [moved(chunk(index + d), **{axis: d}) for d in range(1, size)]
    return functools.reduce(jnp.add, parts, chunk(index))


def summed(value, axis):
    parts = [moved(value, **{axis: d}) for d in range(1, SIZES[axis])]
    return functools.reduce(jnp.add, parts, value)


def gathered(value, axis, index):
    size = SIZES[axis]
    rows = value.shape[0]
    parts = [value] + [moved(value, **{axis: -d}) for d in range(1, size)]
    twice = jnp.concatenate(parts + parts[:-1])
    return lax.dynamic_slice(twice, ((size - index) % size * rows, 0), (size * rows, value.shape[1]))


def total(value):
    if (lax.axis_size("row"), lax.axis_size("col")) != (16, 16):
        return lax.psum(value, AXES)
    shape = value.shape
    row, col = lax.axis_index("row"), lax.axis_index("col")
    z, core = row // 2, col % 2
    value = value.reshape(shape[0] * shape[1], shape[2])
    value = scattered(value, "core", core)
    value = scattered(value, "z", z)
    value = summed(value, "x")
    value = summed(value, "y")
    value = gathered(value, "z", z)
    value = gathered(value, "core", core)
    return value.reshape(shape)


def shards(object_field, probe, positions, amplitudes, counts):
    tile = object_field.shape[1]
    window = probe.shape[1]
    below0 = shifted(object_field[:, :window, :window], "row", -1)
    below1 = shifted(object_field[:, :window, window:], "row", -1)
    right = shifted(object_field[:, :, :window], "col", -1)
    turned = turned_probe(positions, probe, tile)
    corner = shifted(below0, "col", -1)
    tile_grad, right_grad, below0_grad, below1_grad, corner_grad, probe_grad = slot_terms(
        counts, positions, object_field, right, below0, below1, corner, turned, amplitudes
    )
    corner_in = shifted(corner_grad, "col", 1)
    above1 = shifted(below1_grad, "row", 1)
    from_left = shifted(right_grad, "col", 1)
    above0 = shifted(below0_grad + corner_in, "row", 1)
    probe_total = total(probe_grad)
    return combined(tile_grad, from_left, above0, above1), probe_total


def solution(mesh):
    return jax.shard_map(
        shards,
        mesh=mesh,
        in_specs=(
            P(None, "row", "col"),
            P(),
            P(("row", "col"), None),
            P(("row", "col"), None, None),
            P(("row", "col")),
        ),
        out_specs=(P(None, "row", "col"), P()),
        check_vma=False,
    )
```

```python
import functools
import math

import jax
import jax.numpy as jnp
import ml_dtypes
import numpy as np
from jax import lax
from jax.experimental import pallas as pl
from jax.experimental.pallas import tpu as pltpu
from jax.sharding import PartitionSpec as P

AXES = ("row", "col")
HBM = pl.BlockSpec(memory_space=pltpu.HBM)
SMEM = pl.BlockSpec(memory_space=pltpu.SMEM)
MIB = 1024 * 1024
SIZES = {"x": 4, "y": 4, "z": 8, "core": 2}


def shifted(block, axis, distance):
    devices = range(lax.axis_size(axis))
    route = [(i - distance, i) for i in devices if i - distance in devices]
    return lax.ppermute(block, axis, route)


def dft_tables(window):
    index = np.arange(window)
    phases = (np.outer(index, index) % window) * (2.0 * math.pi / window)
    tables = []
    for part in (np.cos(phases), -np.sin(phases)):
        part = part / math.sqrt(window)
        high = part.astype(ml_dtypes.bfloat16)
        tables += [high, (part - high.astype(np.float64)).astype(ml_dtypes.bfloat16)]
    return np.stack(tables)


def split(value):
    high = value.astype(jnp.bfloat16)
    return high, (value - high.astype(jnp.float32)).astype(jnp.bfloat16)


def dot(first, second):
    return jnp.dot(first, second, preferred_element_type=jnp.float32)


def times_table(re, im, tables, sign):
    w = re.shape[0]
    high, low = split(jnp.concatenate([re, im], axis=0))
    by_re = dot(high, tables[0]) + (dot(low, tables[0]) + dot(high, tables[1]))
    by_im = dot(high, tables[2]) + (dot(low, tables[2]) + dot(high, tables[3]))
    if sign > 0:
        return by_re[:w] - by_im[w:], by_re[w:] + by_im[:w]
    return by_re[:w] + by_im[w:], by_re[w:] - by_im[:w]


def table_times(re, im, tables, sign):
    w = re.shape[1]
    high, low = split(jnp.concatenate([re, im], axis=1))
    by_re = dot(tables[0], high) + (dot(tables[0], low) + dot(tables[1], high))
    by_im = dot(tables[2], high) + (dot(tables[2], low) + dot(tables[3], high))
    if sign > 0:
        return by_re[:, :w] - by_im[:, w:], by_re[:, w:] + by_im[:, :w]
    return by_re[:, :w] + by_im[:, w:], by_re[:, w:] - by_im[:, :w]


def slots_kernel(
    window, tile,
    counts_ref, pos_ref, place_ref, object_hbm, right0_hbm, right1_hbm, relayed_hbm, below0_hbm, below1_hbm,
    corner_hbm, diagonal_hbm, probe_hbm, amp_hbm, tables_hbm,
    tile_out, right_out, below0_out, below1_out, corner_out, keep_out, send_out,
    ext, grad, probe, turned, amp, tables, patch, probe_grad, sems,
):
    w, t = window, tile
    e = t + w
    live = counts_ref[0]
    core, at_seam = place_ref[0], place_ref[1]
    moves = [
        (probe_hbm, probe),
        (tables_hbm, tables),
        (amp_hbm, amp),
        (object_hbm, ext.at[:, 0:t, 0:t]),
        (right0_hbm, ext.at[:, 0:w, t:e]),
        (below0_hbm, ext.at[:, t:e, 0:w]),
        (below1_hbm, ext.at[:, t:e, w:t]),
    ]
    copies = [pltpu.make_async_copy(a, b, sems.at[i]) for i, (a, b) in enumerate(moves)]
    for copy in copies:
        copy.start()

    def choose(act):
        for flag, lower, last in ((0, right1_hbm, corner_hbm), (1, relayed_hbm, diagonal_hbm)):
            @pl.when(at_seam == flag)
            def _():
                act(pltpu.make_async_copy(lower, ext.at[:, w:t, t:e], sems.at[7]))
                act(pltpu.make_async_copy(last, ext.at[:, t:e, t:e], sems.at[8]))

    choose(lambda copy: copy.start())
    grad[...] = jnp.zeros_like(grad)
    probe_grad[...] = jnp.zeros_like(probe_grad)
    copies[0].wait()

    def turn(slot, carry):
        row = lax.rem(lax.rem(pos_ref[slot, 0], t), w)
        col = lax.rem(lax.rem(pos_ref[slot, 1], t), w)
        for plane in range(2):
            turned[slot, plane] = pltpu.roll(pltpu.roll(probe[plane], row, 0), col, 1)
        return carry

    lax.fori_loop(0, live, turn, 0)
    for copy in copies[1:]:
        copy.wait()
    choose(lambda copy: copy.wait())
    moves = [
        (grad.at[:, t:e, t:e], corner_out),
        (grad.at[:, t:e, w:t], below1_out),
        (grad.at[:, t:e, 0:w], below0_out),
        (grad.at[:, 0:t, t:e], right_out),
        (grad.at[:, 0:t, 0:t], tile_out),
    ]
    results = [pltpu.make_async_copy(a, b, sems.at[i]) for i, (a, b) in enumerate(moves)]
    rows = lax.broadcasted_iota(jnp.int32, (w, w), 0)
    cols = lax.broadcasted_iota(jnp.int32, (w, w), 1)

    def one_slot(slot, carry):
        top = lax.rem(pos_ref[slot, 0], t)
        left = lax.rem(pos_ref[slot, 1], t)
        row_turn, col_turn = lax.rem(top, w), lax.rem(left, w)
        row_at = pl.multiple_of((top // w) * w, w)
        col_at = pl.multiple_of((left // w) * w, w)
        in_low = rows < row_turn
        in_right = cols < col_turn
        blocks = [
            (pl.ds(row_at, w), pl.ds(col_at, w), ~in_low & ~in_right),
            (pl.ds(row_at, w), pl.ds(col_at + w, w), ~in_low & in_right),
            (pl.ds(row_at + w, w), pl.ds(col_at, w), in_low & ~in_right),
            (pl.ds(row_at + w, w), pl.ds(col_at + w, w), in_low & in_right),
        ]
        for plane in range(2):
            parts = [ext[plane, at_rows, at_cols] for at_rows, at_cols, _ in blocks]
            patch[plane] = jnp.where(
                in_low, jnp.where(in_right, parts[3], parts[2]), jnp.where(in_right, parts[1], parts[0])
            )
        re = turned[slot, 0] * patch[0] - turned[slot, 1] * patch[1]
        im = turned[slot, 0] * patch[1] + turned[slot, 1] * patch[0]
        re, im = times_table(re, im, tables, 1)
        re, im = table_times(re, im, tables, 1)
        factor = 1.0 - amp[slot] / jnp.sqrt(re * re + im * im + 1.0)
        re, im = times_table(factor * re, factor * im, tables, -1)
        re, im = table_times(re, im, tables, -1)
        terms = (turned[slot, 0] * re + turned[slot, 1] * im, turned[slot, 0] * im - turned[slot, 1] * re)
        for at_rows, at_cols, mask in blocks:
            for plane in range(2):
                grad[plane, at_rows, at_cols] += jnp.where(mask, terms[plane], 0.0)

        @pl.when(slot == live - 1)
        def _():
            for copy in results:
                copy.start()

        terms = (patch[0] * re + patch[1] * im, patch[0] * im - patch[1] * re)
        for plane in range(2):
            term = pltpu.roll(terms[plane], lax.rem(w - row_turn, w), 0)
            probe_grad[plane] += pltpu.roll(term, lax.rem(w - col_turn, w), 1)
        return carry

    lax.fori_loop(0, live, one_slot, 0)
    keep = pltpu.make_async_copy(probe_grad.at[core], keep_out, sems.at[7])
    send = pltpu.make_async_copy(probe_grad.at[1 - core], send_out, sems.at[8])
    for copy in (send, keep):
        copy.start()
    for copy in (send, keep, *results):
        copy.wait()


def slot_terms(counts, positions, where, object_field, halos, probe, amplitudes):
    w, t = probe.shape[1], object_field.shape[1]
    slots = positions.shape[0]
    f32 = functools.partial(jax.ShapeDtypeStruct, dtype=jnp.float32)
    block = f32((2, w, w))
    return pl.pallas_call(
        functools.partial(slots_kernel, w, t),
        out_shape=[f32((2, t, t)), f32((2, t, w)), block, block, block, f32((w, w)), f32((w, w))],
        in_specs=[SMEM] * 3 + [HBM] * 11,
        out_specs=[HBM] * 7,
        scratch_shapes=[
            pltpu.VMEM((2, t + w, t + w), jnp.float32),
            pltpu.VMEM((2, t + w, t + w), jnp.float32),
            pltpu.VMEM((2, w, w), jnp.float32),
            pltpu.VMEM((slots, 2, w, w), jnp.float32),
            pltpu.VMEM((slots, w, w), jnp.float32),
            pltpu.VMEM((4, w, w), jnp.bfloat16),
            pltpu.VMEM((2, w, w), jnp.float32),
            pltpu.VMEM((2, w, w), jnp.float32),
            pltpu.SemaphoreType.DMA((9,)),
        ],
        compiler_params=pltpu.CompilerParams(vmem_limit_bytes=60 * MIB),
        cost_estimate=pl.CostEstimate(flops=3 * 10**9, bytes_accessed=14 * MIB, transcendentals=0),
        name="slot_terms",
    )(counts, positions, where, object_field, *halos, probe, amplitudes, jnp.asarray(dft_tables(w)))


def combine_kernel(half, tile_ref, left_ref, above0_ref, above1_ref, out_ref):
    w = left_ref.shape[2]
    first, second = tile_ref[:, :, :w] + left_ref[...], tile_ref[:, :, w:]

    @pl.when(pl.program_id(0) < half)
    def _():
        out_ref[:, :, :w] = first + above0_ref[...]
        out_ref[:, :, w:] = second + above1_ref[...]

    @pl.when(pl.program_id(0) >= half)
    def _():
        out_ref[:, :, :w] = first
        out_ref[:, :, w:] = second


def combined(tile_grad, from_left, above0, above1):
    t, w = tile_grad.shape[1], from_left.shape[2]
    step = w // 2
    half = w // step
    above = pl.BlockSpec((2, step, w), lambda i: (0, jnp.minimum(i, half - 1), 0))
    return pl.pallas_call(
        functools.partial(combine_kernel, half),
        out_shape=jax.ShapeDtypeStruct(tile_grad.shape, jnp.float32),
        grid=(t // step,),
        in_specs=[
            pl.BlockSpec((2, step, t), lambda i: (0, i, 0)),
            pl.BlockSpec((2, step, w), lambda i: (0, i, 0)),
            above,
            above,
        ],
        out_specs=pl.BlockSpec((2, step, t), lambda i: (0, i, 0)),
        cost_estimate=pl.CostEstimate(flops=10**6, bytes_accessed=6 * MIB, transcendentals=0),
        name="combined",
    )(tile_grad, from_left, above0, above1)


def place(x, y, z, core):
    return (z % 8 * 2 + y % 4 // 2) * 16 + y % 2 * 8 + x % 4 * 2 + core % 2


def moved(value, **distance):
    route = []
    for x in range(4):
        for y in range(4):
            for z in range(8):
                for core in range(2):
                    target = place(
                        x + distance.get("x", 0), y + distance.get("y", 0),
                        z + distance.get("z", 0), core + distance.get("core", 0),
                    )
                    route.append((place(x, y, z, core), target))
    return lax.ppermute(value, AXES, route)


def summed(value, axis):
    parts = [moved(value, **{axis: d}) for d in range(1, SIZES[axis])]
    return functools.reduce(jnp.add, parts, value)


def z_exchange(chunks):
    groups = [[place(x, y, z, c) for z in range(8)] for x in range(4) for y in range(4) for c in range(2)]
    return lax.all_to_all(chunks, AXES, 0, 0, tiled=True, axis_index_groups=groups)


def total(keep, send, core):
    if (lax.axis_size("row"), lax.axis_size("col")) != (16, 16):
        return lax.psum(jnp.where(core == 0, jnp.stack([keep, send]), jnp.stack([send, keep])), AXES)
    w = keep.shape[0]
    value = keep + moved(send, core=1)
    value = jnp.sum(z_exchange(value.reshape(8, w // 8, w)), axis=0)
    value = summed(summed(value, "x"), "y")
    value = z_exchange(jnp.broadcast_to(value, (8,) + value.shape)).reshape(w, w)
    other = moved(value, core=1)
    return jnp.where(core == 0, jnp.stack([value, other]), jnp.stack([other, value]))


def halos_in(object_field, window):
    rows, cols = lax.axis_size("row"), lax.axis_size("col")
    seam = cols // 2
    w = window
    below0_own = object_field[:, :w, :w]
    right1_own = object_field[:, w:, :w]
    below0 = shifted(below0_own, "row", -1)
    below1 = shifted(object_field[:, :w, w:], "row", -1)
    relayed = lax.ppermute(right1_own, "col", [(seam, 0)])
    right0 = shifted(below0_own, "col", -1)
    plain = [(i + 1, i) for i in range(cols - 1) if i + 1 != seam]
    right1 = lax.ppermute(right1_own, "col", plain)
    route = [((r + 1) * cols + seam, r * cols + seam - 1) for r in range(rows - 1)]
    diagonal = lax.ppermute(below0_own, AXES, route)
    relayed = lax.ppermute(relayed, "col", [(0, seam - 1)])
    corner = lax.ppermute(below0, "col", plain)
    return right0, right1, relayed, below0, below1, corner, diagonal


def shards(object_field, probe, positions, amplitudes, counts):
    window = probe.shape[1]
    col = lax.axis_index("col")
    core = col % 2
    at_seam = (col == lax.axis_size("col") // 2 - 1).astype(jnp.int32)
    halos = halos_in(object_field, window)
    where = jnp.stack([core, at_seam])
    tile_grad, right_grad, below0_grad, below1_grad, corner_grad, keep, send = slot_terms(
        counts, positions, where, object_field, halos, probe, amplitudes
    )
    corner_in = shifted(corner_grad, "col", 1)
    above1 = shifted(below1_grad, "row", 1)
    from_left = shifted(right_grad, "col", 1)
    above0 = shifted(below0_grad + corner_in, "row", 1)
    probe_total = total(keep, send, core)
    return combined(tile_grad, from_left, above0, above1), probe_total


def solution(mesh):
    return jax.shard_map(
        shards,
        mesh=mesh,
        in_specs=(
            P(None, "row", "col"),
            P(),
            P(("row", "col"), None),
            P(("row", "col"), None, None),
            P(("row", "col")),
        ),
        out_specs=(P(None, "row", "col"), P()),
        check_vma=False,
    )
```

```python
import functools
import math

import jax
import jax.numpy as jnp
import ml_dtypes
import numpy as np
from jax import lax
from jax.experimental import pallas as pl
from jax.experimental.pallas import tpu as pltpu
from jax.sharding import PartitionSpec as P

AXES = ("row", "col")
HBM = pl.BlockSpec(memory_space=pltpu.HBM)
SMEM = pl.BlockSpec(memory_space=pltpu.SMEM)
VMEM = pl.BlockSpec(memory_space=pltpu.VMEM)
MIB = 1024 * 1024
SIZES = {"x": 4, "y": 4, "z": 8, "core": 2}


def shifted(block, axis, distance):
    devices = range(lax.axis_size(axis))
    route = [(i - distance, i) for i in devices if i - distance in devices]
    return lax.ppermute(block, axis, route)


def dft_tables(window):
    index = np.arange(window)
    phases = (np.outer(index, index) % window) * (2.0 * math.pi / window)
    tables = []
    for part in (np.cos(phases), -np.sin(phases)):
        part = part / math.sqrt(window)
        high = part.astype(ml_dtypes.bfloat16)
        tables += [high, (part - high.astype(np.float64)).astype(ml_dtypes.bfloat16)]
    return np.stack(tables)


def split(value):
    high = value.astype(jnp.bfloat16)
    return high, (value - high.astype(jnp.float32)).astype(jnp.bfloat16)


def dot(first, second):
    return jnp.dot(first, second, preferred_element_type=jnp.float32)


def times_table(re, im, tables, sign):
    w = re.shape[0]
    high, low = split(jnp.concatenate([re, im], axis=0))
    by_re = dot(high, tables[0]) + (dot(low, tables[0]) + dot(high, tables[1]))
    by_im = dot(high, tables[2]) + (dot(low, tables[2]) + dot(high, tables[3]))
    if sign > 0:
        return by_re[:w] - by_im[w:], by_re[w:] + by_im[:w]
    return by_re[:w] + by_im[w:], by_re[w:] - by_im[:w]


def table_times(re, im, tables, sign):
    w = re.shape[1]
    high, low = split(jnp.concatenate([re, im], axis=1))
    by_re = dot(tables[0], high) + (dot(tables[0], low) + dot(tables[1], high))
    by_im = dot(tables[2], high) + (dot(tables[2], low) + dot(tables[3], high))
    if sign > 0:
        return by_re[:, :w] - by_im[:, w:], by_re[:, w:] + by_im[:, :w]
    return by_re[:, :w] + by_im[:, w:], by_re[:, w:] - by_im[:, :w]


def slots_kernel(
    window, tile,
    counts_ref, pos_ref, place_ref, object_hbm, right_hbm, below0_hbm, below1_hbm, corner_hbm,
    seam_right_hbm, seam_corner_hbm, probe_hbm, amp_hbm, tables_hbm,
    tile_out, right_out, below0_out, below1_out, corner_out, keep_out, send_out,
    ext, grad, probe, turned, amp, tables, patch, probe_grad, sems,
):
    w, t = window, tile
    e = t + w
    live = counts_ref[0]
    core, at_seam = place_ref[0], place_ref[1]
    moves = [
        (probe_hbm, probe),
        (tables_hbm, tables),
        (amp_hbm, amp),
        (object_hbm, ext.at[:, 0:t, 0:t]),
        (below0_hbm, ext.at[:, t:e, 0:w]),
        (below1_hbm, ext.at[:, t:e, w:t]),
    ]
    copies = [pltpu.make_async_copy(a, b, sems.at[i]) for i, (a, b) in enumerate(moves)]
    for copy in copies:
        copy.start()

    def choose(act):
        sources = [(right_hbm.at[:, 0:w], right_hbm.at[:, w:t], corner_hbm), (seam_right_hbm, corner_hbm, seam_corner_hbm)]
        for flag, parts in enumerate(sources):
            @pl.when(at_seam == flag)
            def _():
                for i, part in enumerate(parts):
                    act(pltpu.make_async_copy(part, ext.at[:, i * w : i * w + w, t:e], sems.at[6 + i]))

    choose(lambda copy: copy.start())
    grad[...] = jnp.zeros_like(grad)
    probe_grad[...] = jnp.zeros_like(probe_grad)
    copies[0].wait()

    def turn(slot, carry):
        row = lax.rem(lax.rem(pos_ref[slot, 0], t), w)
        col = lax.rem(lax.rem(pos_ref[slot, 1], t), w)
        for plane in range(2):
            turned[slot, plane] = pltpu.roll(pltpu.roll(probe[plane], row, 0), col, 1)
        return carry

    lax.fori_loop(0, live, turn, 0)
    for copy in copies[1:]:
        copy.wait()
    choose(lambda copy: copy.wait())
    moves = [
        (grad.at[:, t:e, t:e], corner_out),
        (grad.at[:, t:e, w:t], below1_out),
        (grad.at[:, t:e, 0:w], below0_out),
        (grad.at[:, 0:t, t:e], right_out),
        (grad.at[:, 0:t, 0:t], tile_out),
    ]
    results = [pltpu.make_async_copy(a, b, sems.at[i]) for i, (a, b) in enumerate(moves)]
    rows = lax.broadcasted_iota(jnp.int32, (w, w), 0)
    cols = lax.broadcasted_iota(jnp.int32, (w, w), 1)

    def one_slot(slot, carry):
        top = lax.rem(pos_ref[slot, 0], t)
        left = lax.rem(pos_ref[slot, 1], t)
        row_turn, col_turn = lax.rem(top, w), lax.rem(left, w)
        row_at = pl.multiple_of((top // w) * w, w)
        col_at = pl.multiple_of((left // w) * w, w)
        in_low = rows < row_turn
        in_right = cols < col_turn
        blocks = [
            (pl.ds(row_at, w), pl.ds(col_at, w), ~in_low & ~in_right),
            (pl.ds(row_at, w), pl.ds(col_at + w, w), ~in_low & in_right),
            (pl.ds(row_at + w, w), pl.ds(col_at, w), in_low & ~in_right),
            (pl.ds(row_at + w, w), pl.ds(col_at + w, w), in_low & in_right),
        ]
        for plane in range(2):
            parts = [ext[plane, at_rows, at_cols] for at_rows, at_cols, _ in blocks]
            patch[plane] = jnp.where(
                in_low, jnp.where(in_right, parts[3], parts[2]), jnp.where(in_right, parts[1], parts[0])
            )
        re = turned[slot, 0] * patch[0] - turned[slot, 1] * patch[1]
        im = turned[slot, 0] * patch[1] + turned[slot, 1] * patch[0]
        re, im = times_table(re, im, tables, 1)
        re, im = table_times(re, im, tables, 1)
        factor = 1.0 - amp[slot] / jnp.sqrt(re * re + im * im + 1.0)
        re, im = times_table(factor * re, factor * im, tables, -1)
        re, im = table_times(re, im, tables, -1)
        terms = (turned[slot, 0] * re + turned[slot, 1] * im, turned[slot, 0] * im - turned[slot, 1] * re)
        for at_rows, at_cols, mask in blocks:
            for plane in range(2):
                grad[plane, at_rows, at_cols] += jnp.where(mask, terms[plane], 0.0)

        @pl.when(slot == live - 1)
        def _():
            for copy in results:
                copy.start()

        terms = (patch[0] * re + patch[1] * im, patch[0] * im - patch[1] * re)
        for plane in range(2):
            term = pltpu.roll(terms[plane], lax.rem(w - row_turn, w), 0)
            probe_grad[plane] += pltpu.roll(term, lax.rem(w - col_turn, w), 1)
        return carry

    lax.fori_loop(0, live, one_slot, 0)
    keep = pltpu.make_async_copy(probe_grad.at[core], keep_out, sems.at[7])
    send = pltpu.make_async_copy(probe_grad.at[1 - core], send_out, sems.at[8])
    for copy in (send, keep):
        copy.start()
    for copy in (send, keep, *results):
        copy.wait()


def slot_terms(counts, positions, where, object_field, halos, probe, amplitudes):
    w, t = probe.shape[1], object_field.shape[1]
    slots = positions.shape[0]
    f32 = functools.partial(jax.ShapeDtypeStruct, dtype=jnp.float32)
    block = f32((2, w, w))
    return pl.pallas_call(
        functools.partial(slots_kernel, w, t),
        out_shape=[f32((2, t, t)), f32((2, t, w)), block, block, block, f32((w, w)), f32((w, w))],
        in_specs=[SMEM] * 3 + [HBM] * 10,
        out_specs=[HBM] * 7,
        scratch_shapes=[
            pltpu.VMEM((2, t + w, t + w), jnp.float32),
            pltpu.VMEM((2, t + w, t + w), jnp.float32),
            pltpu.VMEM((2, w, w), jnp.float32),
            pltpu.VMEM((slots, 2, w, w), jnp.float32),
            pltpu.VMEM((slots, w, w), jnp.float32),
            pltpu.VMEM((4, w, w), jnp.bfloat16),
            pltpu.VMEM((2, w, w), jnp.float32),
            pltpu.VMEM((2, w, w), jnp.float32),
            pltpu.SemaphoreType.DMA((9,)),
        ],
        compiler_params=pltpu.CompilerParams(vmem_limit_bytes=60 * MIB),
        cost_estimate=pl.CostEstimate(flops=3 * 10**9, bytes_accessed=14 * MIB, transcendentals=0),
        name="slot_terms",
    )(counts, positions, where, object_field, *halos, probe, amplitudes, jnp.asarray(dft_tables(w)))


def combine_kernel(half, tile_ref, left_ref, above0_ref, above1_ref, out_ref):
    w = left_ref.shape[2]
    first, second = tile_ref[:, :, :w] + left_ref[...], tile_ref[:, :, w:]

    @pl.when(pl.program_id(0) < half)
    def _():
        out_ref[:, :, :w] = first + above0_ref[...]
        out_ref[:, :, w:] = second + above1_ref[...]

    @pl.when(pl.program_id(0) >= half)
    def _():
        out_ref[:, :, :w] = first
        out_ref[:, :, w:] = second


def combined(tile_grad, from_left, above0, above1):
    t, w = tile_grad.shape[1], from_left.shape[2]
    step = w // 2
    half = w // step
    above = pl.BlockSpec((2, step, w), lambda i: (0, jnp.minimum(i, half - 1), 0))
    return pl.pallas_call(
        functools.partial(combine_kernel, half),
        out_shape=jax.ShapeDtypeStruct(tile_grad.shape, jnp.float32),
        grid=(t // step,),
        in_specs=[
            pl.BlockSpec((2, step, t), lambda i: (0, i, 0)),
            pl.BlockSpec((2, step, w), lambda i: (0, i, 0)),
            above,
            above,
        ],
        out_specs=pl.BlockSpec((2, step, t), lambda i: (0, i, 0)),
        cost_estimate=pl.CostEstimate(flops=10**6, bytes_accessed=6 * MIB, transcendentals=0),
        name="combined",
    )(tile_grad, from_left, above0, above1)


def place(x, y, z, core):
    return (z % 8 * 2 + y % 4 // 2) * 16 + y % 2 * 8 + x % 4 * 2 + core % 2


def moved(value, **distance):
    route = []
    for x in range(4):
        for y in range(4):
            for z in range(8):
                for core in range(2):
                    target = place(
                        x + distance.get("x", 0), y + distance.get("y", 0),
                        z + distance.get("z", 0), core + distance.get("core", 0),
                    )
                    route.append((place(x, y, z, core), target))
    return lax.ppermute(value, AXES, route)


def add_kernel(count, *refs):
    refs[count + (len(refs) - count) // 2][...] = functools.reduce(jnp.add, [part[...] for part in add_parts(refs[:count])])


def add_parts(refs):
    return [ref.at[i] for ref in refs for i in range(ref.shape[0])] if len(refs) == 1 else refs


def added(parts, *arrived):
    shape = parts[0].shape[-2:]
    n, m = len(parts), len(arrived)
    result = pl.pallas_call(
        functools.partial(add_kernel, n),
        out_shape=[jax.ShapeDtypeStruct(shape, jnp.float32)] + [jax.ShapeDtypeStruct(a.shape, a.dtype) for a in arrived],
        in_specs=[VMEM] * n + [HBM] * m,
        out_specs=[VMEM] + [HBM] * m,
        input_output_aliases={n + i: 1 + i for i in range(m)},
        compiler_params=pltpu.CompilerParams(vmem_limit_bytes=2 * MIB),
        name="added",
    )(*parts, *arrived)
    return result[0], result[1:]


def summed(value, axis, *arrived):
    parts = [moved(value, **{axis: d}) for d in range(1, SIZES[axis])]
    return added([value] + parts, *arrived)


def z_exchange(chunks):
    groups = [[place(x, y, z, c) for z in range(8)] for x in range(4) for y in range(4) for c in range(2)]
    return lax.all_to_all(chunks, AXES, 0, 0, tiled=True, axis_index_groups=groups)


def total(keep, send, core, above1, from_left, above0):
    if (lax.axis_size("row"), lax.axis_size("col")) != (16, 16):
        planes = jnp.where(core == 0, jnp.stack([keep, send]), jnp.stack([send, keep]))
        return lax.psum(planes, AXES), (above1, from_left, above0)
    w = keep.shape[0]
    value = keep + moved(send, core=1)
    value = z_exchange(value.reshape(8, w // 8, w))
    value, (above1, from_left) = added([value], above1, from_left)
    value, (above0,) = summed(value, "x", above0)
    value, _ = summed(value, "y")
    value = z_exchange(jnp.broadcast_to(value, (8,) + value.shape)).reshape(w, w)
    other = moved(value, core=1)
    planes = jnp.where(core == 0, jnp.stack([value, other]), jnp.stack([other, value]))
    return planes, (above1, from_left, above0)


def halos_in(object_field, window):
    rows, cols = lax.axis_size("row"), lax.axis_size("col")
    seam = cols // 2
    w = window
    own0 = object_field[:, :w, :w]
    plain = [(i + 1, i) for i in range(cols - 1) if i + 1 != seam]
    below0 = shifted(own0, "row", -1)
    below1 = shifted(object_field[:, :w, w:], "row", -1)
    right = lax.ppermute(object_field[:, :, :w], "col", plain)
    relayed = lax.ppermute(object_field[:, w:, :w], "col", [(seam, 0)])
    seam_right = lax.ppermute(own0, "col", [(seam, seam - 1)])
    route = [((r + 1) * cols + seam, r * cols + seam - 1) for r in range(rows - 1)]
    seam_corner = lax.ppermute(own0, AXES, route)
    first = lax.axis_index("col") == 0
    corner = lax.ppermute(jnp.where(first, relayed, below0), "col", plain + [(0, seam - 1)])
    return right, below0, below1, corner, seam_right, seam_corner


def shards(object_field, probe, positions, amplitudes, counts):
    window = probe.shape[1]
    col = lax.axis_index("col")
    core = col % 2
    at_seam = (col == lax.axis_size("col") // 2 - 1).astype(jnp.int32)
    halos = halos_in(object_field, window)
    where = jnp.stack([core, at_seam])
    tile_grad, right_grad, below0_grad, below1_grad, corner_grad, keep, send = slot_terms(
        counts, positions, where, object_field, halos, probe, amplitudes
    )
    corner_in = shifted(corner_grad, "col", 1)
    above1 = shifted(below1_grad, "row", 1)
    from_left = shifted(right_grad, "col", 1)
    above0 = shifted(below0_grad + corner_in, "row", 1)
    probe_total, (above1, from_left, above0) = total(keep, send, core, above1, from_left, above0)
    return combined(tile_grad, from_left, above0, above1), probe_total


def solution(mesh):
    return jax.shard_map(
        shards,
        mesh=mesh,
        in_specs=(
            P(None, "row", "col"),
            P(),
            P(("row", "col"), None),
            P(("row", "col"), None, None),
            P(("row", "col")),
        ),
        out_specs=(P(None, "row", "col"), P()),
        check_vma=False,
    )
```

```python
import functools
import math

import jax
import jax.numpy as jnp
import ml_dtypes
import numpy as np
from jax import lax
from jax.experimental import pallas as pl
from jax.experimental.pallas import tpu as pltpu
from jax.sharding import PartitionSpec as P

AXES = ("row", "col")
HBM = pl.BlockSpec(memory_space=pltpu.HBM)
SMEM = pl.BlockSpec(memory_space=pltpu.SMEM)
VMEM = pl.BlockSpec(memory_space=pltpu.VMEM)
MIB = 1024 * 1024
SIZES = {"x": 4, "y": 4, "z": 8, "core": 2}


def shifted(block, axis, distance):
    devices = range(lax.axis_size(axis))
    route = [(i - distance, i) for i in devices if i - distance in devices]
    return lax.ppermute(block, axis, route)


def dft_tables(window):
    index = np.arange(window)
    phases = (np.outer(index, index) % window) * (2.0 * math.pi / window)
    tables = []
    for part in (np.cos(phases), -np.sin(phases)):
        part = part / math.sqrt(window)
        high = part.astype(ml_dtypes.bfloat16)
        tables += [high, (part - high.astype(np.float64)).astype(ml_dtypes.bfloat16)]
    return np.stack(tables)


def split(value):
    high = value.astype(jnp.bfloat16)
    return high, (value - high.astype(jnp.float32)).astype(jnp.bfloat16)


def dot(first, second):
    return jnp.dot(first, second, preferred_element_type=jnp.float32)


def times_table(re, im, tables, sign):
    w = re.shape[0]
    high, low = split(jnp.concatenate([re, im], axis=0))
    by_re = dot(high, tables[0]) + (dot(low, tables[0]) + dot(high, tables[1]))
    by_im = dot(high, tables[2]) + (dot(low, tables[2]) + dot(high, tables[3]))
    if sign > 0:
        return by_re[:w] - by_im[w:], by_re[w:] + by_im[:w]
    return by_re[:w] + by_im[w:], by_re[w:] - by_im[:w]


def table_times(re, im, tables, sign):
    w = re.shape[1]
    high, low = split(jnp.concatenate([re, im], axis=1))
    by_re = dot(tables[0], high) + (dot(tables[0], low) + dot(tables[1], high))
    by_im = dot(tables[2], high) + (dot(tables[2], low) + dot(tables[3], high))
    if sign > 0:
        return by_re[:, :w] - by_im[:, w:], by_re[:, w:] + by_im[:, :w]
    return by_re[:, :w] + by_im[:, w:], by_re[:, w:] - by_im[:, :w]


def slots_kernel(
    window, tile,
    counts_ref, pos_ref, place_ref, object_hbm, right_hbm, below0_hbm, below1_hbm, corner_hbm,
    seam_right_hbm, seam_corner_hbm, probe_hbm, amp_hbm, tables_hbm,
    tile_out, right_out, below0_out, below1_out, corner_out, keep_out, send_out,
    ext, grad, probe, turned, amp, tables, patch, probe_grad, sems,
):
    w, t = window, tile
    e = t + w
    live = counts_ref[0]
    core, at_seam = place_ref[0], place_ref[1]
    moves = [
        (probe_hbm, probe),
        (tables_hbm, tables),
        (amp_hbm, amp),
        (object_hbm, ext.at[:, 0:t, 0:t]),
        (below0_hbm, ext.at[:, t:e, 0:w]),
        (below1_hbm, ext.at[:, t:e, w:t]),
    ]
    copies = [pltpu.make_async_copy(a, b, sems.at[i]) for i, (a, b) in enumerate(moves)]
    for copy in copies:
        copy.start()

    def choose(act):
        sources = [(right_hbm.at[:, 0:w], right_hbm.at[:, w:t], corner_hbm), (seam_right_hbm, corner_hbm, seam_corner_hbm)]
        for flag, parts in enumerate(sources):
            @pl.when(at_seam == flag)
            def _():
                for i, part in enumerate(parts):
                    act(pltpu.make_async_copy(part, ext.at[:, i * w : i * w + w, t:e], sems.at[6 + i]))

    choose(lambda copy: copy.start())
    grad[...] = jnp.zeros_like(grad)
    probe_grad[...] = jnp.zeros_like(probe_grad)
    copies[0].wait()

    def turn(slot, carry):
        row = lax.rem(lax.rem(pos_ref[slot, 0], t), w)
        col = lax.rem(lax.rem(pos_ref[slot, 1], t), w)
        for plane in range(2):
            turned[slot, plane] = pltpu.roll(pltpu.roll(probe[plane], row, 0), col, 1)
        return carry

    lax.fori_loop(0, live, turn, 0)
    for copy in copies[1:]:
        copy.wait()
    choose(lambda copy: copy.wait())
    moves = [
        (grad.at[:, t:e, t:e], corner_out),
        (grad.at[:, t:e, w:t], below1_out),
        (grad.at[:, t:e, 0:w], below0_out),
        (grad.at[:, 0:t, t:e], right_out),
        (grad.at[:, 0:t, 0:t], tile_out),
    ]
    results = [pltpu.make_async_copy(a, b, sems.at[i]) for i, (a, b) in enumerate(moves)]
    rows = lax.broadcasted_iota(jnp.int32, (w, w), 0)
    cols = lax.broadcasted_iota(jnp.int32, (w, w), 1)

    def one_slot(slot, carry):
        top = lax.rem(pos_ref[slot, 0], t)
        left = lax.rem(pos_ref[slot, 1], t)
        row_turn, col_turn = lax.rem(top, w), lax.rem(left, w)
        row_at = pl.multiple_of((top // w) * w, w)
        col_at = pl.multiple_of((left // w) * w, w)
        in_low = rows < row_turn
        in_right = cols < col_turn
        blocks = [
            (pl.ds(row_at, w), pl.ds(col_at, w), ~in_low & ~in_right),
            (pl.ds(row_at, w), pl.ds(col_at + w, w), ~in_low & in_right),
            (pl.ds(row_at + w, w), pl.ds(col_at, w), in_low & ~in_right),
            (pl.ds(row_at + w, w), pl.ds(col_at + w, w), in_low & in_right),
        ]
        for plane in range(2):
            parts = [ext[plane, at_rows, at_cols] for at_rows, at_cols, _ in blocks]
            patch[plane] = jnp.where(
                in_low, jnp.where(in_right, parts[3], parts[2]), jnp.where(in_right, parts[1], parts[0])
            )
        re = turned[slot, 0] * patch[0] - turned[slot, 1] * patch[1]
        im = turned[slot, 0] * patch[1] + turned[slot, 1] * patch[0]
        re, im = times_table(re, im, tables, 1)
        re, im = table_times(re, im, tables, 1)
        factor = 1.0 - amp[slot] / jnp.sqrt(re * re + im * im + 1.0)
        re, im = times_table(factor * re, factor * im, tables, -1)
        re, im = table_times(re, im, tables, -1)
        terms = (turned[slot, 0] * re + turned[slot, 1] * im, turned[slot, 0] * im - turned[slot, 1] * re)
        for at_rows, at_cols, mask in blocks:
            for plane in range(2):
                grad[plane, at_rows, at_cols] += jnp.where(mask, terms[plane], 0.0)

        @pl.when(slot == live - 1)
        def _():
            for copy in results:
                copy.start()

        terms = (patch[0] * re + patch[1] * im, patch[0] * im - patch[1] * re)
        for plane in range(2):
            term = pltpu.roll(terms[plane], lax.rem(w - row_turn, w), 0)
            probe_grad[plane] += pltpu.roll(term, lax.rem(w - col_turn, w), 1)
        return carry

    lax.fori_loop(0, live, one_slot, 0)
    keep = pltpu.make_async_copy(probe_grad.at[core], keep_out, sems.at[7])
    send = pltpu.make_async_copy(probe_grad.at[1 - core], send_out, sems.at[8])
    for copy in (send, keep):
        copy.start()
    for copy in (send, keep, *results):
        copy.wait()


def slot_terms(counts, positions, where, object_field, halos, probe, amplitudes):
    w, t = probe.shape[1], object_field.shape[1]
    slots = positions.shape[0]
    f32 = functools.partial(jax.ShapeDtypeStruct, dtype=jnp.float32)
    block = f32((2, w, w))
    return pl.pallas_call(
        functools.partial(slots_kernel, w, t),
        out_shape=[f32((2, t, t)), f32((2, t, w)), block, block, block, f32((w, w)), f32((w, w))],
        in_specs=[SMEM] * 3 + [HBM] * 10,
        out_specs=[HBM] * 7,
        scratch_shapes=[
            pltpu.VMEM((2, t + w, t + w), jnp.float32),
            pltpu.VMEM((2, t + w, t + w), jnp.float32),
            pltpu.VMEM((2, w, w), jnp.float32),
            pltpu.VMEM((slots, 2, w, w), jnp.float32),
            pltpu.VMEM((slots, w, w), jnp.float32),
            pltpu.VMEM((4, w, w), jnp.bfloat16),
            pltpu.VMEM((2, w, w), jnp.float32),
            pltpu.VMEM((2, w, w), jnp.float32),
            pltpu.SemaphoreType.DMA((9,)),
        ],
        compiler_params=pltpu.CompilerParams(vmem_limit_bytes=60 * MIB),
        cost_estimate=pl.CostEstimate(flops=3 * 10**9, bytes_accessed=14 * MIB, transcendentals=0),
        name="slot_terms",
    )(counts, positions, where, object_field, *halos, probe, amplitudes, jnp.asarray(dft_tables(w)))


def combine_kernel(half, tile_ref, left_ref, seam_ref, above0_ref, above1_ref, out_ref):
    w = left_ref.shape[2]
    first, second = tile_ref[:, :, :w] + (left_ref[...] + seam_ref[...]), tile_ref[:, :, w:]

    @pl.when(pl.program_id(0) < half)
    def _():
        out_ref[:, :, :w] = first + above0_ref[...]
        out_ref[:, :, w:] = second + above1_ref[...]

    @pl.when(pl.program_id(0) >= half)
    def _():
        out_ref[:, :, :w] = first
        out_ref[:, :, w:] = second


def combined(tile_grad, from_left, from_seam, above0, above1):
    t, w = tile_grad.shape[1], from_left.shape[2]
    step = w // 4
    half = w // step
    above = pl.BlockSpec((2, step, w), lambda i: (0, jnp.minimum(i, half - 1), 0))
    return pl.pallas_call(
        functools.partial(combine_kernel, half),
        out_shape=jax.ShapeDtypeStruct(tile_grad.shape, jnp.float32),
        grid=(t // step,),
        in_specs=[
            pl.BlockSpec((2, step, t), lambda i: (0, i, 0)),
            pl.BlockSpec((2, step, w), lambda i: (0, i, 0)),
            pl.BlockSpec((2, step, w), lambda i: (0, i, 0)),
            above,
            above,
        ],
        out_specs=pl.BlockSpec((2, step, t), lambda i: (0, i, 0)),
        cost_estimate=pl.CostEstimate(flops=10**6, bytes_accessed=6 * MIB, transcendentals=0),
        name="combined",
    )(tile_grad, from_left, from_seam, above0, above1)


def place(x, y, z, core):
    return (z % 8 * 2 + y % 4 // 2) * 16 + y % 2 * 8 + x % 4 * 2 + core % 2


def moved(value, **distance):
    route = []
    for x in range(4):
        for y in range(4):
            for z in range(8):
                for core in range(2):
                    target = place(
                        x + distance.get("x", 0), y + distance.get("y", 0),
                        z + distance.get("z", 0), core + distance.get("core", 0),
                    )
                    route.append((place(x, y, z, core), target))
    return lax.ppermute(value, AXES, route)


def add_kernel(groups, *refs):
    count = sum(groups)
    outs = refs[count + (len(refs) - count - len(groups)) // 2 :]
    at = 0
    for out, size in zip(outs, groups):
        parts = refs[at : at + size] if size > 1 else [refs[at].at[i] for i in range(refs[at].shape[0])]
        out[...] = functools.reduce(jnp.add, [part[...] for part in parts])
        at += size


def added(groups, *arrived, vmem=4):
    shapes = [group[0].shape[1:] if len(group) == 1 else group[0].shape for group in groups]
    parts = [part for group in groups for part in group]
    n, m, k = len(parts), len(arrived), len(groups)
    result = pl.pallas_call(
        functools.partial(add_kernel, [len(group) for group in groups]),
        out_shape=[jax.ShapeDtypeStruct(s, jnp.float32) for s in shapes]
        + [jax.ShapeDtypeStruct(a.shape, a.dtype) for a in arrived],
        in_specs=[VMEM] * n + [HBM] * m,
        out_specs=[VMEM] * k + [HBM] * m,
        input_output_aliases={n + i: k + i for i in range(m)},
        compiler_params=pltpu.CompilerParams(vmem_limit_bytes=vmem * MIB),
        name="added",
    )(*parts, *arrived)
    return result


def summed(value, axis, *arrived):
    parts = [moved(value, **{axis: d}) for d in range(1, SIZES[axis])]
    return added([[value] + parts], *arrived)


def z_exchange(chunks):
    groups = [[place(x, y, z, c) for z in range(8)] for x in range(4) for y in range(4) for c in range(2)]
    return lax.all_to_all(chunks, AXES, 0, 0, tiled=True, axis_index_groups=groups)


def total(value, above1, from_left, above0):
    w = value.shape[0]
    core = lax.axis_index("col") % 2
    value = z_exchange(value.reshape(8, w // 8, w))
    value = added([[value]])[0]
    value, above0, above1 = summed(value, "x", above0, above1)
    value, from_left = summed(value, "y", from_left)
    value = z_exchange(jnp.broadcast_to(value, (8,) + value.shape)).reshape(w, w)
    other = moved(value, core=1)
    planes = jnp.where(core == 0, jnp.stack([value, other]), jnp.stack([other, value]))
    return planes, (above1, from_left, above0)


def halos_in(object_field, window):
    rows, cols = lax.axis_size("row"), lax.axis_size("col")
    seam = cols // 2
    w = window
    own0 = object_field[:, :w, :w]
    plain = [(i + 1, i) for i in range(cols - 1) if i + 1 != seam]
    below0 = shifted(own0, "row", -1)
    below1 = shifted(object_field[:, :w, w:], "row", -1)
    right = lax.ppermute(object_field[:, :, :w], "col", plain)
    relayed = lax.ppermute(object_field[:, w:, :w], "col", [(seam, 0)])
    seam_right = lax.ppermute(own0, "col", [(seam, seam - 1)])
    route = [((r + 1) * cols + seam, r * cols + seam - 1) for r in range(rows - 1)]
    seam_corner = lax.ppermute(own0, AXES, route)
    first = lax.axis_index("col") == 0
    corner = lax.ppermute(jnp.where(first, relayed, below0), "col", plain + [(0, seam - 1)])
    return right, below0, below1, corner, seam_right, seam_corner


def shards(object_field, probe, positions, amplitudes, counts):
    window = probe.shape[1]
    col = lax.axis_index("col")
    core = col % 2
    at_seam = (col == lax.axis_size("col") // 2 - 1).astype(jnp.int32)
    halos = halos_in(object_field, window)
    where = jnp.stack([core, at_seam])
    tile_grad, right_grad, below0_grad, below1_grad, corner_grad, keep, send = slot_terms(
        counts, positions, where, object_field, halos, probe, amplitudes
    )
    corner_in = shifted(corner_grad, "col", 1)
    above1 = shifted(below1_grad, "row", 1)
    rows, cols = lax.axis_size("row"), lax.axis_size("col")
    staged = (rows, cols) == (16, 16)
    other = moved(send, core=1) if staged else send
    value, below0_grad, right_grad = added([[keep, other], [below0_grad, corner_in]], right_grad, vmem=60)
    above0 = shifted(below0_grad, "row", 1)
    plain = [(i, i + 1) for i in range(cols - 1) if i + 1 != cols // 2]
    from_left = lax.ppermute(right_grad, "col", plain)
    from_seam = lax.ppermute(right_grad, "col", [(cols // 2 - 1, cols // 2)])
    if staged:
        probe_total, (above1, from_left, above0) = total(value, above1, from_left, above0)
    else:
        probe_total = lax.psum(jnp.where(core == 0, jnp.stack([keep, send]), jnp.stack([send, keep])), AXES)
    return combined(tile_grad, from_left, from_seam, above0, above1), probe_total


def solution(mesh):
    return jax.shard_map(
        shards,
        mesh=mesh,
        in_specs=(
            P(None, "row", "col"),
            P(),
            P(("row", "col"), None),
            P(("row", "col"), None, None),
            P(("row", "col")),
        ),
        out_specs=(P(None, "row", "col"), P()),
        check_vma=False,
    )
```

```python
import functools
import math

import jax
import jax.numpy as jnp
import ml_dtypes
import numpy as np
from jax import lax
from jax.experimental import pallas as pl
from jax.experimental.pallas import tpu as pltpu
from jax.sharding import PartitionSpec as P

AXES = ("row", "col")
HBM = pl.BlockSpec(memory_space=pltpu.HBM)
SMEM = pl.BlockSpec(memory_space=pltpu.SMEM)
VMEM = pl.BlockSpec(memory_space=pltpu.VMEM)
MIB = 1024 * 1024
SIZES = {"x": 4, "y": 4, "z": 8, "core": 2}


def shifted(block, axis, distance):
    devices = range(lax.axis_size(axis))
    route = [(i - distance, i) for i in devices if i - distance in devices]
    return lax.ppermute(block, axis, route)


def dft_tables(window):
    index = np.arange(window)
    phases = (np.outer(index, index) % window) * (2.0 * math.pi / window)
    tables = []
    for part in (np.cos(phases), -np.sin(phases)):
        part = part / math.sqrt(window)
        high = part.astype(ml_dtypes.bfloat16)
        tables += [high, (part - high.astype(np.float64)).astype(ml_dtypes.bfloat16)]
    return np.stack(tables)


def split(value):
    high = value.astype(jnp.bfloat16)
    return high, (value - high.astype(jnp.float32)).astype(jnp.bfloat16)


def dot(first, second):
    return jnp.dot(first, second, preferred_element_type=jnp.float32)


def times_table(re, im, tables, sign):
    w = re.shape[0]
    high, low = split(jnp.concatenate([re, im], axis=0))
    by_re = dot(high, tables[0]) + (dot(low, tables[0]) + dot(high, tables[1]))
    by_im = dot(high, tables[2]) + (dot(low, tables[2]) + dot(high, tables[3]))
    if sign > 0:
        return by_re[:w] - by_im[w:], by_re[w:] + by_im[:w]
    return by_re[:w] + by_im[w:], by_re[w:] - by_im[:w]


def table_times(re, im, tables, sign):
    w = re.shape[1]
    high, low = split(jnp.concatenate([re, im], axis=1))
    by_re = dot(tables[0], high) + (dot(tables[0], low) + dot(tables[1], high))
    by_im = dot(tables[2], high) + (dot(tables[2], low) + dot(tables[3], high))
    if sign > 0:
        return by_re[:, :w] - by_im[:, w:], by_re[:, w:] + by_im[:, :w]
    return by_re[:, :w] + by_im[:, w:], by_re[:, w:] - by_im[:, :w]


def slots_kernel(
    window, tile,
    counts_ref, pos_ref, place_ref, object_hbm, right0_hbm, right1_hbm, below0_hbm, below1_hbm,
    corner_hbm, probe_hbm, amp_hbm, tables_hbm,
    tile_out, right_out, below0_out, below1_out, corner_out, keep_out, send_out,
    ext, grad, probe, turned, amp, tables, patch, probe_grad, sems,
):
    w, t = window, tile
    e = t + w
    live = counts_ref[0]
    core, at_seam = place_ref[0], place_ref[1]
    moves = [
        (probe_hbm, probe),
        (tables_hbm, tables),
        (amp_hbm, amp),
        (object_hbm, ext.at[:, 0:t, 0:t]),
        (right0_hbm, ext.at[:, 0:w, t:e]),
        (below0_hbm, ext.at[:, t:e, 0:w]),
        (below1_hbm, ext.at[:, t:e, w:t]),
    ]
    copies = [pltpu.make_async_copy(a, b, sems.at[i]) for i, (a, b) in enumerate(moves)]
    for copy in copies:
        copy.start()

    def choose(act):
        for flag, parts in enumerate([(right1_hbm, corner_hbm), (corner_hbm, right1_hbm)]):
            @pl.when(at_seam == flag)
            def _():
                for i, part in enumerate(parts):
                    act(pltpu.make_async_copy(part, ext.at[:, (i + 1) * w : (i + 2) * w, t:e], sems.at[7 + i]))

    choose(lambda copy: copy.start())
    grad[...] = jnp.zeros_like(grad)
    probe_grad[...] = jnp.zeros_like(probe_grad)
    copies[0].wait()

    def turn(slot, carry):
        row = lax.rem(lax.rem(pos_ref[slot, 0], t), w)
        col = lax.rem(lax.rem(pos_ref[slot, 1], t), w)
        for plane in range(2):
            turned[slot, plane] = pltpu.roll(pltpu.roll(probe[plane], row, 0), col, 1)
        return carry

    lax.fori_loop(0, live, turn, 0)
    for copy in copies[1:]:
        copy.wait()
    choose(lambda copy: copy.wait())
    moves = [
        (grad.at[:, t:e, t:e], corner_out),
        (grad.at[:, t:e, w:t], below1_out),
        (grad.at[:, t:e, 0:w], below0_out),
        (grad.at[:, 0:t, t:e], right_out),
        (grad.at[:, 0:t, 0:t], tile_out),
    ]
    results = [pltpu.make_async_copy(a, b, sems.at[i]) for i, (a, b) in enumerate(moves)]
    rows = lax.broadcasted_iota(jnp.int32, (w, w), 0)
    cols = lax.broadcasted_iota(jnp.int32, (w, w), 1)

    def one_slot(slot, carry):
        top = lax.rem(pos_ref[slot, 0], t)
        left = lax.rem(pos_ref[slot, 1], t)
        row_turn, col_turn = lax.rem(top, w), lax.rem(left, w)
        row_at = pl.multiple_of((top // w) * w, w)
        col_at = pl.multiple_of((left // w) * w, w)
        in_low = rows < row_turn
        in_right = cols < col_turn
        blocks = [
            (pl.ds(row_at, w), pl.ds(col_at, w), ~in_low & ~in_right),
            (pl.ds(row_at, w), pl.ds(col_at + w, w), ~in_low & in_right),
            (pl.ds(row_at + w, w), pl.ds(col_at, w), in_low & ~in_right),
            (pl.ds(row_at + w, w), pl.ds(col_at + w, w), in_low & in_right),
        ]
        for plane in range(2):
            parts = [ext[plane, at_rows, at_cols] for at_rows, at_cols, _ in blocks]
            patch[plane] = jnp.where(
                in_low, jnp.where(in_right, parts[3], parts[2]), jnp.where(in_right, parts[1], parts[0])
            )
        re = turned[slot, 0] * patch[0] - turned[slot, 1] * patch[1]
        im = turned[slot, 0] * patch[1] + turned[slot, 1] * patch[0]
        re, im = times_table(re, im, tables, 1)
        re, im = table_times(re, im, tables, 1)
        factor = 1.0 - amp[slot] / jnp.sqrt(re * re + im * im + 1.0)
        re, im = times_table(factor * re, factor * im, tables, -1)
        re, im = table_times(re, im, tables, -1)
        terms = (turned[slot, 0] * re + turned[slot, 1] * im, turned[slot, 0] * im - turned[slot, 1] * re)
        for at_rows, at_cols, mask in blocks:
            for plane in range(2):
                grad[plane, at_rows, at_cols] += jnp.where(mask, terms[plane], 0.0)

        @pl.when(slot == live - 1)
        def _():
            for copy in results:
                copy.start()

        terms = (patch[0] * re + patch[1] * im, patch[0] * im - patch[1] * re)
        for plane in range(2):
            term = pltpu.roll(terms[plane], lax.rem(w - row_turn, w), 0)
            probe_grad[plane] += pltpu.roll(term, lax.rem(w - col_turn, w), 1)
        return carry

    lax.fori_loop(0, live, one_slot, 0)
    keep = pltpu.make_async_copy(probe_grad.at[core], keep_out, sems.at[7])
    send = pltpu.make_async_copy(probe_grad.at[1 - core], send_out, sems.at[8])
    for copy in (send, keep):
        copy.start()
    for copy in (send, keep, *results):
        copy.wait()


def slot_terms(counts, positions, where, object_field, halos, probe, amplitudes):
    w, t = probe.shape[1], object_field.shape[1]
    slots = positions.shape[0]
    f32 = functools.partial(jax.ShapeDtypeStruct, dtype=jnp.float32)
    block = f32((2, w, w))
    return pl.pallas_call(
        functools.partial(slots_kernel, w, t),
        out_shape=[f32((2, t, t)), f32((2, t, w)), block, block, block, f32((w, w)), f32((w, w))],
        in_specs=[SMEM] * 3 + [HBM] * 9,
        out_specs=[HBM] * 7,
        scratch_shapes=[
            pltpu.VMEM((2, t + w, t + w), jnp.float32),
            pltpu.VMEM((2, t + w, t + w), jnp.float32),
            pltpu.VMEM((2, w, w), jnp.float32),
            pltpu.VMEM((slots, 2, w, w), jnp.float32),
            pltpu.VMEM((slots, w, w), jnp.float32),
            pltpu.VMEM((4, w, w), jnp.bfloat16),
            pltpu.VMEM((2, w, w), jnp.float32),
            pltpu.VMEM((2, w, w), jnp.float32),
            pltpu.SemaphoreType.DMA((9,)),
        ],
        compiler_params=pltpu.CompilerParams(vmem_limit_bytes=60 * MIB),
        cost_estimate=pl.CostEstimate(flops=3 * 10**9, bytes_accessed=14 * MIB, transcendentals=0),
        name="slot_terms",
    )(counts, positions, where, object_field, *halos, probe, amplitudes, jnp.asarray(dft_tables(w)))


def combine_kernel(
    window, place_ref, tile_hbm, left_hbm, seam_hbm, above0_hbm, above1_hbm, out_hbm, tile, side, above0, above1, sems
):
    w, t = window, tile.shape[1]
    after_seam = place_ref[2]
    mine = [
        pltpu.make_async_copy(tile_hbm.at[:, 0:w, :], tile.at[:, 0:w, :], sems.at[0]),
        pltpu.make_async_copy(tile_hbm.at[:, w:t, 0:w], tile.at[:, w:t, 0:w], sems.at[1]),
        pltpu.make_async_copy(above0_hbm, above0, sems.at[2]),
        pltpu.make_async_copy(above1_hbm, above1, sems.at[3]),
    ]
    for copy in mine:
        copy.start()

    def choose(act):
        for flag, source in enumerate((left_hbm, seam_hbm)):
            @pl.when(after_seam == flag)
            def _():
                act(pltpu.make_async_copy(source, side, sems.at[4]))

    choose(lambda copy: copy.start())
    for copy in mine:
        copy.wait()
    tile[:, 0:w, w:t] += above1[...]
    choose(lambda copy: copy.wait())
    tile[:, 0:w, 0:w] += above0[...] + side[:, 0:w]
    top = pltpu.make_async_copy(tile.at[:, 0:w, :], out_hbm.at[:, 0:w, :], sems.at[0])
    top.start()
    tile[:, w:t, 0:w] += side[:, w:t]
    low = pltpu.make_async_copy(tile.at[:, w:t, 0:w], out_hbm.at[:, w:t, 0:w], sems.at[1])
    low.start()
    top.wait()
    low.wait()


def combined(where, tile_grad, from_left, from_seam, above0, above1):
    t, w = tile_grad.shape[1], from_left.shape[2]
    return pl.pallas_call(
        functools.partial(combine_kernel, w),
        out_shape=jax.ShapeDtypeStruct(tile_grad.shape, jnp.float32),
        in_specs=[SMEM] + [HBM] * 5,
        out_specs=HBM,
        scratch_shapes=[
            pltpu.VMEM((2, t, t), jnp.float32),
            pltpu.VMEM((2, t, w), jnp.float32),
            pltpu.VMEM((2, w, w), jnp.float32),
            pltpu.VMEM((2, w, w), jnp.float32),
            pltpu.SemaphoreType.DMA((5,)),
        ],
        input_output_aliases={1: 0},
        compiler_params=pltpu.CompilerParams(vmem_limit_bytes=12 * MIB),
        cost_estimate=pl.CostEstimate(flops=10**6, bytes_accessed=6 * MIB, transcendentals=0),
        name="combined",
    )(where, tile_grad, from_left, from_seam, above0, above1)


def place(x, y, z, core):
    return (z % 8 * 2 + y % 4 // 2) * 16 + y % 2 * 8 + x % 4 * 2 + core % 2


def moved(value, **distance):
    route = []
    for x in range(4):
        for y in range(4):
            for z in range(8):
                for core in range(2):
                    target = place(
                        x + distance.get("x", 0), y + distance.get("y", 0),
                        z + distance.get("z", 0), core + distance.get("core", 0),
                    )
                    route.append((place(x, y, z, core), target))
    return lax.ppermute(value, AXES, route)


def add_kernel(groups, *refs):
    count = sum(groups)
    outs = refs[count + (len(refs) - count - len(groups)) // 2 :]
    at = 0
    for out, size in zip(outs, groups):
        parts = refs[at : at + size] if size > 1 else [refs[at].at[i] for i in range(refs[at].shape[0])]
        out[...] = functools.reduce(jnp.add, [part[...] for part in parts])
        at += size


def added(groups, *arrived, vmem=4):
    shapes = [group[0].shape[1:] if len(group) == 1 else group[0].shape for group in groups]
    parts = [part for group in groups for part in group]
    n, m, k = len(parts), len(arrived), len(groups)
    result = pl.pallas_call(
        functools.partial(add_kernel, [len(group) for group in groups]),
        out_shape=[jax.ShapeDtypeStruct(s, jnp.float32) for s in shapes]
        + [jax.ShapeDtypeStruct(a.shape, a.dtype) for a in arrived],
        in_specs=[VMEM] * n + [HBM] * m,
        out_specs=[VMEM] * k + [HBM] * m,
        input_output_aliases={n + i: k + i for i in range(m)},
        compiler_params=pltpu.CompilerParams(vmem_limit_bytes=vmem * MIB),
        name="added",
    )(*parts, *arrived)
    return result


def summed(value, axis, *arrived):
    parts = [moved(value, **{axis: d}) for d in range(1, SIZES[axis])]
    return added([[value] + parts], *arrived)


def z_exchange(chunks):
    groups = [[place(x, y, z, c) for z in range(8)] for x in range(4) for y in range(4) for c in range(2)]
    return lax.all_to_all(chunks, AXES, 0, 0, tiled=True, axis_index_groups=groups)


def halos_in(object_field, window):
    rows, cols = lax.axis_size("row"), lax.axis_size("col")
    col = lax.axis_index("col")
    seam = cols // 2
    w = window
    own0, own1 = object_field[:, :w, :w], object_field[:, w:, :w]
    plain = [(i + 1, i) for i in range(cols - 1) if i + 1 != seam]
    below0 = shifted(own0, "row", -1)
    below1 = shifted(object_field[:, :w, w:], "row", -1)
    relayed = lax.ppermute(own1, "col", [(seam, 0)])
    right0 = shifted(own0, "col", -1)
    route = [(r * cols + a, r * cols + b) for r in range(rows) for a, b in plain]
    route += [((r + 1) * cols + seam, r * cols + seam - 1) for r in range(rows - 1)]
    right1 = lax.ppermute(jnp.where(col == seam, own0, own1), AXES, route)
    corner = lax.ppermute(jnp.where(col == 0, relayed, below0), "col", plain + [(0, seam - 1)])
    return right0, right1, below0, below1, corner


def shards(object_field, probe, positions, amplitudes, counts):
    window = probe.shape[1]
    col = lax.axis_index("col")
    core = col % 2
    seam = lax.axis_size("col") // 2
    halos = halos_in(object_field, window)
    where = jnp.stack([core, (col == seam - 1).astype(jnp.int32), (col == seam).astype(jnp.int32)])
    tile_grad, right_grad, below0_grad, below1_grad, corner_grad, keep, send = slot_terms(
        counts, positions, where, object_field, halos, probe, amplitudes
    )
    corner_in = shifted(corner_grad, "col", 1)
    above1 = shifted(below1_grad, "row", 1)
    rows, cols = lax.axis_size("row"), lax.axis_size("col")
    plain = [(i, i + 1) for i in range(cols - 1) if i + 1 != seam]

    def halos_out(below0_grad, right_grad):
        above0 = shifted(below0_grad, "row", 1)
        from_left = lax.ppermute(right_grad, "col", plain)
        return above0, from_left, lax.ppermute(right_grad, "col", [(seam - 1, seam)])

    if (rows, cols) == (16, 16):
        value = keep + moved(send, core=1)
        value = z_exchange(value.reshape(8, window // 8, window))
        value, below0_grad, right_grad, above1 = added([[value], [below0_grad, corner_in]], right_grad, above1, vmem=8)
        above0, from_left, from_seam = halos_out(below0_grad, right_grad)
        value = summed(value, "x")[0]
        value, above0, from_left, from_seam = summed(value, "y", above0, from_left, from_seam)
        value = z_exchange(jnp.broadcast_to(value, (8,) + value.shape)).reshape(window, window)
        other = moved(value, core=1)
        probe_total = jnp.where(core == 0, jnp.stack([value, other]), jnp.stack([other, value]))
    else:
        above0, from_left, from_seam = halos_out(below0_grad + corner_in, right_grad)
        probe_total = lax.psum(jnp.where(core == 0, jnp.stack([keep, send]), jnp.stack([send, keep])), AXES)
    return combined(where, tile_grad, from_left, from_seam, above0, above1), probe_total


def solution(mesh):
    return jax.shard_map(
        shards,
        mesh=mesh,
        in_specs=(
            P(None, "row", "col"),
            P(),
            P(("row", "col"), None),
            P(("row", "col"), None, None),
            P(("row", "col")),
        ),
        out_specs=(P(None, "row", "col"), P()),
        check_vma=False,
    )
```

```python
import functools
import math

import jax
import jax.numpy as jnp
import ml_dtypes
import numpy as np
from jax import lax
from jax.experimental import pallas as pl
from jax.experimental.pallas import tpu as pltpu
from jax.sharding import PartitionSpec as P

AXES = ("row", "col")
HBM = pl.BlockSpec(memory_space=pltpu.HBM)
SMEM = pl.BlockSpec(memory_space=pltpu.SMEM)
VMEM = pl.BlockSpec(memory_space=pltpu.VMEM)
MIB = 1024 * 1024
SIZES = {"x": 4, "y": 4, "z": 8, "core": 2}


def shifted(block, axis, distance):
    devices = range(lax.axis_size(axis))
    route = [(i - distance, i) for i in devices if i - distance in devices]
    return lax.ppermute(block, axis, route)


def dft_tables(window):
    index = np.arange(window)
    phases = (np.outer(index, index) % window) * (2.0 * math.pi / window)
    tables = []
    for part in (np.cos(phases), -np.sin(phases)):
        part = part / math.sqrt(window)
        high = part.astype(ml_dtypes.bfloat16)
        tables += [high, (part - high.astype(np.float64)).astype(ml_dtypes.bfloat16)]
    return np.stack(tables)


def split(value):
    high = value.astype(jnp.bfloat16)
    return high, (value - high.astype(jnp.float32)).astype(jnp.bfloat16)


def dot(first, second):
    return jnp.dot(first, second, preferred_element_type=jnp.float32)


def times_table(re, im, tables, sign):
    w = re.shape[0]
    high, low = split(jnp.concatenate([re, im], axis=0))
    by_re = dot(high, tables[0]) + (dot(low, tables[0]) + dot(high, tables[1]))
    by_im = dot(high, tables[2]) + (dot(low, tables[2]) + dot(high, tables[3]))
    if sign > 0:
        return by_re[:w] - by_im[w:], by_re[w:] + by_im[:w]
    return by_re[:w] + by_im[w:], by_re[w:] - by_im[:w]


def table_times(re, im, tables, sign):
    w = re.shape[1]
    high, low = split(jnp.concatenate([re, im], axis=1))
    by_re = dot(tables[0], high) + (dot(tables[0], low) + dot(tables[1], high))
    by_im = dot(tables[2], high) + (dot(tables[2], low) + dot(tables[3], high))
    if sign > 0:
        return by_re[:, :w] - by_im[:, w:], by_re[:, w:] + by_im[:, :w]
    return by_re[:, :w] + by_im[:, w:], by_re[:, w:] - by_im[:, :w]


def slots_kernel(
    window, tile,
    counts_ref, pos_ref, place_ref, object_hbm, right0_hbm, right1_hbm, below0_hbm, below1_hbm,
    corner_hbm, probe_hbm, amp_hbm, tables_hbm,
    tile_out, right_out, below0_out, below1_out, corner_out, keep_out, send_out,
    ext, grad, probe, turned, amp, tables, patch, probe_grad, sems,
):
    w, t = window, tile
    e = t + w
    live = counts_ref[0]
    core, at_seam = place_ref[0], place_ref[1]
    moves = [
        (probe_hbm, probe),
        (tables_hbm, tables),
        (amp_hbm, amp),
        (object_hbm, ext.at[:, 0:t, 0:t]),
        (right0_hbm, ext.at[:, 0:w, t:e]),
        (below0_hbm, ext.at[:, t:e, 0:w]),
        (below1_hbm, ext.at[:, t:e, w:t]),
    ]
    copies = [pltpu.make_async_copy(a, b, sems.at[i]) for i, (a, b) in enumerate(moves)]
    for copy in copies:
        copy.start()

    def choose(act):
        for flag, parts in enumerate([(right1_hbm, corner_hbm), (corner_hbm, right1_hbm)]):
            @pl.when(at_seam == flag)
            def _():
                for i, part in enumerate(parts):
                    act(pltpu.make_async_copy(part, ext.at[:, (i + 1) * w : (i + 2) * w, t:e], sems.at[7 + i]))

    choose(lambda copy: copy.start())
    grad[...] = jnp.zeros_like(grad)
    probe_grad[...] = jnp.zeros_like(probe_grad)
    copies[0].wait()

    def turn(slot, carry):
        row = lax.rem(lax.rem(pos_ref[slot, 0], t), w)
        col = lax.rem(lax.rem(pos_ref[slot, 1], t), w)
        for plane in range(2):
            turned[slot, plane] = pltpu.roll(pltpu.roll(probe[plane], row, 0), col, 1)
        return carry

    lax.fori_loop(0, live, turn, 0)
    for copy in copies[1:]:
        copy.wait()
    choose(lambda copy: copy.wait())
    moves = [
        (grad.at[:, t:e, t:e], corner_out),
        (grad.at[:, t:e, w:t], below1_out),
        (grad.at[:, t:e, 0:w], below0_out),
        (grad.at[:, 0:t, t:e], right_out),
        (grad.at[:, 0:t, 0:t], tile_out),
    ]
    results = [pltpu.make_async_copy(a, b, sems.at[i]) for i, (a, b) in enumerate(moves)]
    rows = lax.broadcasted_iota(jnp.int32, (w, w), 0)
    cols = lax.broadcasted_iota(jnp.int32, (w, w), 1)

    def one_slot(slot, carry):
        top = lax.rem(pos_ref[slot, 0], t)
        left = lax.rem(pos_ref[slot, 1], t)
        row_turn, col_turn = lax.rem(top, w), lax.rem(left, w)
        row_at = pl.multiple_of((top // w) * w, w)
        col_at = pl.multiple_of((left // w) * w, w)
        in_low = rows < row_turn
        in_right = cols < col_turn
        blocks = [
            (pl.ds(row_at, w), pl.ds(col_at, w), ~in_low & ~in_right),
            (pl.ds(row_at, w), pl.ds(col_at + w, w), ~in_low & in_right),
            (pl.ds(row_at + w, w), pl.ds(col_at, w), in_low & ~in_right),
            (pl.ds(row_at + w, w), pl.ds(col_at + w, w), in_low & in_right),
        ]
        for plane in range(2):
            parts = [ext[plane, at_rows, at_cols] for at_rows, at_cols, _ in blocks]
            patch[plane] = jnp.where(
                in_low, jnp.where(in_right, parts[3], parts[2]), jnp.where(in_right, parts[1], parts[0])
            )
        re = turned[slot, 0] * patch[0] - turned[slot, 1] * patch[1]
        im = turned[slot, 0] * patch[1] + turned[slot, 1] * patch[0]
        re, im = times_table(re, im, tables, 1)
        re, im = table_times(re, im, tables, 1)
        factor = 1.0 - amp[slot] / jnp.sqrt(re * re + im * im + 1.0)
        re, im = times_table(factor * re, factor * im, tables, -1)
        re, im = table_times(re, im, tables, -1)
        terms = (turned[slot, 0] * re + turned[slot, 1] * im, turned[slot, 0] * im - turned[slot, 1] * re)
        for at_rows, at_cols, mask in blocks:
            for plane in range(2):
                grad[plane, at_rows, at_cols] += jnp.where(mask, terms[plane], 0.0)

        @pl.when(slot == live - 1)
        def _():
            for copy in results:
                copy.start()

        terms = (patch[0] * re + patch[1] * im, patch[0] * im - patch[1] * re)
        for plane in range(2):
            term = pltpu.roll(terms[plane], lax.rem(w - row_turn, w), 0)
            probe_grad[plane] += pltpu.roll(term, lax.rem(w - col_turn, w), 1)
        return carry

    lax.fori_loop(0, live, one_slot, 0)
    keep = pltpu.make_async_copy(probe_grad.at[core], keep_out, sems.at[7])
    send = pltpu.make_async_copy(probe_grad.at[1 - core], send_out, sems.at[8])
    for copy in (send, keep):
        copy.start()
    for copy in (send, keep, *results):
        copy.wait()


def slot_terms(counts, positions, where, object_field, halos, probe, amplitudes):
    w, t = probe.shape[1], object_field.shape[1]
    slots = positions.shape[0]
    f32 = functools.partial(jax.ShapeDtypeStruct, dtype=jnp.float32)
    block = f32((2, w, w))
    return pl.pallas_call(
        functools.partial(slots_kernel, w, t),
        out_shape=[f32((2, t, t)), f32((2, t, w)), block, block, block, f32((w, w)), f32((w, w))],
        in_specs=[SMEM] * 3 + [HBM] * 9,
        out_specs=[HBM] * 7,
        scratch_shapes=[
            pltpu.VMEM((2, t + w, t + w), jnp.float32),
            pltpu.VMEM((2, t + w, t + w), jnp.float32),
            pltpu.VMEM((2, w, w), jnp.float32),
            pltpu.VMEM((slots, 2, w, w), jnp.float32),
            pltpu.VMEM((slots, w, w), jnp.float32),
            pltpu.VMEM((4, w, w), jnp.bfloat16),
            pltpu.VMEM((2, w, w), jnp.float32),
            pltpu.VMEM((2, w, w), jnp.float32),
            pltpu.SemaphoreType.DMA((9,)),
        ],
        compiler_params=pltpu.CompilerParams(vmem_limit_bytes=60 * MIB),
        cost_estimate=pl.CostEstimate(flops=3 * 10**9, bytes_accessed=14 * MIB, transcendentals=0),
        name="slot_terms",
    )(counts, positions, where, object_field, *halos, probe, amplitudes, jnp.asarray(dft_tables(w)))


def combine_kernel(
    window, place_ref, tile_hbm, left_hbm, seam_hbm, above0_hbm, above1_hbm, out_hbm, tile, side, above0, above1, sems
):
    w, t = window, tile.shape[1]
    after_seam = place_ref[2]
    mine = [
        pltpu.make_async_copy(tile_hbm.at[:, 0:w, :], tile.at[:, 0:w, :], sems.at[0]),
        pltpu.make_async_copy(tile_hbm.at[:, w:t, 0:w], tile.at[:, w:t, 0:w], sems.at[1]),
        pltpu.make_async_copy(above0_hbm, above0, sems.at[2]),
        pltpu.make_async_copy(above1_hbm, above1, sems.at[3]),
    ]
    for copy in mine:
        copy.start()

    def choose(act):
        for flag, source in enumerate((left_hbm, seam_hbm)):
            @pl.when(after_seam == flag)
            def _():
                act(pltpu.make_async_copy(source, side, sems.at[4]))

    choose(lambda copy: copy.start())
    for copy in mine:
        copy.wait()
    tile[:, 0:w, w:t] += above1[...]
    choose(lambda copy: copy.wait())
    tile[:, 0:w, 0:w] += above0[...] + side[:, 0:w]
    top = pltpu.make_async_copy(tile.at[:, 0:w, :], out_hbm.at[:, 0:w, :], sems.at[0])
    top.start()
    tile[:, w:t, 0:w] += side[:, w:t]
    low = pltpu.make_async_copy(tile.at[:, w:t, 0:w], out_hbm.at[:, w:t, 0:w], sems.at[1])
    low.start()
    top.wait()
    low.wait()


def combined(where, tile_grad, from_left, from_seam, above0, above1):
    t, w = tile_grad.shape[1], from_left.shape[2]
    return pl.pallas_call(
        functools.partial(combine_kernel, w),
        out_shape=jax.ShapeDtypeStruct(tile_grad.shape, jnp.float32),
        in_specs=[SMEM] + [HBM] * 5,
        out_specs=HBM,
        scratch_shapes=[
            pltpu.VMEM((2, t, t), jnp.float32),
            pltpu.VMEM((2, t, w), jnp.float32),
            pltpu.VMEM((2, w, w), jnp.float32),
            pltpu.VMEM((2, w, w), jnp.float32),
            pltpu.SemaphoreType.DMA((5,)),
        ],
        input_output_aliases={1: 0},
        compiler_params=pltpu.CompilerParams(vmem_limit_bytes=12 * MIB),
        cost_estimate=pl.CostEstimate(flops=10**6, bytes_accessed=6 * MIB, transcendentals=0),
        name="combined",
    )(where, tile_grad, from_left, from_seam, above0, above1)


def place(x, y, z, core):
    return (z % 8 * 2 + y % 4 // 2) * 16 + y % 2 * 8 + x % 4 * 2 + core % 2


def moved(value, **distance):
    route = []
    for x in range(4):
        for y in range(4):
            for z in range(8):
                for core in range(2):
                    target = place(
                        x + distance.get("x", 0), y + distance.get("y", 0),
                        z + distance.get("z", 0), core + distance.get("core", 0),
                    )
                    route.append((place(x, y, z, core), target))
    return lax.ppermute(value, AXES, route)


def add_kernel(groups, *refs):
    count = sum(groups)
    outs = refs[count + (len(refs) - count - len(groups)) // 2 :]
    at = 0
    for out, size in zip(outs, groups):
        parts = refs[at : at + size] if size > 1 else [refs[at].at[i] for i in range(refs[at].shape[0])]
        out[...] = functools.reduce(jnp.add, [part[...] for part in parts])
        at += size


def added(groups, *arrived, vmem=4):
    shapes = [group[0].shape[1:] if len(group) == 1 else group[0].shape for group in groups]
    parts = [part for group in groups for part in group]
    n, m, k = len(parts), len(arrived), len(groups)
    result = pl.pallas_call(
        functools.partial(add_kernel, [len(group) for group in groups]),
        out_shape=[jax.ShapeDtypeStruct(s, jnp.float32) for s in shapes]
        + [jax.ShapeDtypeStruct(a.shape, a.dtype) for a in arrived],
        in_specs=[VMEM] * n + [HBM] * m,
        out_specs=[VMEM] * k + [HBM] * m,
        input_output_aliases={n + i: k + i for i in range(m)},
        compiler_params=pltpu.CompilerParams(vmem_limit_bytes=vmem * MIB),
        name="added",
    )(*parts, *arrived)
    return result


def neighbours(value, axis):
    return [moved(value, **{axis: d}) for d in range(1, SIZES[axis])]


def z_exchange(chunks):
    groups = [[place(x, y, z, c) for z in range(8)] for x in range(4) for y in range(4) for c in range(2)]
    return lax.all_to_all(chunks, AXES, 0, 0, tiled=True, axis_index_groups=groups)


def halos_in(object_field, window):
    rows, cols = lax.axis_size("row"), lax.axis_size("col")
    col = lax.axis_index("col")
    seam = cols // 2
    w = window
    own0, own1 = object_field[:, :w, :w], object_field[:, w:, :w]
    plain = [(i + 1, i) for i in range(cols - 1) if i + 1 != seam]
    below0 = shifted(own0, "row", -1)
    below1 = shifted(object_field[:, :w, w:], "row", -1)
    relayed = lax.ppermute(own1, "col", [(seam, 0)])
    right0 = shifted(own0, "col", -1)
    route = [(r * cols + a, r * cols + b) for r in range(rows) for a, b in plain]
    route += [((r + 1) * cols + seam, r * cols + seam - 1) for r in range(rows - 1)]
    right1 = lax.ppermute(jnp.where(col == seam, own0, own1), AXES, route)
    corner = lax.ppermute(jnp.where(col == 0, relayed, below0), "col", plain + [(0, seam - 1)])
    return right0, right1, below0, below1, corner


def shards(object_field, probe, positions, amplitudes, counts):
    window = probe.shape[1]
    col = lax.axis_index("col")
    core = col % 2
    seam = lax.axis_size("col") // 2
    halos = halos_in(object_field, window)
    where = jnp.stack([core, (col == seam - 1).astype(jnp.int32), (col == seam).astype(jnp.int32)])
    tile_grad, right_grad, below0_grad, below1_grad, corner_grad, keep, send = slot_terms(
        counts, positions, where, object_field, halos, probe, amplitudes
    )
    corner_in = shifted(corner_grad, "col", 1)
    above1 = shifted(below1_grad, "row", 1)
    rows, cols = lax.axis_size("row"), lax.axis_size("col")
    plain = [(i, i + 1) for i in range(cols - 1) if i + 1 != seam]

    from_left = lax.ppermute(right_grad, "col", plain)
    from_seam = lax.ppermute(right_grad, "col", [(seam - 1, seam)])
    if (rows, cols) == (16, 16):
        value = keep + moved(send, core=1)
        value = z_exchange(value.reshape(8, window // 8, window))
        value = added([[value]])[0]
        parts = [value] + neighbours(value, "x")
        value, below0_grad, above1, from_left = added([parts, [below0_grad, corner_in]], above1, from_left, vmem=8)
        above0 = shifted(below0_grad, "row", 1)
        value = added([[value] + neighbours(value, "y")])[0]
        value = z_exchange(jnp.broadcast_to(value, (8,) + value.shape)).reshape(window, window)
        other = moved(value, core=1)
        probe_total = jnp.where(core == 0, jnp.stack([value, other]), jnp.stack([other, value]))
    else:
        above0 = shifted(below0_grad + corner_in, "row", 1)
        probe_total = lax.psum(jnp.where(core == 0, jnp.stack([keep, send]), jnp.stack([send, keep])), AXES)
    return combined(where, tile_grad, from_left, from_seam, above0, above1), probe_total


def solution(mesh):
    return jax.shard_map(
        shards,
        mesh=mesh,
        in_specs=(
            P(None, "row", "col"),
            P(),
            P(("row", "col"), None),
            P(("row", "col"), None, None),
            P(("row", "col")),
        ),
        out_specs=(P(None, "row", "col"), P()),
        check_vma=False,
    )
```

```python
import functools
import math

import jax
import jax.numpy as jnp
import ml_dtypes
import numpy as np
from jax import lax
from jax.experimental import pallas as pl
from jax.experimental.pallas import tpu as pltpu
from jax.sharding import PartitionSpec as P

AXES = ("row", "col")
HBM = pl.BlockSpec(memory_space=pltpu.HBM)
SMEM = pl.BlockSpec(memory_space=pltpu.SMEM)
VMEM = pl.BlockSpec(memory_space=pltpu.VMEM)
MIB = 1024 * 1024
SIZES = {"x": 4, "y": 4, "z": 8, "core": 2}


def shifted(block, axis, distance):
    devices = range(lax.axis_size(axis))
    route = [(i - distance, i) for i in devices if i - distance in devices]
    return lax.ppermute(block, axis, route)


def dft_tables(window):
    index = np.arange(window)
    phases = (np.outer(index, index) % window) * (2.0 * math.pi / window)
    tables = []
    for part in (np.cos(phases), -np.sin(phases)):
        part = part / math.sqrt(window)
        high = part.astype(ml_dtypes.bfloat16)
        tables += [high, (part - high.astype(np.float64)).astype(ml_dtypes.bfloat16)]
    return np.stack(tables)


def split(value):
    high = value.astype(jnp.bfloat16)
    return high, (value - high.astype(jnp.float32)).astype(jnp.bfloat16)


def dot(first, second):
    return jnp.dot(first, second, preferred_element_type=jnp.float32)


def times_table(re, im, tables, sign):
    w = re.shape[0]
    high, low = split(jnp.concatenate([re, im], axis=0))
    by_re = dot(high, tables[0]) + (dot(low, tables[0]) + dot(high, tables[1]))
    by_im = dot(high, tables[2]) + (dot(low, tables[2]) + dot(high, tables[3]))
    if sign > 0:
        return by_re[:w] - by_im[w:], by_re[w:] + by_im[:w]
    return by_re[:w] + by_im[w:], by_re[w:] - by_im[:w]


def table_times(re, im, tables, sign):
    w = re.shape[1]
    high, low = split(jnp.concatenate([re, im], axis=1))
    by_re = dot(tables[0], high) + (dot(tables[0], low) + dot(tables[1], high))
    by_im = dot(tables[2], high) + (dot(tables[2], low) + dot(tables[3], high))
    if sign > 0:
        return by_re[:, :w] - by_im[:, w:], by_re[:, w:] + by_im[:, :w]
    return by_re[:, :w] + by_im[:, w:], by_re[:, w:] - by_im[:, :w]


def slots_kernel(
    window, tile,
    counts_ref, pos_ref, place_ref, object_hbm, below1_hbm, below0_hbm, right0_hbm, right1_hbm,
    corner_hbm, probe_hbm, amp_hbm, tables_hbm,
    tile_out, right_out, below0_out, below1_out, corner_out, keep_out, send_out,
    ext, grad, probe, turned, amp, tables, patch, probe_grad, sems,
):
    w, t = window, tile
    e = t + w
    live = counts_ref[0]
    core, at_seam = place_ref[0], place_ref[1]
    moves = [
        (probe_hbm, probe),
        (tables_hbm, tables),
        (amp_hbm, amp),
        (object_hbm, ext.at[:, 0:t, 0:t]),
        (right0_hbm, ext.at[:, 0:w, t:e]),
        (below0_hbm, ext.at[:, t:e, 0:w]),
        (below1_hbm, ext.at[:, t:e, w:t]),
    ]
    copies = [pltpu.make_async_copy(a, b, sems.at[i]) for i, (a, b) in enumerate(moves)]
    for copy in copies:
        copy.start()

    def choose(act):
        for flag, parts in enumerate([(right1_hbm, corner_hbm), (corner_hbm, right1_hbm)]):
            @pl.when(at_seam == flag)
            def _():
                for i, part in enumerate(parts):
                    act(pltpu.make_async_copy(part, ext.at[:, (i + 1) * w : (i + 2) * w, t:e], sems.at[7 + i]))

    choose(lambda copy: copy.start())
    grad[...] = jnp.zeros_like(grad)
    probe_grad[...] = jnp.zeros_like(probe_grad)
    copies[0].wait()

    def turn(slot, carry):
        row = lax.rem(lax.rem(pos_ref[slot, 0], t), w)
        col = lax.rem(lax.rem(pos_ref[slot, 1], t), w)
        for plane in range(2):
            turned[slot, plane] = pltpu.roll(pltpu.roll(probe[plane], row, 0), col, 1)
        return carry

    lax.fori_loop(0, live, turn, 0)
    for copy in copies[1:]:
        copy.wait()
    choose(lambda copy: copy.wait())
    moves = [
        (grad.at[:, t:e, t:e], corner_out),
        (grad.at[:, t:e, w:t], below1_out),
        (grad.at[:, t:e, 0:w], below0_out),
        (grad.at[:, 0:t, t:e], right_out),
        (grad.at[:, 0:t, 0:t], tile_out),
    ]
    results = [pltpu.make_async_copy(a, b, sems.at[i]) for i, (a, b) in enumerate(moves)]
    rows = lax.broadcasted_iota(jnp.int32, (w, w), 0)
    cols = lax.broadcasted_iota(jnp.int32, (w, w), 1)

    def one_slot(slot, carry):
        top = lax.rem(pos_ref[slot, 0], t)
        left = lax.rem(pos_ref[slot, 1], t)
        row_turn, col_turn = lax.rem(top, w), lax.rem(left, w)
        row_at = pl.multiple_of((top // w) * w, w)
        col_at = pl.multiple_of((left // w) * w, w)
        in_low = rows < row_turn
        in_right = cols < col_turn
        blocks = [
            (pl.ds(row_at, w), pl.ds(col_at, w), ~in_low & ~in_right),
            (pl.ds(row_at, w), pl.ds(col_at + w, w), ~in_low & in_right),
            (pl.ds(row_at + w, w), pl.ds(col_at, w), in_low & ~in_right),
            (pl.ds(row_at + w, w), pl.ds(col_at + w, w), in_low & in_right),
        ]
        for plane in range(2):
            parts = [ext[plane, at_rows, at_cols] for at_rows, at_cols, _ in blocks]
            patch[plane] = jnp.where(
                in_low, jnp.where(in_right, parts[3], parts[2]), jnp.where(in_right, parts[1], parts[0])
            )
        re = turned[slot, 0] * patch[0] - turned[slot, 1] * patch[1]
        im = turned[slot, 0] * patch[1] + turned[slot, 1] * patch[0]
        re, im = times_table(re, im, tables, 1)
        re, im = table_times(re, im, tables, 1)
        factor = 1.0 - amp[slot] / jnp.sqrt(re * re + im * im + 1.0)
        re, im = times_table(factor * re, factor * im, tables, -1)
        re, im = table_times(re, im, tables, -1)
        terms = (turned[slot, 0] * re + turned[slot, 1] * im, turned[slot, 0] * im - turned[slot, 1] * re)
        for at_rows, at_cols, mask in blocks:
            for plane in range(2):
                grad[plane, at_rows, at_cols] += jnp.where(mask, terms[plane], 0.0)

        @pl.when(slot == live - 1)
        def _():
            for copy in results:
                copy.start()

        terms = (patch[0] * re + patch[1] * im, patch[0] * im - patch[1] * re)
        for plane in range(2):
            term = pltpu.roll(terms[plane], lax.rem(w - row_turn, w), 0)
            probe_grad[plane] += pltpu.roll(term, lax.rem(w - col_turn, w), 1)
        return carry

    lax.fori_loop(0, live, one_slot, 0)
    keep = pltpu.make_async_copy(probe_grad.at[core], keep_out, sems.at[7])
    send = pltpu.make_async_copy(probe_grad.at[1 - core], send_out, sems.at[8])
    for copy in (send, keep):
        copy.start()
    for copy in (send, keep, *results):
        copy.wait()


def slot_terms(counts, positions, where, object_field, halos, probe, amplitudes):
    w, t = probe.shape[1], object_field.shape[1]
    slots = positions.shape[0]
    f32 = functools.partial(jax.ShapeDtypeStruct, dtype=jnp.float32)
    block = f32((2, w, w))
    return pl.pallas_call(
        functools.partial(slots_kernel, w, t),
        out_shape=[f32((2, t, t)), f32((2, t, w)), block, block, block, f32((w, w)), f32((w, w))],
        in_specs=[SMEM] * 3 + [HBM] * 9,
        out_specs=[HBM] * 7,
        scratch_shapes=[
            pltpu.VMEM((2, t + w, t + w), jnp.float32),
            pltpu.VMEM((2, t + w, t + w), jnp.float32),
            pltpu.VMEM((2, w, w), jnp.float32),
            pltpu.VMEM((slots, 2, w, w), jnp.float32),
            pltpu.VMEM((slots, w, w), jnp.float32),
            pltpu.VMEM((4, w, w), jnp.bfloat16),
            pltpu.VMEM((2, w, w), jnp.float32),
            pltpu.VMEM((2, w, w), jnp.float32),
            pltpu.SemaphoreType.DMA((9,)),
        ],
        compiler_params=pltpu.CompilerParams(vmem_limit_bytes=60 * MIB),
        cost_estimate=pl.CostEstimate(flops=3 * 10**9, bytes_accessed=14 * MIB, transcendentals=0),
        name="slot_terms",
    )(counts, positions, where, object_field, *halos, probe, amplitudes, jnp.asarray(dft_tables(w)))


def combine_kernel(
    window, place_ref, tile_hbm, left_hbm, seam_hbm, upper_hbm, lower_hbm, above1_hbm, out_hbm, tile, side, above0, above1, sems
):
    w, t = window, tile.shape[1]
    after_seam = place_ref[2]
    mine = [
        pltpu.make_async_copy(tile_hbm.at[:, 0:w, :], tile.at[:, 0:w, :], sems.at[0]),
        pltpu.make_async_copy(tile_hbm.at[:, w:t, 0:w], tile.at[:, w:t, 0:w], sems.at[1]),
        pltpu.make_async_copy(upper_hbm, above0.at[:, 0 : w // 2], sems.at[2]),
        pltpu.make_async_copy(lower_hbm, above0.at[:, w // 2 : w], sems.at[5]),
        pltpu.make_async_copy(above1_hbm, above1, sems.at[3]),
    ]
    for copy in mine:
        copy.start()

    def choose(act):
        for flag, source in enumerate((left_hbm, seam_hbm)):
            @pl.when(after_seam == flag)
            def _():
                act(pltpu.make_async_copy(source, side, sems.at[4]))

    choose(lambda copy: copy.start())
    for copy in mine:
        copy.wait()
    tile[:, 0:w, w:t] += above1[...]
    choose(lambda copy: copy.wait())
    tile[:, 0:w, 0:w] += above0[...] + side[:, 0:w]
    top = pltpu.make_async_copy(tile.at[:, 0:w, :], out_hbm.at[:, 0:w, :], sems.at[0])
    top.start()
    tile[:, w:t, 0:w] += side[:, w:t]
    low = pltpu.make_async_copy(tile.at[:, w:t, 0:w], out_hbm.at[:, w:t, 0:w], sems.at[1])
    low.start()
    top.wait()
    low.wait()


def combined(where, tile_grad, from_left, from_seam, upper, lower, above1):
    t, w = tile_grad.shape[1], from_left.shape[2]
    return pl.pallas_call(
        functools.partial(combine_kernel, w),
        out_shape=jax.ShapeDtypeStruct(tile_grad.shape, jnp.float32),
        in_specs=[SMEM] + [HBM] * 6,
        out_specs=HBM,
        scratch_shapes=[
            pltpu.VMEM((2, t, t), jnp.float32),
            pltpu.VMEM((2, t, w), jnp.float32),
            pltpu.VMEM((2, w, w), jnp.float32),
            pltpu.VMEM((2, w, w), jnp.float32),
            pltpu.SemaphoreType.DMA((6,)),
        ],
        input_output_aliases={1: 0},
        compiler_params=pltpu.CompilerParams(vmem_limit_bytes=12 * MIB),
        cost_estimate=pl.CostEstimate(flops=10**6, bytes_accessed=6 * MIB, transcendentals=0),
        name="combined",
    )(where, tile_grad, from_left, from_seam, upper, lower, above1)


def place(x, y, z, core):
    return (z % 8 * 2 + y % 4 // 2) * 16 + y % 2 * 8 + x % 4 * 2 + core % 2


def moved(value, **distance):
    route = []
    for x in range(4):
        for y in range(4):
            for z in range(8):
                for core in range(2):
                    target = place(
                        x + distance.get("x", 0), y + distance.get("y", 0),
                        z + distance.get("z", 0), core + distance.get("core", 0),
                    )
                    route.append((place(x, y, z, core), target))
    return lax.ppermute(value, AXES, route)


def add_kernel(groups, *refs):
    count = sum(groups)
    outs = refs[count + (len(refs) - count - len(groups)) // 2 :]
    at = 0
    for out, size in zip(outs, groups):
        parts = refs[at : at + size] if size > 1 else [refs[at].at[i] for i in range(refs[at].shape[0])]
        out[...] = functools.reduce(jnp.add, [part[...] for part in parts])
        at += size


def added(groups, *arrived, vmem=4):
    shapes = [group[0].shape[1:] if len(group) == 1 else group[0].shape for group in groups]
    parts = [part for group in groups for part in group]
    n, m, k = len(parts), len(arrived), len(groups)
    result = pl.pallas_call(
        functools.partial(add_kernel, [len(group) for group in groups]),
        out_shape=[jax.ShapeDtypeStruct(s, jnp.float32) for s in shapes]
        + [jax.ShapeDtypeStruct(a.shape, a.dtype) for a in arrived],
        in_specs=[VMEM] * n + [HBM] * m,
        out_specs=[VMEM] * k + [HBM] * m,
        input_output_aliases={n + i: k + i for i in range(m)},
        compiler_params=pltpu.CompilerParams(vmem_limit_bytes=vmem * MIB),
        name="added",
    )(*parts, *arrived)
    return result


def neighbours(value, axis):
    return [moved(value, **{axis: d}) for d in range(1, SIZES[axis])]


def middle_kernel(first, second, third, fourth, below_ref, corner_ref, *refs):
    sum_out, upper_out, lower_out = refs[2:5]
    half = upper_out.shape[1]
    sum_out[...] = first[...] + second[...] + third[...] + fourth[...]
    upper_out[...] = below_ref[:, :half] + corner_ref[:, :half]
    lower_out[...] = below_ref[:, half:] + corner_ref[:, half:]


def middle(parts, below0, corner, above1, from_left):
    f32 = functools.partial(jax.ShapeDtypeStruct, dtype=jnp.float32)
    planes, w, _ = below0.shape
    half = f32((planes, w // 2, w))
    return pl.pallas_call(
        middle_kernel,
        out_shape=[f32(parts[0].shape), half, half, f32(above1.shape), f32(from_left.shape)],
        in_specs=[VMEM] * 6 + [HBM] * 2,
        out_specs=[VMEM] * 3 + [HBM] * 2,
        input_output_aliases={6: 3, 7: 4},
        compiler_params=pltpu.CompilerParams(vmem_limit_bytes=8 * MIB),
        name="middle",
    )(*parts, below0, corner, above1, from_left)


def planes_kernel(place_ref, own_hbm, other_hbm, out_hbm, sems):
    core = place_ref[0]
    copies = [
        pltpu.make_async_copy(own_hbm, out_hbm.at[core], sems.at[0]),
        pltpu.make_async_copy(other_hbm, out_hbm.at[1 - core], sems.at[1]),
    ]
    for copy in copies:
        copy.start()
    for copy in copies:
        copy.wait()


def both_planes(where, own, other):
    return pl.pallas_call(
        planes_kernel,
        out_shape=jax.ShapeDtypeStruct((2,) + own.shape, own.dtype),
        in_specs=[SMEM, HBM, HBM],
        out_specs=HBM,
        scratch_shapes=[pltpu.SemaphoreType.DMA((2,))],
        compiler_params=pltpu.CompilerParams(vmem_limit_bytes=2 * MIB),
        name="both_planes",
    )(where, own, other)


def z_exchange(chunks):
    groups = [[place(x, y, z, c) for z in range(8)] for x in range(4) for y in range(4) for c in range(2)]
    return lax.all_to_all(chunks, AXES, 0, 0, tiled=True, axis_index_groups=groups)


def halos_in(object_field, window):
    rows, cols = lax.axis_size("row"), lax.axis_size("col")
    col = lax.axis_index("col")
    seam = cols // 2
    w = window
    own0, own1 = object_field[:, :w, :w], object_field[:, w:, :w]
    plain = [(i + 1, i) for i in range(cols - 1) if i + 1 != seam]
    below0 = shifted(own0, "row", -1)
    below1 = shifted(object_field[:, :w, w:], "row", -1)
    relayed = lax.ppermute(own1, "col", [(seam, 0)])
    right0 = shifted(own0, "col", -1)
    route = [(r * cols + a, r * cols + b) for r in range(rows) for a, b in plain]
    route += [((r + 1) * cols + seam, r * cols + seam - 1) for r in range(rows - 1)]
    right1 = lax.ppermute(jnp.where(col == seam, own0, own1), AXES, route)
    corner = lax.ppermute(jnp.where(col == 0, relayed, below0), "col", plain + [(0, seam - 1)])
    return below1, below0, right0, right1, corner


def shards(object_field, probe, positions, amplitudes, counts):
    window = probe.shape[1]
    col = lax.axis_index("col")
    core = col % 2
    seam = lax.axis_size("col") // 2
    halos = halos_in(object_field, window)
    where = jnp.stack([core, (col == seam - 1).astype(jnp.int32), (col == seam).astype(jnp.int32)])
    tile_grad, right_grad, below0_grad, below1_grad, corner_grad, keep, send = slot_terms(
        counts, positions, where, object_field, halos, probe, amplitudes
    )
    corner_in = shifted(corner_grad, "col", 1)
    above1 = shifted(below1_grad, "row", 1)
    rows, cols = lax.axis_size("row"), lax.axis_size("col")
    plain = [(i, i + 1) for i in range(cols - 1) if i + 1 != seam]

    from_left = lax.ppermute(right_grad, "col", plain)
    from_seam = lax.ppermute(right_grad, "col", [(seam - 1, seam)])
    if (rows, cols) == (16, 16):
        value = keep + moved(send, core=1)
        value = z_exchange(value.reshape(8, window // 8, window))
        value = added([[value]])[0]
        parts = [value] + neighbours(value, "x")
        value, upper, lower, above1, from_left = middle(parts, below0_grad, corner_in, above1, from_left)
        upper = shifted(upper, "row", 1)
        lower = shifted(lower, "row", 1)
        value, upper = added([[value] + neighbours(value, "y")], upper)
        value = z_exchange(jnp.broadcast_to(value, (8,) + value.shape)).reshape(window, window)
        other = moved(value, core=1)
        probe_total = both_planes(where, value, other)
    else:
        above0 = shifted(below0_grad + corner_in, "row", 1)
        upper, lower = above0[:, : window // 2], above0[:, window // 2 :]
        probe_total = lax.psum(jnp.where(core == 0, jnp.stack([keep, send]), jnp.stack([send, keep])), AXES)
    return combined(where, tile_grad, from_left, from_seam, upper, lower, above1), probe_total


def solution(mesh):
    return jax.shard_map(
        shards,
        mesh=mesh,
        in_specs=(
            P(None, "row", "col"),
            P(),
            P(("row", "col"), None),
            P(("row", "col"), None, None),
            P(("row", "col")),
        ),
        out_specs=(P(None, "row", "col"), P()),
        check_vma=False,
    )
```

```python
import functools
import math

import jax
import jax.numpy as jnp
import ml_dtypes
import numpy as np
from jax import lax
from jax.experimental import pallas as pl
from jax.experimental.pallas import tpu as pltpu
from jax.sharding import PartitionSpec as P

AXES = ("row", "col")
HBM = pl.BlockSpec(memory_space=pltpu.HBM)
SMEM = pl.BlockSpec(memory_space=pltpu.SMEM)
VMEM = pl.BlockSpec(memory_space=pltpu.VMEM)
MIB = 1024 * 1024
SIZES = {"x": 4, "y": 4, "z": 8, "core": 2}


def shifted(block, axis, distance):
    devices = range(lax.axis_size(axis))
    route = [(i - distance, i) for i in devices if i - distance in devices]
    return lax.ppermute(block, axis, route)


def dft_tables(window):
    index = np.arange(window)
    phases = (np.outer(index, index) % window) * (2.0 * math.pi / window)
    tables = []
    for part in (np.cos(phases), -np.sin(phases)):
        part = part / math.sqrt(window)
        high = part.astype(ml_dtypes.bfloat16)
        tables += [high, (part - high.astype(np.float64)).astype(ml_dtypes.bfloat16)]
    return np.stack(tables)


def split(value):
    high = value.astype(jnp.bfloat16)
    return high, (value - high.astype(jnp.float32)).astype(jnp.bfloat16)


def dot(first, second):
    return jnp.dot(first, second, preferred_element_type=jnp.float32)


def times_table(re, im, tables, sign):
    w = re.shape[0]
    high, low = split(jnp.concatenate([re, im], axis=0))
    by_re = dot(high, tables[0]) + (dot(low, tables[0]) + dot(high, tables[1]))
    by_im = dot(high, tables[2]) + (dot(low, tables[2]) + dot(high, tables[3]))
    if sign > 0:
        return by_re[:w] - by_im[w:], by_re[w:] + by_im[:w]
    return by_re[:w] + by_im[w:], by_re[w:] - by_im[:w]


def table_times(re, im, tables, sign):
    w = re.shape[1]
    high, low = split(jnp.concatenate([re, im], axis=1))
    by_re = dot(tables[0], high) + (dot(tables[0], low) + dot(tables[1], high))
    by_im = dot(tables[2], high) + (dot(tables[2], low) + dot(tables[3], high))
    if sign > 0:
        return by_re[:, :w] - by_im[:, w:], by_re[:, w:] + by_im[:, :w]
    return by_re[:, :w] + by_im[:, w:], by_re[:, w:] - by_im[:, :w]


def slots_kernel(
    window, tile,
    counts_ref, pos_ref, place_ref, object_hbm, below1_hbm, below0_hbm, right0_hbm, right1_hbm,
    corner_hbm, probe_hbm, amp_hbm, tables_hbm,
    tile_out, right_out, below0_out, below1_out, corner_out, keep_out, send_out,
    ext, grad, probe, turned, amp, tables, patch, probe_grad, sems,
):
    w, t = window, tile
    e = t + w
    live = counts_ref[0]
    core, at_seam = place_ref[0], place_ref[1]
    moves = [
        (probe_hbm, probe),
        (tables_hbm, tables),
        (amp_hbm, amp),
        (object_hbm, ext.at[:, 0:t, 0:t]),
        (right0_hbm, ext.at[:, 0:w, t:e]),
        (below0_hbm, ext.at[:, t:e, 0:w]),
        (below1_hbm, ext.at[:, t:e, w:t]),
    ]
    copies = [pltpu.make_async_copy(a, b, sems.at[i]) for i, (a, b) in enumerate(moves)]
    for copy in copies:
        copy.start()

    def choose(act):
        for flag, parts in enumerate([(right1_hbm, corner_hbm), (corner_hbm, right1_hbm)]):
            @pl.when(at_seam == flag)
            def _():
                for i, part in enumerate(parts):
                    act(pltpu.make_async_copy(part, ext.at[:, (i + 1) * w : (i + 2) * w, t:e], sems.at[7 + i]))

    choose(lambda copy: copy.start())
    grad[...] = jnp.zeros_like(grad)
    probe_grad[...] = jnp.zeros_like(probe_grad)
    copies[0].wait()

    def turn(slot, carry):
        row = lax.rem(lax.rem(pos_ref[slot, 0], t), w)
        col = lax.rem(lax.rem(pos_ref[slot, 1], t), w)
        for plane in range(2):
            turned[slot, plane] = pltpu.roll(pltpu.roll(probe[plane], row, 0), col, 1)
        return carry

    lax.fori_loop(0, live, turn, 0)
    for copy in copies[1:]:
        copy.wait()
    choose(lambda copy: copy.wait())
    moves = [
        (grad.at[:, t:e, t:e], corner_out),
        (grad.at[:, t:e, w:t], below1_out),
        (grad.at[:, t:e, 0:w], below0_out),
        (grad.at[:, 0:t, t:e], right_out),
        (grad.at[:, 0:t, 0:t], tile_out),
    ]
    results = [pltpu.make_async_copy(a, b, sems.at[i]) for i, (a, b) in enumerate(moves)]
    rows = lax.broadcasted_iota(jnp.int32, (w, w), 0)
    cols = lax.broadcasted_iota(jnp.int32, (w, w), 1)

    def one_slot(slot, carry):
        top = lax.rem(pos_ref[slot, 0], t)
        left = lax.rem(pos_ref[slot, 1], t)
        row_turn, col_turn = lax.rem(top, w), lax.rem(left, w)
        row_at = pl.multiple_of((top // w) * w, w)
        col_at = pl.multiple_of((left // w) * w, w)
        in_low = rows < row_turn
        in_right = cols < col_turn
        blocks = [
            (pl.ds(row_at, w), pl.ds(col_at, w), ~in_low & ~in_right),
            (pl.ds(row_at, w), pl.ds(col_at + w, w), ~in_low & in_right),
            (pl.ds(row_at + w, w), pl.ds(col_at, w), in_low & ~in_right),
            (pl.ds(row_at + w, w), pl.ds(col_at + w, w), in_low & in_right),
        ]
        for plane in range(2):
            parts = [ext[plane, at_rows, at_cols] for at_rows, at_cols, _ in blocks]
            patch[plane] = jnp.where(
                in_low, jnp.where(in_right, parts[3], parts[2]), jnp.where(in_right, parts[1], parts[0])
            )
        re = turned[slot, 0] * patch[0] - turned[slot, 1] * patch[1]
        im = turned[slot, 0] * patch[1] + turned[slot, 1] * patch[0]
        re, im = times_table(re, im, tables, 1)
        re, im = table_times(re, im, tables, 1)
        factor = 1.0 - amp[slot] / jnp.sqrt(re * re + im * im + 1.0)
        re, im = times_table(factor * re, factor * im, tables, -1)
        re, im = table_times(re, im, tables, -1)
        terms = (turned[slot, 0] * re + turned[slot, 1] * im, turned[slot, 0] * im - turned[slot, 1] * re)
        for at_rows, at_cols, mask in blocks:
            for plane in range(2):
                grad[plane, at_rows, at_cols] += jnp.where(mask, terms[plane], 0.0)

        @pl.when(slot == live - 1)
        def _():
            for copy in results:
                copy.start()

        terms = (patch[0] * re + patch[1] * im, patch[0] * im - patch[1] * re)
        for plane in range(2):
            term = pltpu.roll(terms[plane], lax.rem(w - row_turn, w), 0)
            probe_grad[plane] += pltpu.roll(term, lax.rem(w - col_turn, w), 1)
        return carry

    lax.fori_loop(0, live, one_slot, 0)
    keep = pltpu.make_async_copy(probe_grad.at[core], keep_out, sems.at[7])
    send = pltpu.make_async_copy(probe_grad.at[1 - core], send_out, sems.at[8])
    for copy in (send, keep):
        copy.start()
    for copy in (send, keep, *results):
        copy.wait()


def slot_terms(counts, positions, where, object_field, halos, probe, amplitudes):
    w, t = probe.shape[1], object_field.shape[1]
    slots = positions.shape[0]
    f32 = functools.partial(jax.ShapeDtypeStruct, dtype=jnp.float32)
    block = f32((2, w, w))
    return pl.pallas_call(
        functools.partial(slots_kernel, w, t),
        out_shape=[f32((2, t, t)), f32((2, t, w)), block, block, block, f32((w, w)), f32((w, w))],
        in_specs=[SMEM] * 3 + [HBM] * 9,
        out_specs=[HBM] * 7,
        scratch_shapes=[
            pltpu.VMEM((2, t + w, t + w), jnp.float32),
            pltpu.VMEM((2, t + w, t + w), jnp.float32),
            pltpu.VMEM((2, w, w), jnp.float32),
            pltpu.VMEM((slots, 2, w, w), jnp.float32),
            pltpu.VMEM((slots, w, w), jnp.float32),
            pltpu.VMEM((4, w, w), jnp.bfloat16),
            pltpu.VMEM((2, w, w), jnp.float32),
            pltpu.VMEM((2, w, w), jnp.float32),
            pltpu.SemaphoreType.DMA((9,)),
        ],
        compiler_params=pltpu.CompilerParams(vmem_limit_bytes=60 * MIB),
        cost_estimate=pl.CostEstimate(flops=3 * 10**9, bytes_accessed=14 * MIB, transcendentals=0),
        name="slot_terms",
    )(counts, positions, where, object_field, *halos, probe, amplitudes, jnp.asarray(dft_tables(w)))


def combine_kernel(
    window, place_ref, tile_hbm, left_hbm, seam_hbm, above0_hbm, above1_hbm, out_hbm, tile, side, above0, above1, sems
):
    w, t = window, tile.shape[1]
    after_seam = place_ref[2]
    mine = [
        pltpu.make_async_copy(tile_hbm.at[:, 0:w, :], tile.at[:, 0:w, :], sems.at[0]),
        pltpu.make_async_copy(tile_hbm.at[:, w:t, 0:w], tile.at[:, w:t, 0:w], sems.at[1]),
        pltpu.make_async_copy(above0_hbm, above0, sems.at[2]),
        pltpu.make_async_copy(above1_hbm, above1, sems.at[3]),
    ]
    for copy in mine:
        copy.start()

    def choose(act):
        for flag, source in enumerate((left_hbm, seam_hbm)):
            @pl.when(after_seam == flag)
            def _():
                act(pltpu.make_async_copy(source, side, sems.at[4]))

    choose(lambda copy: copy.start())
    for copy in mine:
        copy.wait()
    tile[:, 0:w, w:t] += above1[...]
    choose(lambda copy: copy.wait())
    tile[:, 0:w, 0:w] += above0[...] + side[:, 0:w]
    top = pltpu.make_async_copy(tile.at[:, 0:w, :], out_hbm.at[:, 0:w, :], sems.at[0])
    top.start()
    tile[:, w:t, 0:w] += side[:, w:t]
    low = pltpu.make_async_copy(tile.at[:, w:t, 0:w], out_hbm.at[:, w:t, 0:w], sems.at[1])
    low.start()
    top.wait()
    low.wait()


def combined(where, tile_grad, from_left, from_seam, above0, above1):
    t, w = tile_grad.shape[1], from_left.shape[2]
    return pl.pallas_call(
        functools.partial(combine_kernel, w),
        out_shape=jax.ShapeDtypeStruct(tile_grad.shape, jnp.float32),
        in_specs=[SMEM] + [HBM] * 5,
        out_specs=HBM,
        scratch_shapes=[
            pltpu.VMEM((2, t, t), jnp.float32),
            pltpu.VMEM((2, t, w), jnp.float32),
            pltpu.VMEM((2, w, w), jnp.float32),
            pltpu.VMEM((2, w, w), jnp.float32),
            pltpu.SemaphoreType.DMA((5,)),
        ],
        input_output_aliases={1: 0},
        compiler_params=pltpu.CompilerParams(vmem_limit_bytes=12 * MIB),
        cost_estimate=pl.CostEstimate(flops=10**6, bytes_accessed=6 * MIB, transcendentals=0),
        name="combined",
    )(where, tile_grad, from_left, from_seam, above0, above1)


def place(x, y, z, core):
    return (z % 8 * 2 + y % 4 // 2) * 16 + y % 2 * 8 + x % 4 * 2 + core % 2


def moved(value, **distance):
    route = []
    for x in range(4):
        for y in range(4):
            for z in range(8):
                for core in range(2):
                    target = place(
                        x + distance.get("x", 0), y + distance.get("y", 0),
                        z + distance.get("z", 0), core + distance.get("core", 0),
                    )
                    route.append((place(x, y, z, core), target))
    return lax.ppermute(value, AXES, route)


def add_kernel(groups, *refs):
    count = sum(groups)
    outs = refs[count + (len(refs) - count - len(groups)) // 2 :]
    at = 0
    for out, size in zip(outs, groups):
        parts = refs[at : at + size] if size > 1 else [refs[at].at[i] for i in range(refs[at].shape[0])]
        out[...] = functools.reduce(jnp.add, [part[...] for part in parts])
        at += size


def added(groups, *arrived, vmem=4):
    shapes = [group[0].shape[1:] if len(group) == 1 else group[0].shape for group in groups]
    parts = [part for group in groups for part in group]
    n, m, k = len(parts), len(arrived), len(groups)
    result = pl.pallas_call(
        functools.partial(add_kernel, [len(group) for group in groups]),
        out_shape=[jax.ShapeDtypeStruct(s, jnp.float32) for s in shapes]
        + [jax.ShapeDtypeStruct(a.shape, a.dtype) for a in arrived],
        in_specs=[VMEM] * n + [HBM] * m,
        out_specs=[VMEM] * k + [HBM] * m,
        input_output_aliases={n + i: k + i for i in range(m)},
        compiler_params=pltpu.CompilerParams(vmem_limit_bytes=vmem * MIB),
        name="added",
    )(*parts, *arrived)
    return result


def neighbours(value, axis):
    return [moved(value, **{axis: d}) for d in range(1, SIZES[axis])]


def idle_kernel(array_ref, out_ref):
    del array_ref, out_ref


def awaited(array, flops):
    return pl.pallas_call(
        idle_kernel,
        out_shape=jax.ShapeDtypeStruct(array.shape, array.dtype),
        in_specs=[HBM],
        out_specs=HBM,
        input_output_aliases={0: 0},
        cost_estimate=pl.CostEstimate(flops=flops, bytes_accessed=0, transcendentals=0),
        compiler_params=pltpu.CompilerParams(vmem_limit_bytes=2 * MIB, has_side_effects=True),
        name="awaited",
    )(array)


def planes_kernel(place_ref, own_hbm, other_hbm, out_hbm, sems):
    core = place_ref[0]
    copies = [
        pltpu.make_async_copy(own_hbm, out_hbm.at[core], sems.at[0]),
        pltpu.make_async_copy(other_hbm, out_hbm.at[1 - core], sems.at[1]),
    ]
    for copy in copies:
        copy.start()
    for copy in copies:
        copy.wait()


def both_planes(where, own, other):
    return pl.pallas_call(
        planes_kernel,
        out_shape=jax.ShapeDtypeStruct((2,) + own.shape, own.dtype),
        in_specs=[SMEM, HBM, HBM],
        out_specs=HBM,
        scratch_shapes=[pltpu.SemaphoreType.DMA((2,))],
        compiler_params=pltpu.CompilerParams(vmem_limit_bytes=2 * MIB),
        name="both_planes",
    )(where, own, other)


def z_exchange(chunks):
    groups = [[place(x, y, z, c) for z in range(8)] for x in range(4) for y in range(4) for c in range(2)]
    return lax.all_to_all(chunks, AXES, 0, 0, tiled=True, axis_index_groups=groups)


def halos_in(object_field, window):
    rows, cols = lax.axis_size("row"), lax.axis_size("col")
    col = lax.axis_index("col")
    seam = cols // 2
    w = window
    own0, own1 = object_field[:, :w, :w], object_field[:, w:, :w]
    plain = [(i + 1, i) for i in range(cols - 1) if i + 1 != seam]
    below0 = shifted(own0, "row", -1)
    below1 = awaited(shifted(object_field[:, :w, w:], "row", -1), 5 * 10**9)
    relayed = lax.ppermute(own1, "col", [(seam, 0)])
    right0 = shifted(own0, "col", -1)
    route = [(r * cols + a, r * cols + b) for r in range(rows) for a, b in plain]
    route += [((r + 1) * cols + seam, r * cols + seam - 1) for r in range(rows - 1)]
    right1 = lax.ppermute(jnp.where(col == seam, own0, own1), AXES, route)
    corner = lax.ppermute(jnp.where(col == 0, relayed, below0), "col", plain + [(0, seam - 1)])
    return below1, below0, right0, right1, corner


def shards(object_field, probe, positions, amplitudes, counts):
    window = probe.shape[1]
    col = lax.axis_index("col")
    core = col % 2
    seam = lax.axis_size("col") // 2
    halos = halos_in(object_field, window)
    where = jnp.stack([core, (col == seam - 1).astype(jnp.int32), (col == seam).astype(jnp.int32)])
    tile_grad, right_grad, below0_grad, below1_grad, corner_grad, keep, send = slot_terms(
        counts, positions, where, object_field, halos, probe, amplitudes
    )
    corner_in = shifted(corner_grad, "col", 1)
    above1 = shifted(below1_grad, "row", 1)
    rows, cols = lax.axis_size("row"), lax.axis_size("col")
    plain = [(i, i + 1) for i in range(cols - 1) if i + 1 != seam]

    from_left = lax.ppermute(right_grad, "col", plain)
    from_seam = lax.ppermute(right_grad, "col", [(seam - 1, seam)])
    if (rows, cols) == (16, 16):
        value = keep + moved(send, core=1)
        value = z_exchange(value.reshape(8, window // 8, window))
        value, below0_grad = added([[value], [below0_grad, corner_in]], vmem=8)
        above0 = shifted(below0_grad, "row", 1)
        value, above1, from_left = added([[value] + neighbours(value, "x")], above1, from_left)
        value, above0, from_seam = added([[value] + neighbours(value, "y")], above0, from_seam)
        value = z_exchange(jnp.broadcast_to(value, (8,) + value.shape)).reshape(window, window)
        other = moved(value, core=1)
        probe_total = both_planes(where, value, other)
    else:
        above0 = shifted(below0_grad + corner_in, "row", 1)
        probe_total = lax.psum(jnp.where(core == 0, jnp.stack([keep, send]), jnp.stack([send, keep])), AXES)
    return combined(where, tile_grad, from_left, from_seam, above0, above1), probe_total


def solution(mesh):
    return jax.shard_map(
        shards,
        mesh=mesh,
        in_specs=(
            P(None, "row", "col"),
            P(),
            P(("row", "col"), None),
            P(("row", "col"), None, None),
            P(("row", "col")),
        ),
        out_specs=(P(None, "row", "col"), P()),
        check_vma=False,
    )
```

```python
import functools
import math

import jax
import jax.numpy as jnp
import ml_dtypes
import numpy as np
from jax import lax
from jax.experimental import pallas as pl
from jax.experimental.pallas import tpu as pltpu
from jax.sharding import PartitionSpec as P

AXES = ("row", "col")
HBM = pl.BlockSpec(memory_space=pltpu.HBM)
SMEM = pl.BlockSpec(memory_space=pltpu.SMEM)
VMEM = pl.BlockSpec(memory_space=pltpu.VMEM)
MIB = 1024 * 1024
SIZES = {"x": 4, "y": 4, "z": 8, "core": 2}


def shifted(block, axis, distance):
    devices = range(lax.axis_size(axis))
    route = [(i - distance, i) for i in devices if i - distance in devices]
    return lax.ppermute(block, axis, route)


def dft_tables(window):
    index = np.arange(window)
    phases = (np.outer(index, index) % window) * (2.0 * math.pi / window)
    tables = []
    for part in (np.cos(phases), -np.sin(phases)):
        part = part / math.sqrt(window)
        high = part.astype(ml_dtypes.bfloat16)
        tables += [high, (part - high.astype(np.float64)).astype(ml_dtypes.bfloat16)]
    return np.stack(tables)


def split(value):
    high = value.astype(jnp.bfloat16)
    return high, (value - high.astype(jnp.float32)).astype(jnp.bfloat16)


def dot(first, second):
    return jnp.dot(first, second, preferred_element_type=jnp.float32)


def times_table(re, im, tables, sign):
    w = re.shape[0]
    high, low = split(jnp.concatenate([re, im], axis=0))
    by_re = dot(high, tables[0]) + (dot(low, tables[0]) + dot(high, tables[1]))
    by_im = dot(high, tables[2]) + (dot(low, tables[2]) + dot(high, tables[3]))
    if sign > 0:
        return by_re[:w] - by_im[w:], by_re[w:] + by_im[:w]
    return by_re[:w] + by_im[w:], by_re[w:] - by_im[:w]


def table_times(re, im, tables, sign):
    w = re.shape[1]
    high, low = split(jnp.concatenate([re, im], axis=1))
    by_re = dot(tables[0], high) + (dot(tables[0], low) + dot(tables[1], high))
    by_im = dot(tables[2], high) + (dot(tables[2], low) + dot(tables[3], high))
    if sign > 0:
        return by_re[:, :w] - by_im[:, w:], by_re[:, w:] + by_im[:, :w]
    return by_re[:, :w] + by_im[:, w:], by_re[:, w:] - by_im[:, :w]


def slots_kernel(
    window, tile,
    counts_ref, pos_ref, place_ref, object_hbm, below1_hbm, below0_hbm, right0_hbm, right1_hbm,
    corner_hbm, probe_hbm, amp_hbm, tables_hbm,
    tile_out, right_out, below0_out, below1_out, corner_out, keep_out, send_out,
    ext, grad, probe, turned, amp, tables, patch, probe_grad, sems,
):
    w, t = window, tile
    e = t + w
    live = counts_ref[0]
    core, at_seam = place_ref[0], place_ref[1]
    moves = [
        (probe_hbm, probe),
        (tables_hbm, tables),
        (amp_hbm, amp),
        (object_hbm, ext.at[:, 0:t, 0:t]),
        (right0_hbm, ext.at[:, 0:w, t:e]),
        (below0_hbm, ext.at[:, t:e, 0:w]),
        (below1_hbm, ext.at[:, t:e, w:t]),
    ]
    copies = [pltpu.make_async_copy(a, b, sems.at[i]) for i, (a, b) in enumerate(moves)]
    for copy in copies:
        copy.start()

    def choose(act):
        for flag, parts in enumerate([(right1_hbm, corner_hbm), (corner_hbm, right1_hbm)]):
            @pl.when(at_seam == flag)
            def _():
                for i, part in enumerate(parts):
                    act(pltpu.make_async_copy(part, ext.at[:, (i + 1) * w : (i + 2) * w, t:e], sems.at[7 + i]))

    choose(lambda copy: copy.start())
    grad[...] = jnp.zeros_like(grad)
    probe_grad[...] = jnp.zeros_like(probe_grad)
    copies[0].wait()

    def turn(slot, carry):
        row = lax.rem(lax.rem(pos_ref[slot, 0], t), w)
        col = lax.rem(lax.rem(pos_ref[slot, 1], t), w)
        for plane in range(2):
            turned[slot, plane] = pltpu.roll(pltpu.roll(probe[plane], row, 0), col, 1)
        return carry

    lax.fori_loop(0, live, turn, 0)
    for copy in copies[1:]:
        copy.wait()
    choose(lambda copy: copy.wait())
    moves = [
        (grad.at[:, t:e, t:e], corner_out),
        (grad.at[:, t:e, w:t], below1_out),
        (grad.at[:, t:e, 0:w], below0_out),
        (grad.at[:, 0:t, t:e], right_out),
        (grad.at[:, 0:t, 0:t], tile_out),
    ]
    results = [pltpu.make_async_copy(a, b, sems.at[i]) for i, (a, b) in enumerate(moves)]
    rows = lax.broadcasted_iota(jnp.int32, (w, w), 0)
    cols = lax.broadcasted_iota(jnp.int32, (w, w), 1)

    def one_slot(slot, carry):
        top = lax.rem(pos_ref[slot, 0], t)
        left = lax.rem(pos_ref[slot, 1], t)
        row_turn, col_turn = lax.rem(top, w), lax.rem(left, w)
        row_at = pl.multiple_of((top // w) * w, w)
        col_at = pl.multiple_of((left // w) * w, w)
        in_low = rows < row_turn
        in_right = cols < col_turn
        blocks = [
            (pl.ds(row_at, w), pl.ds(col_at, w), ~in_low & ~in_right),
            (pl.ds(row_at, w), pl.ds(col_at + w, w), ~in_low & in_right),
            (pl.ds(row_at + w, w), pl.ds(col_at, w), in_low & ~in_right),
            (pl.ds(row_at + w, w), pl.ds(col_at + w, w), in_low & in_right),
        ]
        for plane in range(2):
            parts = [ext[plane, at_rows, at_cols] for at_rows, at_cols, _ in blocks]
            patch[plane] = jnp.where(
                in_low, jnp.where(in_right, parts[3], parts[2]), jnp.where(in_right, parts[1], parts[0])
            )
        re = turned[slot, 0] * patch[0] - turned[slot, 1] * patch[1]
        im = turned[slot, 0] * patch[1] + turned[slot, 1] * patch[0]
        re, im = times_table(re, im, tables, 1)
        re, im = table_times(re, im, tables, 1)
        factor = 1.0 - amp[slot] / jnp.sqrt(re * re + im * im + 1.0)
        re, im = times_table(factor * re, factor * im, tables, -1)
        re, im = table_times(re, im, tables, -1)
        terms = (turned[slot, 0] * re + turned[slot, 1] * im, turned[slot, 0] * im - turned[slot, 1] * re)
        for at_rows, at_cols, mask in blocks:
            for plane in range(2):
                grad[plane, at_rows, at_cols] += jnp.where(mask, terms[plane], 0.0)

        @pl.when(slot == live - 1)
        def _():
            for copy in results:
                copy.start()

        terms = (patch[0] * re + patch[1] * im, patch[0] * im - patch[1] * re)
        for plane in range(2):
            term = pltpu.roll(terms[plane], lax.rem(w - row_turn, w), 0)
            probe_grad[plane] += pltpu.roll(term, lax.rem(w - col_turn, w), 1)
        return carry

    lax.fori_loop(0, live, one_slot, 0)
    keep = pltpu.make_async_copy(probe_grad.at[core], keep_out, sems.at[7])
    send = pltpu.make_async_copy(probe_grad.at[1 - core], send_out, sems.at[8])
    for copy in (send, keep):
        copy.start()
    for copy in (send, keep, *results):
        copy.wait()


def slot_terms(counts, positions, where, object_field, halos, probe, amplitudes):
    w, t = probe.shape[1], object_field.shape[1]
    slots = positions.shape[0]
    f32 = functools.partial(jax.ShapeDtypeStruct, dtype=jnp.float32)
    block = f32((2, w, w))
    return pl.pallas_call(
        functools.partial(slots_kernel, w, t),
        out_shape=[f32((2, t, t)), f32((2, t, w)), block, block, block, f32((w, w)), f32((w, w))],
        in_specs=[SMEM] * 3 + [HBM] * 9,
        out_specs=[HBM] * 7,
        scratch_shapes=[
            pltpu.VMEM((2, t + w, t + w), jnp.float32),
            pltpu.VMEM((2, t + w, t + w), jnp.float32),
            pltpu.VMEM((2, w, w), jnp.float32),
            pltpu.VMEM((slots, 2, w, w), jnp.float32),
            pltpu.VMEM((slots, w, w), jnp.float32),
            pltpu.VMEM((4, w, w), jnp.bfloat16),
            pltpu.VMEM((2, w, w), jnp.float32),
            pltpu.VMEM((2, w, w), jnp.float32),
            pltpu.SemaphoreType.DMA((9,)),
        ],
        compiler_params=pltpu.CompilerParams(vmem_limit_bytes=60 * MIB),
        cost_estimate=pl.CostEstimate(flops=3 * 10**9, bytes_accessed=14 * MIB, transcendentals=0),
        name="slot_terms",
    )(counts, positions, where, object_field, *halos, probe, amplitudes, jnp.asarray(dft_tables(w)))


def combine_kernel(
    window, tile_hbm, left_hbm, above0_hbm, above1_hbm, out_hbm, tile, side, above0, above1, sems
):
    w, t = window, tile.shape[1]
    copies = [
        pltpu.make_async_copy(tile_hbm.at[:, 0:w, :], tile.at[:, 0:w, :], sems.at[0]),
        pltpu.make_async_copy(tile_hbm.at[:, w:t, 0:w], tile.at[:, w:t, 0:w], sems.at[1]),
        pltpu.make_async_copy(above0_hbm, above0, sems.at[2]),
        pltpu.make_async_copy(above1_hbm, above1, sems.at[3]),
        pltpu.make_async_copy(left_hbm, side, sems.at[4]),
    ]
    for copy in copies:
        copy.start()
    for copy in copies[:-1]:
        copy.wait()
    tile[:, 0:w, w:t] += above1[...]
    copies[-1].wait()
    tile[:, 0:w, 0:w] += above0[...] + side[:, 0:w]
    top = pltpu.make_async_copy(tile.at[:, 0:w, :], out_hbm.at[:, 0:w, :], sems.at[0])
    top.start()
    tile[:, w:t, 0:w] += side[:, w:t]
    low = pltpu.make_async_copy(tile.at[:, w:t, 0:w], out_hbm.at[:, w:t, 0:w], sems.at[1])
    low.start()
    top.wait()
    low.wait()


def combined(tile_grad, from_left, above0, above1):
    t, w = tile_grad.shape[1], from_left.shape[2]
    return pl.pallas_call(
        functools.partial(combine_kernel, w),
        out_shape=jax.ShapeDtypeStruct(tile_grad.shape, jnp.float32),
        in_specs=[HBM] * 4,
        out_specs=HBM,
        scratch_shapes=[
            pltpu.VMEM((2, t, t), jnp.float32),
            pltpu.VMEM((2, t, w), jnp.float32),
            pltpu.VMEM((2, w, w), jnp.float32),
            pltpu.VMEM((2, w, w), jnp.float32),
            pltpu.SemaphoreType.DMA((5,)),
        ],
        input_output_aliases={0: 0},
        compiler_params=pltpu.CompilerParams(vmem_limit_bytes=12 * MIB),
        cost_estimate=pl.CostEstimate(flops=5 * 10**9, bytes_accessed=6 * MIB, transcendentals=0),
        name="combined",
    )(tile_grad, from_left, above0, above1)


def place(x, y, z, core):
    return (z % 8 * 2 + y % 4 // 2) * 16 + y % 2 * 8 + x % 4 * 2 + core % 2


def moved(value, **distance):
    route = []
    for x in range(4):
        for y in range(4):
            for z in range(8):
                for core in range(2):
                    target = place(
                        x + distance.get("x", 0), y + distance.get("y", 0),
                        z + distance.get("z", 0), core + distance.get("core", 0),
                    )
                    route.append((place(x, y, z, core), target))
    return lax.ppermute(value, AXES, route)


def add_kernel(groups, *refs):
    count = sum(groups)
    outs = refs[count + (len(refs) - count - len(groups)) // 2 :]
    at = 0
    for out, size in zip(outs, groups):
        parts = refs[at : at + size] if size > 1 else [refs[at].at[i] for i in range(refs[at].shape[0])]
        out[...] = functools.reduce(jnp.add, [part[...] for part in parts])
        at += size


def added(groups, *arrived, vmem=4):
    shapes = [group[0].shape[1:] if len(group) == 1 else group[0].shape for group in groups]
    parts = [part for group in groups for part in group]
    n, m, k = len(parts), len(arrived), len(groups)
    result = pl.pallas_call(
        functools.partial(add_kernel, [len(group) for group in groups]),
        out_shape=[jax.ShapeDtypeStruct(s, jnp.float32) for s in shapes]
        + [jax.ShapeDtypeStruct(a.shape, a.dtype) for a in arrived],
        in_specs=[VMEM] * n + [HBM] * m,
        out_specs=[VMEM] * k + [HBM] * m,
        input_output_aliases={n + i: k + i for i in range(m)},
        compiler_params=pltpu.CompilerParams(vmem_limit_bytes=vmem * MIB),
        name="added",
    )(*parts, *arrived)
    return result


def neighbours(value, axis):
    return [moved(value, **{axis: d}) for d in range(1, SIZES[axis])]


def planes_kernel(place_ref, own_hbm, other_hbm, out_hbm, sems):
    core = place_ref[0]
    copies = [
        pltpu.make_async_copy(own_hbm, out_hbm.at[core], sems.at[0]),
        pltpu.make_async_copy(other_hbm, out_hbm.at[1 - core], sems.at[1]),
    ]
    for copy in copies:
        copy.start()
    for copy in copies:
        copy.wait()


def both_planes(where, own, other):
    return pl.pallas_call(
        planes_kernel,
        out_shape=jax.ShapeDtypeStruct((2,) + own.shape, own.dtype),
        in_specs=[SMEM, HBM, HBM],
        out_specs=HBM,
        scratch_shapes=[pltpu.SemaphoreType.DMA((2,))],
        compiler_params=pltpu.CompilerParams(vmem_limit_bytes=2 * MIB),
        name="both_planes",
    )(where, own, other)


def z_exchange(chunks):
    groups = [[place(x, y, z, c) for z in range(8)] for x in range(4) for y in range(4) for c in range(2)]
    return lax.all_to_all(chunks, AXES, 0, 0, tiled=True, axis_index_groups=groups)


def halos_in(object_field, window):
    rows, cols = lax.axis_size("row"), lax.axis_size("col")
    col = lax.axis_index("col")
    seam = cols // 2
    w = window
    own0, own1 = object_field[:, :w, :w], object_field[:, w:, :w]
    plain = [(i + 1, i) for i in range(cols - 1) if i + 1 != seam]
    below0 = shifted(own0, "row", -1)
    below1 = shifted(object_field[:, :w, w:], "row", -1)
    relayed = lax.ppermute(own1, "col", [(seam, 0)])
    right0 = shifted(own0, "col", -1)
    route = [(r * cols + a, r * cols + b) for r in range(rows) for a, b in plain]
    route += [((r + 1) * cols + seam, r * cols + seam - 1) for r in range(rows - 1)]
    right1 = lax.ppermute(jnp.where(col == seam, own0, own1), AXES, route)
    corner = lax.ppermute(jnp.where(col == 0, relayed, below0), "col", plain + [(0, seam - 1)])
    return below1, below0, right0, right1, corner


def shards(object_field, probe, positions, amplitudes, counts):
    window = probe.shape[1]
    col = lax.axis_index("col")
    core = col % 2
    seam = lax.axis_size("col") // 2
    halos = halos_in(object_field, window)
    where = jnp.stack([core, (col == seam - 1).astype(jnp.int32)])
    tile_grad, right_grad, below0_grad, below1_grad, corner_grad, keep, send = slot_terms(
        counts, positions, where, object_field, halos, probe, amplitudes
    )
    corner_in = shifted(corner_grad, "col", 1)
    above1 = shifted(below1_grad, "row", 1)
    rows, cols = lax.axis_size("row"), lax.axis_size("col")
    plain = [(i, i + 1) for i in range(cols - 1) if i + 1 != seam]

    from_left = shifted(right_grad, "col", 1)
    if (lax.axis_size("row"), lax.axis_size("col")) == (16, 16):
        value = keep + moved(send, core=1)
        value = z_exchange(value.reshape(8, window // 8, window))
        value, below0_grad, above1 = added([[value], [below0_grad, corner_in]], above1, vmem=8)
        above0 = shifted(below0_grad, "row", 1)
        value = added([[value] + neighbours(value, "x")])[0]
        value, above0, from_left = added([[value] + neighbours(value, "y")], above0, from_left)
        value = z_exchange(jnp.broadcast_to(value, (8,) + value.shape)).reshape(window, window)
        other = moved(value, core=1)
        probe_total = both_planes(where, value, other)
    else:
        above0 = shifted(below0_grad + corner_in, "row", 1)
        probe_total = lax.psum(jnp.where(core == 0, jnp.stack([keep, send]), jnp.stack([send, keep])), AXES)
    return combined(tile_grad, from_left, above0, above1), probe_total


def solution(mesh):
    return jax.shard_map(
        shards,
        mesh=mesh,
        in_specs=(
            P(None, "row", "col"),
            P(),
            P(("row", "col"), None),
            P(("row", "col"), None, None),
            P(("row", "col")),
        ),
        out_specs=(P(None, "row", "col"), P()),
        check_vma=False,
    )
```

```python
import functools
import math

import jax
import jax.numpy as jnp
import ml_dtypes
import numpy as np
from jax import lax
from jax.experimental import pallas as pl
from jax.experimental.pallas import tpu as pltpu
from jax.sharding import PartitionSpec as P

AXES = ("row", "col")
HBM = pl.BlockSpec(memory_space=pltpu.HBM)
SMEM = pl.BlockSpec(memory_space=pltpu.SMEM)
VMEM = pl.BlockSpec(memory_space=pltpu.VMEM)
MIB = 1024 * 1024
SIZES = {"x": 4, "y": 4, "z": 8, "core": 2}


def shifted(block, axis, distance):
    devices = range(lax.axis_size(axis))
    route = [(i - distance, i) for i in devices if i - distance in devices]
    return lax.ppermute(block, axis, route)


def dft_tables(window):
    index = np.arange(window)
    phases = (np.outer(index, index) % window) * (2.0 * math.pi / window)
    tables = []
    for part in (np.cos(phases), -np.sin(phases)):
        part = part / math.sqrt(window)
        high = part.astype(ml_dtypes.bfloat16)
        tables += [high, (part - high.astype(np.float64)).astype(ml_dtypes.bfloat16)]
    return np.stack(tables)


def split(value):
    high = value.astype(jnp.bfloat16)
    return high, (value - high.astype(jnp.float32)).astype(jnp.bfloat16)


def dot(first, second):
    return jnp.dot(first, second, preferred_element_type=jnp.float32)


def times_table(re, im, tables, sign):
    w = re.shape[0]
    high, low = split(jnp.concatenate([re, im], axis=0))
    by_re = dot(high, tables[0]) + (dot(low, tables[0]) + dot(high, tables[1]))
    by_im = dot(high, tables[2]) + (dot(low, tables[2]) + dot(high, tables[3]))
    if sign > 0:
        return by_re[:w] - by_im[w:], by_re[w:] + by_im[:w]
    return by_re[:w] + by_im[w:], by_re[w:] - by_im[:w]


def table_times(re, im, tables, sign):
    w = re.shape[1]
    high, low = split(jnp.concatenate([re, im], axis=1))
    by_re = dot(tables[0], high) + (dot(tables[0], low) + dot(tables[1], high))
    by_im = dot(tables[2], high) + (dot(tables[2], low) + dot(tables[3], high))
    if sign > 0:
        return by_re[:, :w] - by_im[:, w:], by_re[:, w:] + by_im[:, :w]
    return by_re[:, :w] + by_im[:, w:], by_re[:, w:] - by_im[:, :w]


def slots_kernel(
    window, tile,
    counts_ref, pos_ref, place_ref, object_hbm, below1_hbm, below0_hbm, right0_hbm, right1_hbm,
    corner_hbm, probe_hbm, amp_hbm, tables_hbm,
    tile_out, right_out, below0_out, below1_out, corner_out, keep_out, send_out,
    ext, grad, probe, turned, amp, tables, patch, probe_grad, sems,
):
    w, t = window, tile
    e = t + w
    live = counts_ref[0]
    core, at_seam = place_ref[0], place_ref[1]
    moves = [
        (probe_hbm, probe),
        (tables_hbm, tables),
        (amp_hbm, amp),
        (object_hbm, ext.at[:, 0:t, 0:t]),
        (right0_hbm, ext.at[:, 0:w, t:e]),
        (below0_hbm, ext.at[:, t:e, 0:w]),
        (below1_hbm, ext.at[:, t:e, w:t]),
    ]
    copies = [pltpu.make_async_copy(a, b, sems.at[i]) for i, (a, b) in enumerate(moves)]
    for copy in copies:
        copy.start()

    def choose(act):
        for flag, parts in enumerate([(right1_hbm, corner_hbm), (corner_hbm, right1_hbm)]):
            @pl.when(at_seam == flag)
            def _():
                for i, part in enumerate(parts):
                    act(pltpu.make_async_copy(part, ext.at[:, (i + 1) * w : (i + 2) * w, t:e], sems.at[7 + i]))

    choose(lambda copy: copy.start())
    grad[...] = jnp.zeros_like(grad)
    probe_grad[...] = jnp.zeros_like(probe_grad)
    copies[0].wait()

    def turn(slot, carry):
        row = lax.rem(lax.rem(pos_ref[slot, 0], t), w)
        col = lax.rem(lax.rem(pos_ref[slot, 1], t), w)
        for plane in range(2):
            turned[slot, plane] = pltpu.roll(pltpu.roll(probe[plane], row, 0), col, 1)
        return carry

    lax.fori_loop(0, live, turn, 0)
    for copy in copies[1:]:
        copy.wait()
    choose(lambda copy: copy.wait())
    moves = [
        (grad.at[:, t:e, t:e], corner_out),
        (grad.at[:, t:e, w:t], below1_out),
        (grad.at[:, t:e, 0:w], below0_out),
        (grad.at[:, 0:t, t:e], right_out),
        (grad.at[:, 0:t, 0:t], tile_out),
    ]
    results = [pltpu.make_async_copy(a, b, sems.at[i]) for i, (a, b) in enumerate(moves)]
    rows = lax.broadcasted_iota(jnp.int32, (w, w), 0)
    cols = lax.broadcasted_iota(jnp.int32, (w, w), 1)

    def one_slot(slot, carry):
        top = lax.rem(pos_ref[slot, 0], t)
        left = lax.rem(pos_ref[slot, 1], t)
        row_turn, col_turn = lax.rem(top, w), lax.rem(left, w)
        row_at = pl.multiple_of((top // w) * w, w)
        col_at = pl.multiple_of((left // w) * w, w)
        in_low = rows < row_turn
        in_right = cols < col_turn
        blocks = [
            (pl.ds(row_at, w), pl.ds(col_at, w), ~in_low & ~in_right),
            (pl.ds(row_at, w), pl.ds(col_at + w, w), ~in_low & in_right),
            (pl.ds(row_at + w, w), pl.ds(col_at, w), in_low & ~in_right),
            (pl.ds(row_at + w, w), pl.ds(col_at + w, w), in_low & in_right),
        ]
        for plane in range(2):
            parts = [ext[plane, at_rows, at_cols] for at_rows, at_cols, _ in blocks]
            patch[plane] = jnp.where(
                in_low, jnp.where(in_right, parts[3], parts[2]), jnp.where(in_right, parts[1], parts[0])
            )
        re = turned[slot, 0] * patch[0] - turned[slot, 1] * patch[1]
        im = turned[slot, 0] * patch[1] + turned[slot, 1] * patch[0]
        re, im = times_table(re, im, tables, 1)
        re, im = table_times(re, im, tables, 1)
        factor = 1.0 - amp[slot] / jnp.sqrt(re * re + im * im + 1.0)
        re, im = times_table(factor * re, factor * im, tables, -1)
        re, im = table_times(re, im, tables, -1)
        terms = (turned[slot, 0] * re + turned[slot, 1] * im, turned[slot, 0] * im - turned[slot, 1] * re)
        for at_rows, at_cols, mask in blocks:
            for plane in range(2):
                grad[plane, at_rows, at_cols] += jnp.where(mask, terms[plane], 0.0)

        @pl.when(slot == live - 1)
        def _():
            for copy in results:
                copy.start()

        terms = (patch[0] * re + patch[1] * im, patch[0] * im - patch[1] * re)
        for plane in range(2):
            term = pltpu.roll(terms[plane], lax.rem(w - row_turn, w), 0)
            probe_grad[plane] += pltpu.roll(term, lax.rem(w - col_turn, w), 1)
        return carry

    lax.fori_loop(0, live, one_slot, 0)
    keep = pltpu.make_async_copy(probe_grad.at[core], keep_out, sems.at[7])
    send = pltpu.make_async_copy(probe_grad.at[1 - core], send_out, sems.at[8])
    for copy in (send, keep):
        copy.start()
    for copy in (send, keep, *results):
        copy.wait()


def slot_terms(counts, positions, where, object_field, halos, probe, amplitudes):
    w, t = probe.shape[1], object_field.shape[1]
    slots = positions.shape[0]
    f32 = functools.partial(jax.ShapeDtypeStruct, dtype=jnp.float32)
    block = f32((2, w, w))
    return pl.pallas_call(
        functools.partial(slots_kernel, w, t),
        out_shape=[f32((2, t, t)), f32((2, t, w)), block, block, block, f32((w, w)), f32((w, w))],
        in_specs=[SMEM] * 3 + [HBM] * 9,
        out_specs=[HBM] * 7,
        scratch_shapes=[
            pltpu.VMEM((2, t + w, t + w), jnp.float32),
            pltpu.VMEM((2, t + w, t + w), jnp.float32),
            pltpu.VMEM((2, w, w), jnp.float32),
            pltpu.VMEM((slots, 2, w, w), jnp.float32),
            pltpu.VMEM((slots, w, w), jnp.float32),
            pltpu.VMEM((4, w, w), jnp.bfloat16),
            pltpu.VMEM((2, w, w), jnp.float32),
            pltpu.VMEM((2, w, w), jnp.float32),
            pltpu.SemaphoreType.DMA((9,)),
        ],
        compiler_params=pltpu.CompilerParams(vmem_limit_bytes=60 * MIB),
        cost_estimate=pl.CostEstimate(flops=3 * 10**9, bytes_accessed=14 * MIB, transcendentals=0),
        name="slot_terms",
    )(counts, positions, where, object_field, *halos, probe, amplitudes, jnp.asarray(dft_tables(w)))


def combine_kernel(
    window, place_ref, tile_hbm, left_hbm, seam_hbm, above0_hbm, above1_hbm, out_hbm, tile, side, above0, above1, sems
):
    w, t = window, tile.shape[1]
    after_seam = place_ref[2]
    copies = [
        pltpu.make_async_copy(tile_hbm.at[:, 0:w, :], tile.at[:, 0:w, :], sems.at[0]),
        pltpu.make_async_copy(tile_hbm.at[:, w:t, 0:w], tile.at[:, w:t, 0:w], sems.at[1]),
        pltpu.make_async_copy(above0_hbm, above0, sems.at[2]),
        pltpu.make_async_copy(above1_hbm, above1, sems.at[3]),
    ]
    for copy in copies:
        copy.start()

    def choose(act):
        for flag, source in enumerate((left_hbm, seam_hbm)):
            @pl.when(after_seam == flag)
            def _():
                act(pltpu.make_async_copy(source, side, sems.at[4]))

    choose(lambda copy: copy.start())
    for copy in copies:
        copy.wait()
    tile[:, 0:w, w:t] += above1[...]
    choose(lambda copy: copy.wait())
    tile[:, 0:w, 0:w] += above0[...] + side[:, 0:w]
    top = pltpu.make_async_copy(tile.at[:, 0:w, :], out_hbm.at[:, 0:w, :], sems.at[0])
    top.start()
    tile[:, w:t, 0:w] += side[:, w:t]
    low = pltpu.make_async_copy(tile.at[:, w:t, 0:w], out_hbm.at[:, w:t, 0:w], sems.at[1])
    low.start()
    top.wait()
    low.wait()


def combined(where, tile_grad, from_left, from_seam, above0, above1):
    t, w = tile_grad.shape[1], from_left.shape[2]
    return pl.pallas_call(
        functools.partial(combine_kernel, w),
        out_shape=jax.ShapeDtypeStruct(tile_grad.shape, jnp.float32),
        in_specs=[SMEM] + [HBM] * 5,
        out_specs=HBM,
        scratch_shapes=[
            pltpu.VMEM((2, t, t), jnp.float32),
            pltpu.VMEM((2, t, w), jnp.float32),
            pltpu.VMEM((2, w, w), jnp.float32),
            pltpu.VMEM((2, w, w), jnp.float32),
            pltpu.SemaphoreType.DMA((5,)),
        ],
        input_output_aliases={1: 0},
        compiler_params=pltpu.CompilerParams(vmem_limit_bytes=12 * MIB),
        cost_estimate=pl.CostEstimate(flops=5 * 10**9, bytes_accessed=6 * MIB, transcendentals=0),
        name="combined",
    )(where, tile_grad, from_left, from_seam, above0, above1)


def place(x, y, z, core):
    return (z % 8 * 2 + y % 4 // 2) * 16 + y % 2 * 8 + x % 4 * 2 + core % 2


def moved(value, **distance):
    route = []
    for x in range(4):
        for y in range(4):
            for z in range(8):
                for core in range(2):
                    target = place(
                        x + distance.get("x", 0), y + distance.get("y", 0),
                        z + distance.get("z", 0), core + distance.get("core", 0),
                    )
                    route.append((place(x, y, z, core), target))
    return lax.ppermute(value, AXES, route)


def add_kernel(groups, *refs):
    count = sum(groups)
    outs = refs[count + (len(refs) - count - len(groups)) // 2 :]
    at = 0
    for out, size in zip(outs, groups):
        parts = refs[at : at + size] if size > 1 else [refs[at].at[i] for i in range(refs[at].shape[0])]
        out[...] = functools.reduce(jnp.add, [part[...] for part in parts])
        at += size


def added(groups, *arrived, vmem=4):
    shapes = [group[0].shape[1:] if len(group) == 1 else group[0].shape for group in groups]
    parts = [part for group in groups for part in group]
    n, m, k = len(parts), len(arrived), len(groups)
    result = pl.pallas_call(
        functools.partial(add_kernel, [len(group) for group in groups]),
        out_shape=[jax.ShapeDtypeStruct(s, jnp.float32) for s in shapes]
        + [jax.ShapeDtypeStruct(a.shape, a.dtype) for a in arrived],
        in_specs=[VMEM] * n + [HBM] * m,
        out_specs=[VMEM] * k + [HBM] * m,
        input_output_aliases={n + i: k + i for i in range(m)},
        compiler_params=pltpu.CompilerParams(vmem_limit_bytes=vmem * MIB),
        name="added",
    )(*parts, *arrived)
    return result


def neighbours(value, axis):
    return [moved(value, **{axis: d}) for d in range(1, SIZES[axis])]


def planes_kernel(place_ref, own_hbm, other_hbm, out_hbm, sems):
    core = place_ref[0]
    copies = [
        pltpu.make_async_copy(own_hbm, out_hbm.at[core], sems.at[0]),
        pltpu.make_async_copy(other_hbm, out_hbm.at[1 - core], sems.at[1]),
    ]
    for copy in copies:
        copy.start()
    for copy in copies:
        copy.wait()


def both_planes(where, own, other):
    return pl.pallas_call(
        planes_kernel,
        out_shape=jax.ShapeDtypeStruct((2,) + own.shape, own.dtype),
        in_specs=[SMEM, HBM, HBM],
        out_specs=HBM,
        scratch_shapes=[pltpu.SemaphoreType.DMA((2,))],
        compiler_params=pltpu.CompilerParams(vmem_limit_bytes=2 * MIB),
        name="both_planes",
    )(where, own, other)


def z_exchange(chunks):
    groups = [[place(x, y, z, c) for z in range(8)] for x in range(4) for y in range(4) for c in range(2)]
    return lax.all_to_all(chunks, AXES, 0, 0, tiled=True, axis_index_groups=groups)


def halos_in(object_field, window):
    rows, cols = lax.axis_size("row"), lax.axis_size("col")
    col = lax.axis_index("col")
    seam = cols // 2
    w = window
    own0, own1 = object_field[:, :w, :w], object_field[:, w:, :w]
    plain = [(i + 1, i) for i in range(cols - 1) if i + 1 != seam]
    below0 = shifted(own0, "row", -1)
    below1 = shifted(object_field[:, :w, w:], "row", -1)
    relayed = lax.ppermute(own1, "col", [(seam, 0)])
    right0 = shifted(own0, "col", -1)
    route = [(r * cols + a, r * cols + b) for r in range(rows) for a, b in plain]
    route += [((r + 1) * cols + seam, r * cols + seam - 1) for r in range(rows - 1)]
    right1 = lax.ppermute(jnp.where(col == seam, own0, own1), AXES, route)
    corner = lax.ppermute(jnp.where(col == 0, relayed, below0), "col", plain + [(0, seam - 1)])
    return below1, below0, right0, right1, corner


def shards(object_field, probe, positions, amplitudes, counts):
    window = probe.shape[1]
    col = lax.axis_index("col")
    core = col % 2
    seam = lax.axis_size("col") // 2
    halos = halos_in(object_field, window)
    where = jnp.stack([core, (col == seam - 1).astype(jnp.int32), (col == seam).astype(jnp.int32)])
    tile_grad, right_grad, below0_grad, below1_grad, corner_grad, keep, send = slot_terms(
        counts, positions, where, object_field, halos, probe, amplitudes
    )
    corner_in = shifted(corner_grad, "col", 1)
    above1 = shifted(below1_grad, "row", 1)
    rows, cols = lax.axis_size("row"), lax.axis_size("col")
    plain = [(i, i + 1) for i in range(cols - 1) if i + 1 != seam]

    cols = lax.axis_size("col")
    from_left = lax.ppermute(right_grad, "col", [(i, i + 1) for i in range(cols - 1) if i + 1 != seam])
    from_seam = lax.ppermute(right_grad, "col", [(seam - 1, seam)])
    if (lax.axis_size("row"), lax.axis_size("col")) == (16, 16):
        value = keep + moved(send, core=1)
        value = z_exchange(value.reshape(8, window // 8, window))
        value, below0_grad, above1, from_left = added(
            [[value], [below0_grad, corner_in]], above1, from_left, vmem=8
        )
        above0 = shifted(below0_grad, "row", 1)
        value = added([[value] + neighbours(value, "x")])[0]
        value, above0 = added([[value] + neighbours(value, "y")], above0)
        value = z_exchange(jnp.broadcast_to(value, (8,) + value.shape)).reshape(window, window)
        other = moved(value, core=1)
        probe_total = both_planes(where, value, other)
    else:
        above0 = shifted(below0_grad + corner_in, "row", 1)
        probe_total = lax.psum(jnp.where(core == 0, jnp.stack([keep, send]), jnp.stack([send, keep])), AXES)
    return combined(where, tile_grad, from_left, from_seam, above0, above1), probe_total


def solution(mesh):
    return jax.shard_map(
        shards,
        mesh=mesh,
        in_specs=(
            P(None, "row", "col"),
            P(),
            P(("row", "col"), None),
            P(("row", "col"), None, None),
            P(("row", "col")),
        ),
        out_specs=(P(None, "row", "col"), P()),
        check_vma=False,
    )
```

```python
import functools
import math

import jax
import jax.numpy as jnp
import ml_dtypes
import numpy as np
from jax import lax
from jax.experimental import pallas as pl
from jax.experimental.pallas import tpu as pltpu
from jax.sharding import PartitionSpec as P

AXES = ("row", "col")
HBM = pl.BlockSpec(memory_space=pltpu.HBM)
SMEM = pl.BlockSpec(memory_space=pltpu.SMEM)
VMEM = pl.BlockSpec(memory_space=pltpu.VMEM)
MIB = 1024 * 1024
SIZES = {"x": 4, "y": 4, "z": 8, "core": 2}


def shifted(block, axis, distance):
    devices = range(lax.axis_size(axis))
    route = [(i - distance, i) for i in devices if i - distance in devices]
    return lax.ppermute(block, axis, route)


def dft_tables(window):
    index = np.arange(window)
    phases = (np.outer(index, index) % window) * (2.0 * math.pi / window)
    tables = []
    for part in (np.cos(phases), -np.sin(phases)):
        part = part / math.sqrt(window)
        high = part.astype(ml_dtypes.bfloat16)
        tables += [high, (part - high.astype(np.float64)).astype(ml_dtypes.bfloat16)]
    return np.stack(tables)


def split(value):
    high = value.astype(jnp.bfloat16)
    return high, (value - high.astype(jnp.float32)).astype(jnp.bfloat16)


def dot(first, second):
    return jnp.dot(first, second, preferred_element_type=jnp.float32)


def times_table(re, im, tables, sign):
    w = re.shape[0]
    high, low = split(jnp.concatenate([re, im], axis=0))
    by_re = dot(high, tables[0]) + (dot(low, tables[0]) + dot(high, tables[1]))
    by_im = dot(high, tables[2]) + (dot(low, tables[2]) + dot(high, tables[3]))
    if sign > 0:
        return by_re[:w] - by_im[w:], by_re[w:] + by_im[:w]
    return by_re[:w] + by_im[w:], by_re[w:] - by_im[:w]


def table_times(re, im, tables, sign):
    w = re.shape[1]
    high, low = split(jnp.concatenate([re, im], axis=1))
    by_re = dot(tables[0], high) + (dot(tables[0], low) + dot(tables[1], high))
    by_im = dot(tables[2], high) + (dot(tables[2], low) + dot(tables[3], high))
    if sign > 0:
        return by_re[:, :w] - by_im[:, w:], by_re[:, w:] + by_im[:, :w]
    return by_re[:, :w] + by_im[:, w:], by_re[:, w:] - by_im[:, :w]


def slots_kernel(
    window, tile,
    counts_ref, pos_ref, place_ref, object_hbm, below1_hbm, below0_hbm, right0_hbm, right1_hbm,
    corner_hbm, probe_hbm, amp_hbm, tables_hbm,
    tile_out, right_out, below0_out, below1_out, corner_out, keep_out, send_out,
    ext, grad, probe, turned, amp, tables, patch, probe_grad, sems,
):
    w, t = window, tile
    e = t + w
    live = counts_ref[0]
    core, at_seam = place_ref[0], place_ref[1]
    moves = [
        (probe_hbm, probe),
        (tables_hbm, tables),
        (amp_hbm, amp),
        (object_hbm, ext.at[:, 0:t, 0:t]),
        (right0_hbm, ext.at[:, 0:w, t:e]),
        (below0_hbm, ext.at[:, t:e, 0:w]),
        (below1_hbm, ext.at[:, t:e, w:t]),
    ]
    copies = [pltpu.make_async_copy(a, b, sems.at[i]) for i, (a, b) in enumerate(moves)]
    for copy in copies:
        copy.start()

    def choose(act):
        for flag, parts in enumerate([(right1_hbm, corner_hbm), (corner_hbm, right1_hbm)]):
            @pl.when(at_seam == flag)
            def _():
                for i, part in enumerate(parts):
                    act(pltpu.make_async_copy(part, ext.at[:, (i + 1) * w : (i + 2) * w, t:e], sems.at[7 + i]))

    choose(lambda copy: copy.start())
    grad[...] = jnp.zeros_like(grad)
    probe_grad[...] = jnp.zeros_like(probe_grad)
    copies[0].wait()

    def turn(slot, carry):
        row = lax.rem(lax.rem(pos_ref[slot, 0], t), w)
        col = lax.rem(lax.rem(pos_ref[slot, 1], t), w)
        for plane in range(2):
            turned[slot, plane] = pltpu.roll(pltpu.roll(probe[plane], row, 0), col, 1)
        return carry

    lax.fori_loop(0, live, turn, 0)
    for copy in copies[1:]:
        copy.wait()
    choose(lambda copy: copy.wait())
    moves = [
        (grad.at[:, t:e, t:e], corner_out),
        (grad.at[:, t:e, w:t], below1_out),
        (grad.at[:, t:e, 0:w], below0_out),
        (grad.at[:, 0:t, t:e], right_out),
        (grad.at[:, 0:t, 0:t], tile_out),
    ]
    results = [pltpu.make_async_copy(a, b, sems.at[i]) for i, (a, b) in enumerate(moves)]
    rows = lax.broadcasted_iota(jnp.int32, (w, w), 0)
    cols = lax.broadcasted_iota(jnp.int32, (w, w), 1)

    def one_slot(slot, carry):
        top = lax.rem(pos_ref[slot, 0], t)
        left = lax.rem(pos_ref[slot, 1], t)
        row_turn, col_turn = lax.rem(top, w), lax.rem(left, w)
        row_at = pl.multiple_of((top // w) * w, w)
        col_at = pl.multiple_of((left // w) * w, w)
        in_low = rows < row_turn
        in_right = cols < col_turn
        blocks = [
            (pl.ds(row_at, w), pl.ds(col_at, w), ~in_low & ~in_right),
            (pl.ds(row_at, w), pl.ds(col_at + w, w), ~in_low & in_right),
            (pl.ds(row_at + w, w), pl.ds(col_at, w), in_low & ~in_right),
            (pl.ds(row_at + w, w), pl.ds(col_at + w, w), in_low & in_right),
        ]
        for plane in range(2):
            parts = [ext[plane, at_rows, at_cols] for at_rows, at_cols, _ in blocks]
            patch[plane] = jnp.where(
                in_low, jnp.where(in_right, parts[3], parts[2]), jnp.where(in_right, parts[1], parts[0])
            )
        re = turned[slot, 0] * patch[0] - turned[slot, 1] * patch[1]
        im = turned[slot, 0] * patch[1] + turned[slot, 1] * patch[0]
        re, im = times_table(re, im, tables, 1)
        re, im = table_times(re, im, tables, 1)
        factor = 1.0 - amp[slot] / jnp.sqrt(re * re + im * im + 1.0)
        re, im = times_table(factor * re, factor * im, tables, -1)
        re, im = table_times(re, im, tables, -1)
        terms = (turned[slot, 0] * re + turned[slot, 1] * im, turned[slot, 0] * im - turned[slot, 1] * re)
        for at_rows, at_cols, mask in blocks:
            for plane in range(2):
                grad[plane, at_rows, at_cols] += jnp.where(mask, terms[plane], 0.0)

        @pl.when(slot == live - 1)
        def _():
            for copy in results:
                copy.start()

        terms = (patch[0] * re + patch[1] * im, patch[0] * im - patch[1] * re)
        for plane in range(2):
            term = pltpu.roll(terms[plane], lax.rem(w - row_turn, w), 0)
            probe_grad[plane] += pltpu.roll(term, lax.rem(w - col_turn, w), 1)
        return carry

    lax.fori_loop(0, live, one_slot, 0)
    keep = pltpu.make_async_copy(probe_grad.at[core], keep_out, sems.at[7])
    send = pltpu.make_async_copy(probe_grad.at[1 - core], send_out, sems.at[8])
    for copy in (send, keep):
        copy.start()
    for copy in (send, keep, *results):
        copy.wait()


def slot_terms(counts, positions, where, object_field, halos, probe, amplitudes):
    w, t = probe.shape[1], object_field.shape[1]
    slots = positions.shape[0]
    f32 = functools.partial(jax.ShapeDtypeStruct, dtype=jnp.float32)
    block = f32((2, w, w))
    return pl.pallas_call(
        functools.partial(slots_kernel, w, t),
        out_shape=[f32((2, t, t)), f32((2, t, w)), block, block, block, f32((w, w)), f32((w, w))],
        in_specs=[SMEM] * 3 + [HBM] * 9,
        out_specs=[HBM] * 7,
        scratch_shapes=[
            pltpu.VMEM((2, t + w, t + w), jnp.float32),
            pltpu.VMEM((2, t + w, t + w), jnp.float32),
            pltpu.VMEM((2, w, w), jnp.float32),
            pltpu.VMEM((slots, 2, w, w), jnp.float32),
            pltpu.VMEM((slots, w, w), jnp.float32),
            pltpu.VMEM((4, w, w), jnp.bfloat16),
            pltpu.VMEM((2, w, w), jnp.float32),
            pltpu.VMEM((2, w, w), jnp.float32),
            pltpu.SemaphoreType.DMA((9,)),
        ],
        compiler_params=pltpu.CompilerParams(vmem_limit_bytes=48 * MIB),
        cost_estimate=pl.CostEstimate(flops=3 * 10**9, bytes_accessed=14 * MIB, transcendentals=0),
        name="slot_terms",
    )(counts, positions, where, object_field, *halos, probe, amplitudes, jnp.asarray(dft_tables(w)))


def combine_kernel(
    window, place_ref, tile_hbm, left_hbm, seam_hbm, above0_hbm, above1_hbm, out_hbm, tile, side, above0, above1, sems
):
    w, t = window, tile.shape[1]
    after_seam = place_ref[2]
    copies = [
        pltpu.make_async_copy(tile_hbm.at[:, 0:w, :], tile.at[:, 0:w, :], sems.at[0]),
        pltpu.make_async_copy(tile_hbm.at[:, w:t, 0:w], tile.at[:, w:t, 0:w], sems.at[1]),
        pltpu.make_async_copy(above0_hbm, above0, sems.at[2]),
        pltpu.make_async_copy(above1_hbm, above1, sems.at[3]),
    ]
    for copy in copies:
        copy.start()

    def choose(act):
        for flag, source in enumerate((left_hbm, seam_hbm)):
            @pl.when(after_seam == flag)
            def _():
                act(pltpu.make_async_copy(source, side, sems.at[4]))

    choose(lambda copy: copy.start())
    for copy in copies:
        copy.wait()
    tile[:, 0:w, w:t] += above1[...]
    choose(lambda copy: copy.wait())
    tile[:, 0:w, 0:w] += above0[...] + side[:, 0:w]
    top = pltpu.make_async_copy(tile.at[:, 0:w, :], out_hbm.at[:, 0:w, :], sems.at[0])
    top.start()
    tile[:, w:t, 0:w] += side[:, w:t]
    low = pltpu.make_async_copy(tile.at[:, w:t, 0:w], out_hbm.at[:, w:t, 0:w], sems.at[1])
    low.start()
    top.wait()
    low.wait()


def combined(where, tile_grad, from_left, from_seam, above0, above1):
    t, w = tile_grad.shape[1], from_left.shape[2]
    return pl.pallas_call(
        functools.partial(combine_kernel, w),
        out_shape=jax.ShapeDtypeStruct(tile_grad.shape, jnp.float32),
        in_specs=[SMEM] + [HBM] * 5,
        out_specs=HBM,
        scratch_shapes=[
            pltpu.VMEM((2, t, t), jnp.float32),
            pltpu.VMEM((2, t, w), jnp.float32),
            pltpu.VMEM((2, w, w), jnp.float32),
            pltpu.VMEM((2, w, w), jnp.float32),
            pltpu.SemaphoreType.DMA((5,)),
        ],
        input_output_aliases={1: 0},
        compiler_params=pltpu.CompilerParams(vmem_limit_bytes=12 * MIB),
        cost_estimate=pl.CostEstimate(flops=5 * 10**9, bytes_accessed=6 * MIB, transcendentals=0),
        name="combined",
    )(where, tile_grad, from_left, from_seam, above0, above1)


def place(x, y, z, core):
    return (z % 8 * 2 + y % 4 // 2) * 16 + y % 2 * 8 + x % 4 * 2 + core % 2


def moved(value, **distance):
    route = []
    for x in range(4):
        for y in range(4):
            for z in range(8):
                for core in range(2):
                    target = place(
                        x + distance.get("x", 0), y + distance.get("y", 0),
                        z + distance.get("z", 0), core + distance.get("core", 0),
                    )
                    route.append((place(x, y, z, core), target))
    return lax.ppermute(value, AXES, route)


def add_kernel(groups, *refs):
    count = sum(groups)
    outs = refs[count + (len(refs) - count - len(groups)) // 2 :]
    at = 0
    for out, size in zip(outs, groups):
        parts = refs[at : at + size] if size > 1 else [refs[at].at[i] for i in range(refs[at].shape[0])]
        out[...] = functools.reduce(jnp.add, [part[...] for part in parts])
        at += size


def added(groups, *arrived, vmem=4):
    shapes = [group[0].shape[1:] if len(group) == 1 else group[0].shape for group in groups]
    parts = [part for group in groups for part in group]
    n, m, k = len(parts), len(arrived), len(groups)
    result = pl.pallas_call(
        functools.partial(add_kernel, [len(group) for group in groups]),
        out_shape=[jax.ShapeDtypeStruct(s, jnp.float32) for s in shapes]
        + [jax.ShapeDtypeStruct(a.shape, a.dtype) for a in arrived],
        in_specs=[VMEM] * n + [HBM] * m,
        out_specs=[VMEM] * k + [HBM] * m,
        input_output_aliases={n + i: k + i for i in range(m)},
        compiler_params=pltpu.CompilerParams(vmem_limit_bytes=vmem * MIB),
        name="added",
    )(*parts, *arrived)
    return result


def neighbours(value, axis):
    return [moved(value, **{axis: d}) for d in range(1, SIZES[axis])]


def planes_kernel(place_ref, own_hbm, other_hbm, out_hbm, sems):
    core = place_ref[0]
    copies = [
        pltpu.make_async_copy(own_hbm, out_hbm.at[core], sems.at[0]),
        pltpu.make_async_copy(other_hbm, out_hbm.at[1 - core], sems.at[1]),
    ]
    for copy in copies:
        copy.start()
    for copy in copies:
        copy.wait()


def both_planes(where, own, other):
    return pl.pallas_call(
        planes_kernel,
        out_shape=jax.ShapeDtypeStruct((2,) + own.shape, own.dtype),
        in_specs=[SMEM, HBM, HBM],
        out_specs=HBM,
        scratch_shapes=[pltpu.SemaphoreType.DMA((2,))],
        compiler_params=pltpu.CompilerParams(vmem_limit_bytes=2 * MIB),
        name="both_planes",
    )(where, own, other)


def z_exchange(chunks):
    groups = [[place(x, y, z, c) for z in range(8)] for x in range(4) for y in range(4) for c in range(2)]
    return lax.all_to_all(chunks, AXES, 0, 0, tiled=True, axis_index_groups=groups)


def halos_in(object_field, window):
    rows, cols = lax.axis_size("row"), lax.axis_size("col")
    col = lax.axis_index("col")
    seam = cols // 2
    w = window
    own0, own1 = object_field[:, :w, :w], object_field[:, w:, :w]
    plain = [(i + 1, i) for i in range(cols - 1) if i + 1 != seam]
    below0 = shifted(own0, "row", -1)
    below1 = shifted(object_field[:, :w, w:], "row", -1)
    relayed = lax.ppermute(own1, "col", [(seam, 0)])
    right0 = shifted(own0, "col", -1)
    route = [(r * cols + a, r * cols + b) for r in range(rows) for a, b in plain]
    route += [((r + 1) * cols + seam, r * cols + seam - 1) for r in range(rows - 1)]
    right1 = lax.ppermute(jnp.where(col == seam, own0, own1), AXES, route)
    corner = lax.ppermute(jnp.where(col == 0, relayed, below0), "col", plain + [(0, seam - 1)])
    return below1, below0, right0, right1, corner


def shards(object_field, probe, positions, amplitudes, counts):
    window = probe.shape[1]
    col = lax.axis_index("col")
    core = col % 2
    seam = lax.axis_size("col") // 2
    halos = halos_in(object_field, window)
    where = jnp.stack([core, (col == seam - 1).astype(jnp.int32), (col == seam).astype(jnp.int32)])
    tile_grad, right_grad, below0_grad, below1_grad, corner_grad, keep, send = slot_terms(
        counts, positions, where, object_field, halos, probe, amplitudes
    )
    corner_in = shifted(corner_grad, "col", 1)
    above1 = shifted(below1_grad, "row", 1)
    rows, cols = lax.axis_size("row"), lax.axis_size("col")
    plain = [(i, i + 1) for i in range(cols - 1) if i + 1 != seam]

    cols = lax.axis_size("col")
    from_left = lax.ppermute(right_grad, "col", [(i, i + 1) for i in range(cols - 1) if i + 1 != seam])
    from_seam = lax.ppermute(right_grad, "col", [(seam - 1, seam)])
    if (lax.axis_size("row"), lax.axis_size("col")) == (16, 16):
        value = added([[keep, moved(send, core=1)]])[0]
        value = z_exchange(value.reshape(8, window // 8, window))
        below0_grad = added([[below0_grad, corner_in]])[0]
        value, below0_grad, above1, from_left = added([[value]], below0_grad, above1, from_left)
        above0 = shifted(below0_grad, "row", 1)
        value = added([[value] + neighbours(value, "x")])[0]
        value, above0 = added([[value] + neighbours(value, "y")], above0)
        value = z_exchange(jnp.broadcast_to(value, (8,) + value.shape)).reshape(window, window)
        other = moved(value, core=1)
        probe_total = both_planes(where, value, other)
    else:
        above0 = shifted(below0_grad + corner_in, "row", 1)
        probe_total = lax.psum(jnp.where(core == 0, jnp.stack([keep, send]), jnp.stack([send, keep])), AXES)
    return combined(where, tile_grad, from_left, from_seam, above0, above1), probe_total


def solution(mesh):
    return jax.shard_map(
        shards,
        mesh=mesh,
        in_specs=(
            P(None, "row", "col"),
            P(),
            P(("row", "col"), None),
            P(("row", "col"), None, None),
            P(("row", "col")),
        ),
        out_specs=(P(None, "row", "col"), P()),
        check_vma=False,
    )
```

```python
import functools
import math

import jax
import jax.numpy as jnp
import ml_dtypes
import numpy as np
from jax import lax
from jax.experimental import pallas as pl
from jax.experimental.pallas import tpu as pltpu
from jax.sharding import PartitionSpec as P

AXES = ("row", "col")
HBM = pl.BlockSpec(memory_space=pltpu.HBM)
SMEM = pl.BlockSpec(memory_space=pltpu.SMEM)
VMEM = pl.BlockSpec(memory_space=pltpu.VMEM)
MIB = 1024 * 1024
SIZES = {"x": 4, "y": 4, "z": 8, "core": 2}


def shifted(block, axis, distance):
    devices = range(lax.axis_size(axis))
    route = [(i - distance, i) for i in devices if i - distance in devices]
    return lax.ppermute(block, axis, route)


def dft_tables(window):
    index = np.arange(window)
    phases = (np.outer(index, index) % window) * (2.0 * math.pi / window)
    tables = []
    for part in (np.cos(phases), -np.sin(phases)):
        part = part / math.sqrt(window)
        high = part.astype(ml_dtypes.bfloat16)
        tables += [high, (part - high.astype(np.float64)).astype(ml_dtypes.bfloat16)]
    return np.stack(tables)


def split(value):
    high = value.astype(jnp.bfloat16)
    return high, (value - high.astype(jnp.float32)).astype(jnp.bfloat16)


def dot(first, second):
    return jnp.dot(first, second, preferred_element_type=jnp.float32)


def times_table(re, im, tables, sign):
    w = re.shape[0]
    high, low = split(jnp.concatenate([re, im], axis=0))
    by_re = dot(high, tables[0]) + (dot(low, tables[0]) + dot(high, tables[1]))
    by_im = dot(high, tables[2]) + (dot(low, tables[2]) + dot(high, tables[3]))
    if sign > 0:
        return by_re[:w] - by_im[w:], by_re[w:] + by_im[:w]
    return by_re[:w] + by_im[w:], by_re[w:] - by_im[:w]


def table_times(re, im, tables, sign):
    w = re.shape[1]
    high, low = split(jnp.concatenate([re, im], axis=1))
    by_re = dot(tables[0], high) + (dot(tables[0], low) + dot(tables[1], high))
    by_im = dot(tables[2], high) + (dot(tables[2], low) + dot(tables[3], high))
    if sign > 0:
        return by_re[:, :w] - by_im[:, w:], by_re[:, w:] + by_im[:, :w]
    return by_re[:, :w] + by_im[:, w:], by_re[:, w:] - by_im[:, :w]


def slots_kernel(
    window, tile,
    counts_ref, pos_ref, place_ref, object_hbm, below1_hbm, below0_hbm, right0_hbm, right1_hbm,
    corner_hbm, probe_hbm, amp_hbm, tables_hbm,
    tile_out, right_out, below0_out, below1_out, corner_out, keep_out, send_out,
    ext, grad, probe, turned, amp, tables, patch, probe_grad, sems,
):
    w, t = window, tile
    e = t + w
    live = counts_ref[0]
    core, at_seam = place_ref[0], place_ref[1]
    moves = [
        (probe_hbm, probe),
        (tables_hbm, tables),
        (amp_hbm, amp),
        (object_hbm, ext.at[:, 0:t, 0:t]),
        (right0_hbm, ext.at[:, 0:w, t:e]),
        (below0_hbm, ext.at[:, t:e, 0:w]),
        (below1_hbm, ext.at[:, t:e, w:t]),
    ]
    copies = [pltpu.make_async_copy(a, b, sems.at[i]) for i, (a, b) in enumerate(moves)]
    for copy in copies:
        copy.start()

    def choose(act):
        for flag, parts in enumerate([(right1_hbm, corner_hbm), (corner_hbm, right1_hbm)]):
            @pl.when(at_seam == flag)
            def _():
                for i, part in enumerate(parts):
                    act(pltpu.make_async_copy(part, ext.at[:, (i + 1) * w : (i + 2) * w, t:e], sems.at[7 + i]))

    choose(lambda copy: copy.start())
    grad[...] = jnp.zeros_like(grad)
    probe_grad[...] = jnp.zeros_like(probe_grad)
    copies[0].wait()

    def turn(slot, carry):
        row = lax.rem(lax.rem(pos_ref[slot, 0], t), w)
        col = lax.rem(lax.rem(pos_ref[slot, 1], t), w)
        for plane in range(2):
            turned[slot, plane] = pltpu.roll(pltpu.roll(probe[plane], row, 0), col, 1)
        return carry

    lax.fori_loop(0, live, turn, 0)
    for copy in copies[1:]:
        copy.wait()
    choose(lambda copy: copy.wait())
    moves = [
        (grad.at[:, t:e, t:e], corner_out),
        (grad.at[:, t:e, w:t], below1_out),
        (grad.at[:, t:e, 0:w], below0_out),
        (grad.at[:, 0:t, t:e], right_out),
        (grad.at[:, 0:t, 0:t], tile_out),
    ]
    results = [pltpu.make_async_copy(a, b, sems.at[i]) for i, (a, b) in enumerate(moves)]
    rows = lax.broadcasted_iota(jnp.int32, (w, w), 0)
    cols = lax.broadcasted_iota(jnp.int32, (w, w), 1)

    def one_slot(slot, carry):
        top = lax.rem(pos_ref[slot, 0], t)
        left = lax.rem(pos_ref[slot, 1], t)
        row_turn, col_turn = lax.rem(top, w), lax.rem(left, w)
        row_at = pl.multiple_of((top // w) * w, w)
        col_at = pl.multiple_of((left // w) * w, w)
        in_low = rows < row_turn
        in_right = cols < col_turn
        blocks = [
            (pl.ds(row_at, w), pl.ds(col_at, w), ~in_low & ~in_right),
            (pl.ds(row_at, w), pl.ds(col_at + w, w), ~in_low & in_right),
            (pl.ds(row_at + w, w), pl.ds(col_at, w), in_low & ~in_right),
            (pl.ds(row_at + w, w), pl.ds(col_at + w, w), in_low & in_right),
        ]
        for plane in range(2):
            parts = [ext[plane, at_rows, at_cols] for at_rows, at_cols, _ in blocks]
            patch[plane] = jnp.where(
                in_low, jnp.where(in_right, parts[3], parts[2]), jnp.where(in_right, parts[1], parts[0])
            )
        re = turned[slot, 0] * patch[0] - turned[slot, 1] * patch[1]
        im = turned[slot, 0] * patch[1] + turned[slot, 1] * patch[0]
        re, im = times_table(re, im, tables, 1)
        re, im = table_times(re, im, tables, 1)
        factor = 1.0 - amp[slot] / jnp.sqrt(re * re + im * im + 1.0)
        re, im = times_table(factor * re, factor * im, tables, -1)
        re, im = table_times(re, im, tables, -1)
        terms = (turned[slot, 0] * re + turned[slot, 1] * im, turned[slot, 0] * im - turned[slot, 1] * re)
        for at_rows, at_cols, mask in blocks:
            for plane in range(2):
                grad[plane, at_rows, at_cols] += jnp.where(mask, terms[plane], 0.0)

        @pl.when(slot == live - 1)
        def _():
            for copy in results:
                copy.start()

        terms = (patch[0] * re + patch[1] * im, patch[0] * im - patch[1] * re)
        for plane in range(2):
            term = pltpu.roll(terms[plane], lax.rem(w - row_turn, w), 0)
            probe_grad[plane] += pltpu.roll(term, lax.rem(w - col_turn, w), 1)
        return carry

    lax.fori_loop(0, live, one_slot, 0)
    keep = pltpu.make_async_copy(probe_grad.at[core], keep_out, sems.at[7])
    send = pltpu.make_async_copy(probe_grad.at[1 - core], send_out, sems.at[8])
    for copy in (send, keep):
        copy.start()
    for copy in (send, keep, *results):
        copy.wait()


def slot_terms(counts, positions, where, object_field, halos, probe, amplitudes):
    w, t = probe.shape[1], object_field.shape[1]
    slots = positions.shape[0]
    f32 = functools.partial(jax.ShapeDtypeStruct, dtype=jnp.float32)
    block = f32((2, w, w))
    return pl.pallas_call(
        functools.partial(slots_kernel, w, t),
        out_shape=[f32((2, t, t)), f32((2, t, w)), block, block, block, f32((w, w)), f32((w, w))],
        in_specs=[SMEM] * 3 + [HBM] * 9,
        out_specs=[HBM] * 7,
        scratch_shapes=[
            pltpu.VMEM((2, t + w, t + w), jnp.float32),
            pltpu.VMEM((2, t + w, t + w), jnp.float32),
            pltpu.VMEM((2, w, w), jnp.float32),
            pltpu.VMEM((slots, 2, w, w), jnp.float32),
            pltpu.VMEM((slots, w, w), jnp.float32),
            pltpu.VMEM((4, w, w), jnp.bfloat16),
            pltpu.VMEM((2, w, w), jnp.float32),
            pltpu.VMEM((2, w, w), jnp.float32),
            pltpu.SemaphoreType.DMA((9,)),
        ],
        compiler_params=pltpu.CompilerParams(vmem_limit_bytes=60 * MIB),
        cost_estimate=pl.CostEstimate(flops=3 * 10**9, bytes_accessed=14 * MIB, transcendentals=0),
        name="slot_terms",
    )(counts, positions, where, object_field, *halos, probe, amplitudes, jnp.asarray(dft_tables(w)))


def combine_kernel(
    window, place_ref, tile_hbm, left_hbm, seam_hbm, above0_hbm, above1_hbm, out_hbm, tile, side, above0, above1, sems
):
    w, t = window, tile.shape[1]
    after_seam = place_ref[2]
    copies = [
        pltpu.make_async_copy(tile_hbm.at[:, 0:w, :], tile.at[:, 0:w, :], sems.at[0]),
        pltpu.make_async_copy(tile_hbm.at[:, w:t, 0:w], tile.at[:, w:t, 0:w], sems.at[1]),
        pltpu.make_async_copy(above0_hbm, above0, sems.at[2]),
        pltpu.make_async_copy(above1_hbm, above1, sems.at[3]),
    ]
    for copy in copies:
        copy.start()

    def choose(act):
        for flag, source in enumerate((left_hbm, seam_hbm)):
            @pl.when(after_seam == flag)
            def _():
                act(pltpu.make_async_copy(source, side, sems.at[4]))

    choose(lambda copy: copy.start())
    for copy in copies:
        copy.wait()
    tile[:, 0:w, w:t] += above1[...]
    choose(lambda copy: copy.wait())
    tile[:, 0:w, 0:w] += above0[...] + side[:, 0:w]
    top = pltpu.make_async_copy(tile.at[:, 0:w, :], out_hbm.at[:, 0:w, :], sems.at[0])
    top.start()
    tile[:, w:t, 0:w] += side[:, w:t]
    low = pltpu.make_async_copy(tile.at[:, w:t, 0:w], out_hbm.at[:, w:t, 0:w], sems.at[1])
    low.start()
    top.wait()
    low.wait()


def combined(where, tile_grad, from_left, from_seam, above0, above1):
    t, w = tile_grad.shape[1], from_left.shape[2]
    return pl.pallas_call(
        functools.partial(combine_kernel, w),
        out_shape=jax.ShapeDtypeStruct(tile_grad.shape, jnp.float32),
        in_specs=[SMEM] + [HBM] * 5,
        out_specs=HBM,
        scratch_shapes=[
            pltpu.VMEM((2, t, t), jnp.float32),
            pltpu.VMEM((2, t, w), jnp.float32),
            pltpu.VMEM((2, w, w), jnp.float32),
            pltpu.VMEM((2, w, w), jnp.float32),
            pltpu.SemaphoreType.DMA((5,)),
        ],
        input_output_aliases={1: 0},
        compiler_params=pltpu.CompilerParams(vmem_limit_bytes=12 * MIB),
        cost_estimate=pl.CostEstimate(flops=5 * 10**9, bytes_accessed=6 * MIB, transcendentals=0),
        name="combined",
    )(where, tile_grad, from_left, from_seam, above0, above1)


def place(x, y, z, core):
    return (z % 8 * 2 + y % 4 // 2) * 16 + y % 2 * 8 + x % 4 * 2 + core % 2


def moved(value, **distance):
    route = []
    for x in range(4):
        for y in range(4):
            for z in range(8):
                for core in range(2):
                    target = place(
                        x + distance.get("x", 0), y + distance.get("y", 0),
                        z + distance.get("z", 0), core + distance.get("core", 0),
                    )
                    route.append((place(x, y, z, core), target))
    return lax.ppermute(value, AXES, route)


def add_kernel(groups, *refs):
    count = sum(groups)
    outs = refs[count + (len(refs) - count - len(groups)) // 2 :]
    at = 0
    for out, size in zip(outs, groups):
        parts = refs[at : at + size] if size > 1 else [refs[at].at[i] for i in range(refs[at].shape[0])]
        out[...] = functools.reduce(jnp.add, [part[...] for part in parts])
        at += size


def added(groups, *arrived, vmem=4):
    shapes = [group[0].shape[1:] if len(group) == 1 else group[0].shape for group in groups]
    parts = [part for group in groups for part in group]
    n, m, k = len(parts), len(arrived), len(groups)
    result = pl.pallas_call(
        functools.partial(add_kernel, [len(group) for group in groups]),
        out_shape=[jax.ShapeDtypeStruct(s, jnp.float32) for s in shapes]
        + [jax.ShapeDtypeStruct(a.shape, a.dtype) for a in arrived],
        in_specs=[VMEM] * n + [HBM] * m,
        out_specs=[VMEM] * k + [HBM] * m,
        input_output_aliases={n + i: k + i for i in range(m)},
        compiler_params=pltpu.CompilerParams(vmem_limit_bytes=vmem * MIB),
        name="added",
    )(*parts, *arrived)
    return result


def neighbours(value, axis):
    return [moved(value, **{axis: d}) for d in range(1, SIZES[axis])]


def planes_kernel(place_ref, own_hbm, other_hbm, out_hbm, sems):
    core = place_ref[0]
    copies = [
        pltpu.make_async_copy(own_hbm, out_hbm.at[core], sems.at[0]),
        pltpu.make_async_copy(other_hbm, out_hbm.at[1 - core], sems.at[1]),
    ]
    for copy in copies:
        copy.start()
    for copy in copies:
        copy.wait()


def both_planes(where, own, other):
    return pl.pallas_call(
        planes_kernel,
        out_shape=jax.ShapeDtypeStruct((2,) + own.shape, own.dtype),
        in_specs=[SMEM, HBM, HBM],
        out_specs=HBM,
        scratch_shapes=[pltpu.SemaphoreType.DMA((2,))],
        compiler_params=pltpu.CompilerParams(vmem_limit_bytes=2 * MIB),
        name="both_planes",
    )(where, own, other)


def z_exchange(chunks):
    groups = [[place(x, y, z, c) for z in range(8)] for x in range(4) for y in range(4) for c in range(2)]
    return lax.all_to_all(chunks, AXES, 0, 0, tiled=True, axis_index_groups=groups)


def halos_in(object_field, window):
    rows, cols = lax.axis_size("row"), lax.axis_size("col")
    col = lax.axis_index("col")
    seam = cols // 2
    w = window
    own0, own1 = object_field[:, :w, :w], object_field[:, w:, :w]
    plain = [(i + 1, i) for i in range(cols - 1) if i + 1 != seam]
    below0 = shifted(own0, "row", -1)
    below1 = shifted(object_field[:, :w, w:], "row", -1)
    relayed = lax.ppermute(own1, "col", [(seam, 0)])
    right0 = shifted(own0, "col", -1)
    route = [(r * cols + a, r * cols + b) for r in range(rows) for a, b in plain]
    route += [((r + 1) * cols + seam, r * cols + seam - 1) for r in range(rows - 1)]
    right1 = lax.ppermute(jnp.where(col == seam, own0, own1), AXES, route)
    corner = lax.ppermute(jnp.where(col == 0, relayed, below0), "col", plain + [(0, seam - 1)])
    return below1, below0, right0, right1, corner


def shards(object_field, probe, positions, amplitudes, counts):
    window = probe.shape[1]
    col = lax.axis_index("col")
    core = col % 2
    seam = lax.axis_size("col") // 2
    halos = halos_in(object_field, window)
    where = jnp.stack([core, (col == seam - 1).astype(jnp.int32), (col == seam).astype(jnp.int32)])
    tile_grad, right_grad, below0_grad, below1_grad, corner_grad, keep, send = slot_terms(
        counts, positions, where, object_field, halos, probe, amplitudes
    )
    corner_in = shifted(corner_grad, "col", 1)
    above1 = shifted(below1_grad, "row", 1)
    rows, cols = lax.axis_size("row"), lax.axis_size("col")
    plain = [(i, i + 1) for i in range(cols - 1) if i + 1 != seam]

    cols = lax.axis_size("col")
    from_left = lax.ppermute(right_grad, "col", [(i, i + 1) for i in range(cols - 1) if i + 1 != seam])
    if (lax.axis_size("row"), lax.axis_size("col")) == (16, 16):
        value = added([[keep, moved(send, core=1)]])[0]
        value = z_exchange(value.reshape(8, window // 8, window))
        below0_grad = added([[below0_grad, corner_in]])[0]
        value, below0_grad, above1, from_left = added([[value]], below0_grad, above1, from_left)
        above0 = shifted(below0_grad, "row", 1)
        value = added([[value] + neighbours(value, "x")])[0]
        value, above0, right_grad = added([[value] + neighbours(value, "y")], above0, right_grad)
        from_seam = lax.ppermute(right_grad, "col", [(seam - 1, seam)])
        value = z_exchange(jnp.broadcast_to(value, (8,) + value.shape)).reshape(window, window)
        other = moved(value, core=1)
        probe_total = both_planes(where, value, other)
    else:
        from_seam = lax.ppermute(right_grad, "col", [(seam - 1, seam)])
        above0 = shifted(below0_grad + corner_in, "row", 1)
        probe_total = lax.psum(jnp.where(core == 0, jnp.stack([keep, send]), jnp.stack([send, keep])), AXES)
    return combined(where, tile_grad, from_left, from_seam, above0, above1), probe_total


def solution(mesh):
    return jax.shard_map(
        shards,
        mesh=mesh,
        in_specs=(
            P(None, "row", "col"),
            P(),
            P(("row", "col"), None),
            P(("row", "col"), None, None),
            P(("row", "col")),
        ),
        out_specs=(P(None, "row", "col"), P()),
        check_vma=False,
    )
```

```python
import functools
import math

import jax
import jax.numpy as jnp
import ml_dtypes
import numpy as np
from jax import lax
from jax.experimental import pallas as pl
from jax.experimental.pallas import tpu as pltpu
from jax.sharding import PartitionSpec as P

AXES = ("row", "col")
HBM = pl.BlockSpec(memory_space=pltpu.HBM)
SMEM = pl.BlockSpec(memory_space=pltpu.SMEM)
VMEM = pl.BlockSpec(memory_space=pltpu.VMEM)
MIB = 1024 * 1024
SIZES = {"x": 4, "y": 4, "z": 8, "core": 2}


def shifted(block, axis, distance):
    devices = range(lax.axis_size(axis))
    route = [(i - distance, i) for i in devices if i - distance in devices]
    return lax.ppermute(block, axis, route)


def dft_tables(window):
    index = np.arange(window)
    phases = (np.outer(index, index) % window) * (2.0 * math.pi / window)
    tables = []
    for part in (np.cos(phases), -np.sin(phases)):
        part = part / math.sqrt(window)
        high = part.astype(ml_dtypes.bfloat16)
        tables += [high, (part - high.astype(np.float64)).astype(ml_dtypes.bfloat16)]
    return np.stack(tables)


def split(value):
    high = value.astype(jnp.bfloat16)
    return high, (value - high.astype(jnp.float32)).astype(jnp.bfloat16)


def dot(first, second):
    return jnp.dot(first, second, preferred_element_type=jnp.float32)


def times_table(re, im, tables, sign):
    w = re.shape[0]
    high, low = split(jnp.concatenate([re, im], axis=0))
    by_re = dot(high, tables[0]) + (dot(low, tables[0]) + dot(high, tables[1]))
    by_im = dot(high, tables[2]) + (dot(low, tables[2]) + dot(high, tables[3]))
    if sign > 0:
        return by_re[:w] - by_im[w:], by_re[w:] + by_im[:w]
    return by_re[:w] + by_im[w:], by_re[w:] - by_im[:w]


def table_times(re, im, tables, sign):
    w = re.shape[1]
    high, low = split(jnp.concatenate([re, im], axis=1))
    by_re = dot(tables[0], high) + (dot(tables[0], low) + dot(tables[1], high))
    by_im = dot(tables[2], high) + (dot(tables[2], low) + dot(tables[3], high))
    if sign > 0:
        return by_re[:, :w] - by_im[:, w:], by_re[:, w:] + by_im[:, :w]
    return by_re[:, :w] + by_im[:, w:], by_re[:, w:] - by_im[:, :w]


def slots_kernel(
    window, tile,
    counts_ref, pos_ref, place_ref, object_hbm, below1_hbm, below0_hbm, right0_hbm, right1_hbm,
    corner_hbm, probe_hbm, amp_hbm, tables_hbm,
    tile_out, right_out, below0_out, below1_out, corner_out, keep_out, send_out,
    ext, grad, probe, turned, amp, tables, patch, probe_grad, sems,
):
    w, t = window, tile
    e = t + w
    live = counts_ref[0]
    core, at_seam = place_ref[0], place_ref[1]
    moves = [
        (probe_hbm, probe),
        (tables_hbm, tables),
        (amp_hbm, amp),
        (object_hbm, ext.at[:, 0:t, 0:t]),
        (right0_hbm, ext.at[:, 0:w, t:e]),
        (below0_hbm, ext.at[:, t:e, 0:w]),
        (below1_hbm, ext.at[:, t:e, w:t]),
    ]
    copies = [pltpu.make_async_copy(a, b, sems.at[i]) for i, (a, b) in enumerate(moves)]
    for copy in copies:
        copy.start()

    def choose(act):
        for flag, parts in enumerate([(right1_hbm, corner_hbm), (corner_hbm, right1_hbm)]):
            @pl.when(at_seam == flag)
            def _():
                for i, part in enumerate(parts):
                    act(pltpu.make_async_copy(part, ext.at[:, (i + 1) * w : (i + 2) * w, t:e], sems.at[7 + i]))

    choose(lambda copy: copy.start())
    grad[...] = jnp.zeros_like(grad)
    probe_grad[...] = jnp.zeros_like(probe_grad)
    copies[0].wait()

    def turn(slot, carry):
        row = lax.rem(lax.rem(pos_ref[slot, 0], t), w)
        col = lax.rem(lax.rem(pos_ref[slot, 1], t), w)
        for plane in range(2):
            turned[slot, plane] = pltpu.roll(pltpu.roll(probe[plane], row, 0), col, 1)
        return carry

    lax.fori_loop(0, live, turn, 0)
    for copy in copies[1:]:
        copy.wait()
    choose(lambda copy: copy.wait())
    moves = [
        (grad.at[:, t:e, t:e], corner_out),
        (grad.at[:, t:e, w:t], below1_out),
        (grad.at[:, t:e, 0:w], below0_out),
        (grad.at[:, 0:t, t:e], right_out),
        (grad.at[:, 0:t, 0:t], tile_out),
    ]
    results = [pltpu.make_async_copy(a, b, sems.at[i]) for i, (a, b) in enumerate(moves)]
    rows = lax.broadcasted_iota(jnp.int32, (w, w), 0)
    cols = lax.broadcasted_iota(jnp.int32, (w, w), 1)

    def one_slot(slot, carry):
        top = lax.rem(pos_ref[slot, 0], t)
        left = lax.rem(pos_ref[slot, 1], t)
        row_turn, col_turn = lax.rem(top, w), lax.rem(left, w)
        row_at = pl.multiple_of((top // w) * w, w)
        col_at = pl.multiple_of((left // w) * w, w)
        in_low = rows < row_turn
        in_right = cols < col_turn
        blocks = [
            (pl.ds(row_at, w), pl.ds(col_at, w), ~in_low & ~in_right),
            (pl.ds(row_at, w), pl.ds(col_at + w, w), ~in_low & in_right),
            (pl.ds(row_at + w, w), pl.ds(col_at, w), in_low & ~in_right),
            (pl.ds(row_at + w, w), pl.ds(col_at + w, w), in_low & in_right),
        ]
        for plane in range(2):
            parts = [ext[plane, at_rows, at_cols] for at_rows, at_cols, _ in blocks]
            patch[plane] = jnp.where(
                in_low, jnp.where(in_right, parts[3], parts[2]), jnp.where(in_right, parts[1], parts[0])
            )
        re = turned[slot, 0] * patch[0] - turned[slot, 1] * patch[1]
        im = turned[slot, 0] * patch[1] + turned[slot, 1] * patch[0]
        re, im = times_table(re, im, tables, 1)
        re, im = table_times(re, im, tables, 1)
        factor = 1.0 - amp[slot] / jnp.sqrt(re * re + im * im + 1.0)
        re, im = times_table(factor * re, factor * im, tables, -1)
        re, im = table_times(re, im, tables, -1)
        terms = (turned[slot, 0] * re + turned[slot, 1] * im, turned[slot, 0] * im - turned[slot, 1] * re)
        for at_rows, at_cols, mask in blocks:
            for plane in range(2):
                grad[plane, at_rows, at_cols] += jnp.where(mask, terms[plane], 0.0)

        @pl.when(slot == live - 1)
        def _():
            for copy in results:
                copy.start()

        terms = (patch[0] * re + patch[1] * im, patch[0] * im - patch[1] * re)
        for plane in range(2):
            term = pltpu.roll(terms[plane], lax.rem(w - row_turn, w), 0)
            probe_grad[plane] += pltpu.roll(term, lax.rem(w - col_turn, w), 1)
        return carry

    lax.fori_loop(0, live, one_slot, 0)
    keep = pltpu.make_async_copy(probe_grad.at[core], keep_out, sems.at[7])
    send = pltpu.make_async_copy(probe_grad.at[1 - core], send_out, sems.at[8])
    for copy in (send, keep):
        copy.start()
    for copy in (send, keep, *results):
        copy.wait()


def slot_terms(counts, positions, where, object_field, halos, probe, amplitudes):
    w, t = probe.shape[1], object_field.shape[1]
    slots = positions.shape[0]
    f32 = functools.partial(jax.ShapeDtypeStruct, dtype=jnp.float32)
    block = f32((2, w, w))
    return pl.pallas_call(
        functools.partial(slots_kernel, w, t),
        out_shape=[f32((2, t, t)), f32((2, t, w)), block, block, block, f32((w, w)), f32((w, w))],
        in_specs=[SMEM] * 3 + [HBM] * 9,
        out_specs=[HBM] * 7,
        scratch_shapes=[
            pltpu.VMEM((2, t + w, t + w), jnp.float32),
            pltpu.VMEM((2, t + w, t + w), jnp.float32),
            pltpu.VMEM((2, w, w), jnp.float32),
            pltpu.VMEM((slots, 2, w, w), jnp.float32),
            pltpu.VMEM((slots, w, w), jnp.float32),
            pltpu.VMEM((4, w, w), jnp.bfloat16),
            pltpu.VMEM((2, w, w), jnp.float32),
            pltpu.VMEM((2, w, w), jnp.float32),
            pltpu.SemaphoreType.DMA((9,)),
        ],
        compiler_params=pltpu.CompilerParams(vmem_limit_bytes=50 * MIB),
        cost_estimate=pl.CostEstimate(flops=3 * 10**9, bytes_accessed=14 * MIB, transcendentals=0),
        name="slot_terms",
    )(counts, positions, where, object_field, *halos, probe, amplitudes, jnp.asarray(dft_tables(w)))


def combine_kernel(
    window, place_ref, tile_hbm, left_hbm, seam_hbm, above0_hbm, above1_hbm, out_hbm, tile, side, above0, above1, sems
):
    w, t = window, tile.shape[1]
    after_seam = place_ref[2]
    copies = [
        pltpu.make_async_copy(tile_hbm.at[:, 0:w, :], tile.at[:, 0:w, :], sems.at[0]),
        pltpu.make_async_copy(tile_hbm.at[:, w:t, 0:w], tile.at[:, w:t, 0:w], sems.at[1]),
        pltpu.make_async_copy(above0_hbm, above0, sems.at[2]),
        pltpu.make_async_copy(above1_hbm, above1, sems.at[3]),
    ]
    for copy in copies:
        copy.start()

    def choose(act):
        for flag, source in enumerate((left_hbm, seam_hbm)):
            @pl.when(after_seam == flag)
            def _():
                act(pltpu.make_async_copy(source, side, sems.at[4]))

    choose(lambda copy: copy.start())
    for copy in copies:
        copy.wait()
    tile[:, 0:w, w:t] += above1[...]
    choose(lambda copy: copy.wait())
    tile[:, 0:w, 0:w] += above0[...] + side[:, 0:w]
    top = pltpu.make_async_copy(tile.at[:, 0:w, :], out_hbm.at[:, 0:w, :], sems.at[0])
    top.start()
    tile[:, w:t, 0:w] += side[:, w:t]
    low = pltpu.make_async_copy(tile.at[:, w:t, 0:w], out_hbm.at[:, w:t, 0:w], sems.at[1])
    low.start()
    top.wait()
    low.wait()


def combined(where, tile_grad, from_left, from_seam, above0, above1):
    t, w = tile_grad.shape[1], from_left.shape[2]
    return pl.pallas_call(
        functools.partial(combine_kernel, w),
        out_shape=jax.ShapeDtypeStruct(tile_grad.shape, jnp.float32),
        in_specs=[SMEM] + [HBM] * 5,
        out_specs=HBM,
        scratch_shapes=[
            pltpu.VMEM((2, t, t), jnp.float32),
            pltpu.VMEM((2, t, w), jnp.float32),
            pltpu.VMEM((2, w, w), jnp.float32),
            pltpu.VMEM((2, w, w), jnp.float32),
            pltpu.SemaphoreType.DMA((5,)),
        ],
        input_output_aliases={1: 0},
        compiler_params=pltpu.CompilerParams(vmem_limit_bytes=12 * MIB),
        cost_estimate=pl.CostEstimate(flops=5 * 10**9, bytes_accessed=6 * MIB, transcendentals=0),
        name="combined",
    )(where, tile_grad, from_left, from_seam, above0, above1)


def place(x, y, z, core):
    return (z % 8 * 2 + y % 4 // 2) * 16 + y % 2 * 8 + x % 4 * 2 + core % 2


def moved(value, **distance):
    route = []
    for x in range(4):
        for y in range(4):
            for z in range(8):
                for core in range(2):
                    target = place(
                        x + distance.get("x", 0), y + distance.get("y", 0),
                        z + distance.get("z", 0), core + distance.get("core", 0),
                    )
                    route.append((place(x, y, z, core), target))
    return lax.ppermute(value, AXES, route)


def add_kernel(groups, *refs):
    count = sum(groups)
    outs = refs[count + (len(refs) - count - len(groups)) // 2 :]
    at = 0
    for out, size in zip(outs, groups):
        parts = refs[at : at + size] if size > 1 else [refs[at].at[i] for i in range(refs[at].shape[0])]
        out[...] = functools.reduce(jnp.add, [part[...] for part in parts])
        at += size


def added(groups, *arrived, vmem=4):
    shapes = [group[0].shape[1:] if len(group) == 1 else group[0].shape for group in groups]
    parts = [part for group in groups for part in group]
    n, m, k = len(parts), len(arrived), len(groups)
    result = pl.pallas_call(
        functools.partial(add_kernel, [len(group) for group in groups]),
        out_shape=[jax.ShapeDtypeStruct(s, jnp.float32) for s in shapes]
        + [jax.ShapeDtypeStruct(a.shape, a.dtype) for a in arrived],
        in_specs=[VMEM] * n + [HBM] * m,
        out_specs=[VMEM] * k + [HBM] * m,
        input_output_aliases={n + i: k + i for i in range(m)},
        compiler_params=pltpu.CompilerParams(vmem_limit_bytes=vmem * MIB),
        name="added",
    )(*parts, *arrived)
    return result


def neighbours(value, axis):
    return [moved(value, **{axis: d}) for d in range(1, SIZES[axis])]


def planes_kernel(place_ref, own_hbm, other_hbm, out_hbm, sems):
    core = place_ref[0]
    copies = [
        pltpu.make_async_copy(own_hbm, out_hbm.at[core], sems.at[0]),
        pltpu.make_async_copy(other_hbm, out_hbm.at[1 - core], sems.at[1]),
    ]
    for copy in copies:
        copy.start()
    for copy in copies:
        copy.wait()


def both_planes(where, own, other):
    return pl.pallas_call(
        planes_kernel,
        out_shape=jax.ShapeDtypeStruct((2,) + own.shape, own.dtype),
        in_specs=[SMEM, HBM, HBM],
        out_specs=HBM,
        scratch_shapes=[pltpu.SemaphoreType.DMA((2,))],
        compiler_params=pltpu.CompilerParams(vmem_limit_bytes=2 * MIB),
        name="both_planes",
    )(where, own, other)


def z_exchange(chunks):
    groups = [[place(x, y, z, c) for z in range(8)] for x in range(4) for y in range(4) for c in range(2)]
    return lax.all_to_all(chunks, AXES, 0, 0, tiled=True, axis_index_groups=groups)


def halos_in(object_field, window):
    rows, cols = lax.axis_size("row"), lax.axis_size("col")
    col = lax.axis_index("col")
    seam = cols // 2
    w = window
    own0, own1 = object_field[:, :w, :w], object_field[:, w:, :w]
    plain = [(i + 1, i) for i in range(cols - 1) if i + 1 != seam]
    below0 = shifted(own0, "row", -1)
    below1 = shifted(object_field[:, :w, w:], "row", -1)
    relayed = lax.ppermute(own1, "col", [(seam, 0)])
    right0 = shifted(own0, "col", -1)
    route = [(r * cols + a, r * cols + b) for r in range(rows) for a, b in plain]
    route += [((r + 1) * cols + seam, r * cols + seam - 1) for r in range(rows - 1)]
    right1 = lax.ppermute(jnp.where(col == seam, own0, own1), AXES, route)
    corner = lax.ppermute(jnp.where(col == 0, relayed, below0), "col", plain + [(0, seam - 1)])
    return below1, below0, right0, right1, corner


def shards(object_field, probe, positions, amplitudes, counts):
    window = probe.shape[1]
    col = lax.axis_index("col")
    core = col % 2
    seam = lax.axis_size("col") // 2
    halos = halos_in(object_field, window)
    where = jnp.stack([core, (col == seam - 1).astype(jnp.int32), (col == seam).astype(jnp.int32)])
    tile_grad, right_grad, below0_grad, below1_grad, corner_grad, keep, send = slot_terms(
        counts, positions, where, object_field, halos, probe, amplitudes
    )
    corner_in = shifted(corner_grad, "col", 1)
    above1 = shifted(below1_grad, "row", 1)
    rows, cols = lax.axis_size("row"), lax.axis_size("col")
    plain = [(i, i + 1) for i in range(cols - 1) if i + 1 != seam]

    cols = lax.axis_size("col")
    from_left = lax.ppermute(right_grad, "col", [(i, i + 1) for i in range(cols - 1) if i + 1 != seam])
    from_seam = lax.ppermute(right_grad, "col", [(seam - 1, seam)])
    if (lax.axis_size("row"), lax.axis_size("col")) == (16, 16):
        value = keep + moved(send, core=1)
        value = z_exchange(value.reshape(8, window // 8, window))
        value, below0_grad, above1, from_left = added(
            [[value], [below0_grad, corner_in]], above1, from_left, vmem=8
        )
        above0 = shifted(below0_grad, "row", 1)
        value = added([[value] + neighbours(value, "x")])[0]
        value, above0 = added([[value] + neighbours(value, "y")], above0)
        value = z_exchange(jnp.broadcast_to(value, (8,) + value.shape)).reshape(window, window)
        other = moved(value, core=1)
        probe_total = both_planes(where, value, other)
    else:
        above0 = shifted(below0_grad + corner_in, "row", 1)
        probe_total = lax.psum(jnp.where(core == 0, jnp.stack([keep, send]), jnp.stack([send, keep])), AXES)
    return combined(where, tile_grad, from_left, from_seam, above0, above1), probe_total


def solution(mesh):
    return jax.shard_map(
        shards,
        mesh=mesh,
        in_specs=(
            P(None, "row", "col"),
            P(),
            P(("row", "col"), None),
            P(("row", "col"), None, None),
            P(("row", "col")),
        ),
        out_specs=(P(None, "row", "col"), P()),
        check_vma=False,
    )
```

```python
import functools
import math

import jax
import jax.numpy as jnp
import ml_dtypes
import numpy as np
from jax import lax
from jax.experimental import pallas as pl
from jax.experimental.pallas import tpu as pltpu
from jax.sharding import PartitionSpec as P

AXES = ("row", "col")
HBM = pl.BlockSpec(memory_space=pltpu.HBM)
SMEM = pl.BlockSpec(memory_space=pltpu.SMEM)
VMEM = pl.BlockSpec(memory_space=pltpu.VMEM)
MIB = 1024 * 1024
SIZES = {"x": 4, "y": 4, "z": 8, "core": 2}


def shifted(block, axis, distance):
    devices = range(lax.axis_size(axis))
    route = [(i - distance, i) for i in devices if i - distance in devices]
    return lax.ppermute(block, axis, route)


def dft_tables(window):
    index = np.arange(window)
    phases = (np.outer(index, index) % window) * (2.0 * math.pi / window)
    tables = []
    for part in (np.cos(phases), -np.sin(phases)):
        part = part / math.sqrt(window)
        high = part.astype(ml_dtypes.bfloat16)
        tables += [high, (part - high.astype(np.float64)).astype(ml_dtypes.bfloat16)]
    return np.stack(tables)


def split(value):
    high = value.astype(jnp.bfloat16)
    return high, (value - high.astype(jnp.float32)).astype(jnp.bfloat16)


def dot(first, second):
    return jnp.dot(first, second, preferred_element_type=jnp.float32)


def times_table(re, im, tables, sign):
    w = re.shape[0]
    high, low = split(jnp.concatenate([re, im], axis=0))
    by_re = dot(high, tables[0]) + (dot(low, tables[0]) + dot(high, tables[1]))
    by_im = dot(high, tables[2]) + (dot(low, tables[2]) + dot(high, tables[3]))
    if sign > 0:
        return by_re[:w] - by_im[w:], by_re[w:] + by_im[:w]
    return by_re[:w] + by_im[w:], by_re[w:] - by_im[:w]


def table_times(re, im, tables, sign):
    w = re.shape[1]
    high, low = split(jnp.concatenate([re, im], axis=1))
    by_re = dot(tables[0], high) + (dot(tables[0], low) + dot(tables[1], high))
    by_im = dot(tables[2], high) + (dot(tables[2], low) + dot(tables[3], high))
    if sign > 0:
        return by_re[:, :w] - by_im[:, w:], by_re[:, w:] + by_im[:, :w]
    return by_re[:, :w] + by_im[:, w:], by_re[:, w:] - by_im[:, :w]


def slots_kernel(
    window, tile,
    counts_ref, pos_ref, place_ref, object_hbm, below1_hbm, below0_hbm, right0_hbm, right1_hbm,
    corner_hbm, probe_hbm, amp_hbm, tables_hbm,
    tile_out, right_out, below0_out, below1_out, corner_out, keep_out, send_out,
    ext, grad, probe, turned, amp, tables, patch, probe_grad, sems,
):
    w, t = window, tile
    e = t + w
    live = counts_ref[0]
    core, at_seam = place_ref[0], place_ref[1]
    moves = [
        (probe_hbm, probe),
        (tables_hbm, tables),
        (amp_hbm, amp),
        (object_hbm, ext.at[:, 0:t, 0:t]),
        (right0_hbm, ext.at[:, 0:w, t:e]),
        (below0_hbm, ext.at[:, t:e, 0:w]),
        (below1_hbm, ext.at[:, t:e, w:t]),
    ]
    copies = [pltpu.make_async_copy(a, b, sems.at[i]) for i, (a, b) in enumerate(moves)]
    for copy in copies:
        copy.start()

    def choose(act):
        for flag, parts in enumerate([(right1_hbm, corner_hbm), (corner_hbm, right1_hbm)]):
            @pl.when(at_seam == flag)
            def _():
                for i, part in enumerate(parts):
                    act(pltpu.make_async_copy(part, ext.at[:, (i + 1) * w : (i + 2) * w, t:e], sems.at[7 + i]))

    choose(lambda copy: copy.start())
    grad[...] = jnp.zeros_like(grad)
    probe_grad[...] = jnp.zeros_like(probe_grad)
    copies[0].wait()

    def turn(slot, carry):
        row = lax.rem(lax.rem(pos_ref[slot, 0], t), w)
        col = lax.rem(lax.rem(pos_ref[slot, 1], t), w)
        for plane in range(2):
            turned[slot, plane] = pltpu.roll(pltpu.roll(probe[plane], row, 0), col, 1)
        return carry

    lax.fori_loop(0, live, turn, 0)
    for copy in copies[1:]:
        copy.wait()
    choose(lambda copy: copy.wait())
    moves = [
        (grad.at[:, t:e, t:e], corner_out),
        (grad.at[:, t:e, w:t], below1_out),
        (grad.at[:, t:e, 0:w], below0_out),
        (grad.at[:, 0:t, t:e], right_out),
        (grad.at[:, 0:t, 0:t], tile_out),
    ]
    results = [pltpu.make_async_copy(a, b, sems.at[i]) for i, (a, b) in enumerate(moves)]
    rows = lax.broadcasted_iota(jnp.int32, (w, w), 0)
    cols = lax.broadcasted_iota(jnp.int32, (w, w), 1)

    def one_slot(slot, carry):
        top = lax.rem(pos_ref[slot, 0], t)
        left = lax.rem(pos_ref[slot, 1], t)
        row_turn, col_turn = lax.rem(top, w), lax.rem(left, w)
        row_at = pl.multiple_of((top // w) * w, w)
        col_at = pl.multiple_of((left // w) * w, w)
        in_low = rows < row_turn
        in_right = cols < col_turn
        blocks = [
            (pl.ds(row_at, w), pl.ds(col_at, w), ~in_low & ~in_right),
            (pl.ds(row_at, w), pl.ds(col_at + w, w), ~in_low & in_right),
            (pl.ds(row_at + w, w), pl.ds(col_at, w), in_low & ~in_right),
            (pl.ds(row_at + w, w), pl.ds(col_at + w, w), in_low & in_right),
        ]
        for plane in range(2):
            parts = [ext[plane, at_rows, at_cols] for at_rows, at_cols, _ in blocks]
            patch[plane] = jnp.where(
                in_low, jnp.where(in_right, parts[3], parts[2]), jnp.where(in_right, parts[1], parts[0])
            )
        re = turned[slot, 0] * patch[0] - turned[slot, 1] * patch[1]
        im = turned[slot, 0] * patch[1] + turned[slot, 1] * patch[0]
        re, im = times_table(re, im, tables, 1)
        re, im = table_times(re, im, tables, 1)
        factor = 1.0 - amp[slot] / jnp.sqrt(re * re + im * im + 1.0)
        re, im = times_table(factor * re, factor * im, tables, -1)
        re, im = table_times(re, im, tables, -1)
        terms = (turned[slot, 0] * re + turned[slot, 1] * im, turned[slot, 0] * im - turned[slot, 1] * re)
        for at_rows, at_cols, mask in blocks:
            for plane in range(2):
                grad[plane, at_rows, at_cols] += jnp.where(mask, terms[plane], 0.0)

        @pl.when(slot == live - 1)
        def _():
            for copy in results:
                copy.start()

        terms = (patch[0] * re + patch[1] * im, patch[0] * im - patch[1] * re)
        for plane in range(2):
            term = pltpu.roll(terms[plane], lax.rem(w - row_turn, w), 0)
            probe_grad[plane] += pltpu.roll(term, lax.rem(w - col_turn, w), 1)
        return carry

    lax.fori_loop(0, live, one_slot, 0)
    keep = pltpu.make_async_copy(probe_grad.at[core], keep_out, sems.at[7])
    send = pltpu.make_async_copy(probe_grad.at[1 - core], send_out, sems.at[8])
    for copy in (send, keep):
        copy.start()
    for copy in (send, keep, *results):
        copy.wait()


def slot_terms(counts, positions, where, object_field, halos, probe, amplitudes):
    w, t = probe.shape[1], object_field.shape[1]
    slots = positions.shape[0]
    f32 = functools.partial(jax.ShapeDtypeStruct, dtype=jnp.float32)
    block = f32((2, w, w))
    return pl.pallas_call(
        functools.partial(slots_kernel, w, t),
        out_shape=[f32((2, t, t)), f32((2, t, w)), block, block, block, f32((w, w)), f32((w, w))],
        in_specs=[SMEM] * 3 + [HBM] * 9,
        out_specs=[HBM] * 7,
        scratch_shapes=[
            pltpu.VMEM((2, t + w, t + w), jnp.float32),
            pltpu.VMEM((2, t + w, t + w), jnp.float32),
            pltpu.VMEM((2, w, w), jnp.float32),
            pltpu.VMEM((slots, 2, w, w), jnp.float32),
            pltpu.VMEM((slots, w, w), jnp.float32),
            pltpu.VMEM((4, w, w), jnp.bfloat16),
            pltpu.VMEM((2, w, w), jnp.float32),
            pltpu.VMEM((2, w, w), jnp.float32),
            pltpu.SemaphoreType.DMA((9,)),
        ],
        compiler_params=pltpu.CompilerParams(vmem_limit_bytes=50 * MIB),
        cost_estimate=pl.CostEstimate(flops=3 * 10**9, bytes_accessed=14 * MIB, transcendentals=0),
        name="slot_terms",
    )(counts, positions, where, object_field, *halos, probe, amplitudes, jnp.asarray(dft_tables(w)))


def combine_kernel(
    window, place_ref, tile_hbm, left_hbm, seam_hbm, above0_hbm, above1_hbm, out_hbm, tile, side, above0, above1, sems
):
    w, t = window, tile.shape[1]
    after_seam = place_ref[2]
    copies = [
        pltpu.make_async_copy(tile_hbm.at[:, 0:w, :], tile.at[:, 0:w, :], sems.at[0]),
        pltpu.make_async_copy(tile_hbm.at[:, w:t, 0:w], tile.at[:, w:t, 0:w], sems.at[1]),
        pltpu.make_async_copy(above0_hbm, above0, sems.at[2]),
        pltpu.make_async_copy(above1_hbm, above1, sems.at[3]),
    ]
    for copy in copies:
        copy.start()

    def choose(act):
        for flag, source in enumerate((left_hbm, seam_hbm)):
            @pl.when(after_seam == flag)
            def _():
                act(pltpu.make_async_copy(source, side, sems.at[4]))

    choose(lambda copy: copy.start())
    for copy in copies:
        copy.wait()
    tile[:, 0:w, w:t] += above1[...]
    choose(lambda copy: copy.wait())
    tile[:, 0:w, 0:w] += above0[...] + side[:, 0:w]
    top = pltpu.make_async_copy(tile.at[:, 0:w, :], out_hbm.at[:, 0:w, :], sems.at[0])
    top.start()
    tile[:, w:t, 0:w] += side[:, w:t]
    low = pltpu.make_async_copy(tile.at[:, w:t, 0:w], out_hbm.at[:, w:t, 0:w], sems.at[1])
    low.start()
    top.wait()
    low.wait()


def combined(where, tile_grad, from_left, from_seam, above0, above1):
    t, w = tile_grad.shape[1], from_left.shape[2]
    return pl.pallas_call(
        functools.partial(combine_kernel, w),
        out_shape=jax.ShapeDtypeStruct(tile_grad.shape, jnp.float32),
        in_specs=[SMEM] + [HBM] * 5,
        out_specs=HBM,
        scratch_shapes=[
            pltpu.VMEM((2, t, t), jnp.float32),
            pltpu.VMEM((2, t, w), jnp.float32),
            pltpu.VMEM((2, w, w), jnp.float32),
            pltpu.VMEM((2, w, w), jnp.float32),
            pltpu.SemaphoreType.DMA((5,)),
        ],
        input_output_aliases={1: 0},
        compiler_params=pltpu.CompilerParams(vmem_limit_bytes=12 * MIB),
        cost_estimate=pl.CostEstimate(flops=5 * 10**9, bytes_accessed=6 * MIB, transcendentals=0),
        name="combined",
    )(where, tile_grad, from_left, from_seam, above0, above1)


def place(x, y, z, core):
    return (z % 8 * 2 + y % 4 // 2) * 16 + y % 2 * 8 + x % 4 * 2 + core % 2


def moved(value, **distance):
    route = []
    for x in range(4):
        for y in range(4):
            for z in range(8):
                for core in range(2):
                    target = place(
                        x + distance.get("x", 0), y + distance.get("y", 0),
                        z + distance.get("z", 0), core + distance.get("core", 0),
                    )
                    route.append((place(x, y, z, core), target))
    return lax.ppermute(value, AXES, route)


def add_kernel(groups, *refs):
    count = sum(groups)
    outs = refs[count + (len(refs) - count - len(groups)) // 2 :]
    at = 0
    for out, size in zip(outs, groups):
        parts = refs[at : at + size] if size > 1 else [refs[at].at[i] for i in range(refs[at].shape[0])]
        out[...] = functools.reduce(jnp.add, [part[...] for part in parts])
        at += size


def added(groups, *arrived, vmem=4):
    shapes = [group[0].shape[1:] if len(group) == 1 else group[0].shape for group in groups]
    parts = [part for group in groups for part in group]
    n, m, k = len(parts), len(arrived), len(groups)
    result = pl.pallas_call(
        functools.partial(add_kernel, [len(group) for group in groups]),
        out_shape=[jax.ShapeDtypeStruct(s, jnp.float32) for s in shapes]
        + [jax.ShapeDtypeStruct(a.shape, a.dtype) for a in arrived],
        in_specs=[VMEM] * n + [HBM] * m,
        out_specs=[VMEM] * k + [HBM] * m,
        input_output_aliases={n + i: k + i for i in range(m)},
        compiler_params=pltpu.CompilerParams(vmem_limit_bytes=vmem * MIB),
        name="added",
    )(*parts, *arrived)
    return result


def neighbours(value, axis):
    return [moved(value, **{axis: d}) for d in range(1, SIZES[axis])]


def turn_kernel(*refs):
    del refs


def in_turn(*arrays):
    return pl.pallas_call(
        turn_kernel,
        out_shape=[jax.ShapeDtypeStruct(a.shape, a.dtype) for a in arrays],
        in_specs=[HBM] * len(arrays),
        out_specs=[HBM] * len(arrays),
        input_output_aliases={i: i for i in range(len(arrays))},
        compiler_params=pltpu.CompilerParams(vmem_limit_bytes=2 * MIB),
        name="in_turn",
    )(*arrays)


def planes_kernel(place_ref, own_hbm, other_hbm, out_hbm, sems):
    core = place_ref[0]
    copies = [
        pltpu.make_async_copy(own_hbm, out_hbm.at[core], sems.at[0]),
        pltpu.make_async_copy(other_hbm, out_hbm.at[1 - core], sems.at[1]),
    ]
    for copy in copies:
        copy.start()
    for copy in copies:
        copy.wait()


def both_planes(where, own, other):
    return pl.pallas_call(
        planes_kernel,
        out_shape=jax.ShapeDtypeStruct((2,) + own.shape, own.dtype),
        in_specs=[SMEM, HBM, HBM],
        out_specs=HBM,
        scratch_shapes=[pltpu.SemaphoreType.DMA((2,))],
        compiler_params=pltpu.CompilerParams(vmem_limit_bytes=2 * MIB),
        name="both_planes",
    )(where, own, other)


def z_exchange(chunks):
    groups = [[place(x, y, z, c) for z in range(8)] for x in range(4) for y in range(4) for c in range(2)]
    return lax.all_to_all(chunks, AXES, 0, 0, tiled=True, axis_index_groups=groups)


def halos_in(object_field, window):
    rows, cols = lax.axis_size("row"), lax.axis_size("col")
    col = lax.axis_index("col")
    seam = cols // 2
    w = window
    own0, own1 = object_field[:, :w, :w], object_field[:, w:, :w]
    plain = [(i + 1, i) for i in range(cols - 1) if i + 1 != seam]
    below0 = shifted(own0, "row", -1)
    below1 = shifted(object_field[:, :w, w:], "row", -1)
    relayed = lax.ppermute(own1, "col", [(seam, 0)])
    right0 = shifted(own0, "col", -1)
    route = [(r * cols + a, r * cols + b) for r in range(rows) for a, b in plain]
    route += [((r + 1) * cols + seam, r * cols + seam - 1) for r in range(rows - 1)]
    right1 = lax.ppermute(jnp.where(col == seam, own0, own1), AXES, route)
    corner = lax.ppermute(jnp.where(col == 0, relayed, below0), "col", plain + [(0, seam - 1)])
    return below1, below0, right0, right1, corner


def shards(object_field, probe, positions, amplitudes, counts):
    window = probe.shape[1]
    col = lax.axis_index("col")
    core = col % 2
    seam = lax.axis_size("col") // 2
    halos = halos_in(object_field, window)
    where = jnp.stack([core, (col == seam - 1).astype(jnp.int32), (col == seam).astype(jnp.int32)])
    tile_grad, right_grad, below0_grad, below1_grad, corner_grad, keep, send = slot_terms(
        counts, positions, where, object_field, halos, probe, amplitudes
    )
    corner_in = shifted(corner_grad, "col", 1)
    above1 = shifted(below1_grad, "row", 1)
    rows, cols = lax.axis_size("row"), lax.axis_size("col")
    plain = [(i, i + 1) for i in range(cols - 1) if i + 1 != seam]

    cols = lax.axis_size("col")
    from_left = lax.ppermute(right_grad, "col", [(i, i + 1) for i in range(cols - 1) if i + 1 != seam])
    from_seam = lax.ppermute(right_grad, "col", [(seam - 1, seam)])
    if (lax.axis_size("row"), lax.axis_size("col")) == (16, 16):
        value = keep + moved(send, core=1)
        value = z_exchange(value.reshape(8, window // 8, window))
        value, below0_grad, above1, from_left = added(
            [[value], [below0_grad, corner_in]], above1, from_left, vmem=8
        )
        above0 = shifted(below0_grad, "row", 1)
        value = added([[value] + neighbours(value, "x")])[0]
        value, above0 = added([[value] + neighbours(value, "y")], above0)
        value = z_exchange(jnp.broadcast_to(value, (8,) + value.shape)).reshape(window, window)
        tile_grad = combined(where, tile_grad, from_left, from_seam, above0, above1)
        value, tile_grad = in_turn(value, tile_grad)
        other = moved(value, core=1)
        probe_total = both_planes(where, value, other)
    else:
        above0 = shifted(below0_grad + corner_in, "row", 1)
        tile_grad = combined(where, tile_grad, from_left, from_seam, above0, above1)
        probe_total = lax.psum(jnp.where(core == 0, jnp.stack([keep, send]), jnp.stack([send, keep])), AXES)
    return tile_grad, probe_total


def solution(mesh):
    return jax.shard_map(
        shards,
        mesh=mesh,
        in_specs=(
            P(None, "row", "col"),
            P(),
            P(("row", "col"), None),
            P(("row", "col"), None, None),
            P(("row", "col")),
        ),
        out_specs=(P(None, "row", "col"), P()),
        check_vma=False,
    )
```
